512 devices in a mesh: bx: 32 (over z_hi, y, core), by: 16 (over x, z_lo).
Axes of the slice: x: 4, y: 8, z: 8 (z_hi: 2, z_lo: 4; z = z_hi * 4 + z_lo), core: 2. Of those that a mesh axis runs over, the one named last changes fastest.
Arguments:
- interface_velocity: float32 [3, 2048, 2048], P(None, 'bx', 'by'), may hold values from -6 to 6
- history: float32 [6, 2, 3, 64, 32, 16, 128], P(None, None, None, 'by', 'bx'), may hold values from -6 to 6
- kernel: float32 [7, 64, 32, 16, 128], P(None, 'by', 'bx'), may hold values from -6 to 6
- velocity: float32 [3, 4, 2048, 2048], P(None, None, 'bx', 'by'), may hold values from -6 to 6
- stress: float32 [6, 4, 2048, 2048], P(None, None, 'bx', 'by'), may hold values from -6 to 6
- cohesion: float32 [4, 2048, 2048], P(None, 'bx', 'by'), may hold values from 0.5 to 4
Outputs:
- velocity_new: float32 [3, 4, 2048, 2048], P(None, None, 'bx', 'by')
- stress_new: float32 [6, 4, 2048, 2048], P(None, None, 'bx', 'by')
The draws below stay inside these ranges and needn't reach their ends.
All inputs are finite; a program needn't handle non-finite values.
Results may differ from the reference program's by a relative error of at most 0.00005.
Values sent between devices are 32-bit elements; how exact they have to be, the bound alone decides.
No kernel may reach another device: no remote copies, remote signals or barrier semaphores. Data moves between devices by JAX's collectives and lax.ppermute only.
A program may use at most 64 MiB of HBM per device.

```python
import math
import jax
import jax.numpy as jnp
from jax import lax

NX = 2048
NY = 2048
NZ = 4
HIST = 6
CX = 64
CY = 128
STRIKE_PARTS = 32
DIP_PARTS = 16


def block_scale(key, dims, cuts, low, largest):
    level, own = 1.0, jax.random.fold_in(key, 6)
    for dim, shards_of in cuts:
        steps = jnp.exp(jax.random.uniform(jax.random.fold_in(own, dim), (shards_of,), jnp.float32, low / len(cuts), largest / len(cuts)))
        level = level * jnp.repeat(steps, dims[dim] // shards_of).reshape([-1 if axis == dim else 1 for axis in range(len(dims))])
    return level


def centred(key, shape, scale, bound, cuts=(), dtype=jnp.bfloat16):
    result = jax.random.normal(key, shape, jnp.float32) * scale
    if len(cuts) > 0:
        result = block_scale(key, shape, cuts, -0.22, 0.18) * result
    return jnp.clip(result, min=-bound, max=bound).astype(dtype)


def setup_inputs(seed: int = 0) -> dict:
    splits = jax.random.split(jax.random.key(seed), 7)
    return {
        "interface_velocity": centred(splits[0], (3, NX, NY), 1.0, 6.0, ((1, 32), (2, 16)), jnp.float32),
        "history": centred(splits[1], (HIST, 2, 3, CX, STRIKE_PARTS, DIP_PARTS, CY), 1.0, 6.0, ((3, 16), (4, 32)), jnp.float32),
        "kernel": centred(splits[2], (HIST + 1, CX, STRIKE_PARTS, DIP_PARTS, CY), ((HIST + 1) ** -0.5), 6.0, ((1, 16), (2, 32)), jnp.float32),
        "velocity": centred(splits[3], (3, NZ, NX, NY), 1.0, 6.0, ((2, 32), (3, 16)), jnp.float32),
        "stress": centred(splits[4], (6, NZ, NX, NY), 1.0, 6.0, ((2, 32), (3, 16)), jnp.float32),
        "cohesion": jnp.clip(jnp.exp(math.log(4.0) - 2.0794415 * jax.random.uniform(splits[5], (NZ, NX, NY), jnp.float32) ** block_scale(splits[5], (NZ, NX, NY), ((1, 32), (2, 16)), -0.2, 0.2)), 0.5, 4.0),
    }


COURANT = 0.3
FRICTION = 0.6

def to_layout(transform):
    stacked = jnp.stack([jnp.real(transform), jnp.imag(transform)])
    stacked = stacked.reshape(2, 3, CX, STRIKE_PARTS, CY, DIP_PARTS)
    return jnp.transpose(stacked, (0, 1, 2, 3, 5, 4))

def from_layout(stacked):
    ordered = jnp.transpose(stacked, (0, 1, 2, 3, 5, 4)).reshape(2, 3, NX, NY)
    return ordered[0] + 1j * ordered[1]

def strike_diff(padded):
    return 0.5 * (padded[..., 2:, 1:-1] - padded[..., :-2, 1:-1])

def dip_diff(padded):
    return 0.5 * (padded[..., 1:-1, 2:] - padded[..., 1:-1, :-2])

def depth_diff(layered, ghost_layer):
    above_layer = jnp.concatenate([layered[1:], jnp.zeros_like(layered[:1])], axis=0)
    below_layer = jnp.concatenate([ghost_layer[None], layered[:-1]], axis=0)
    return 0.5 * (above_layer - below_layer)

def yield_limit(trial_stress, cohesion):
    pressure = (trial_stress[0] + trial_stress[1] + trial_stress[2]) / 3.0
    normal_dev = trial_stress[:3] - pressure[None]
    second = 0.5 * lax.optimization_barrier(jnp.sum(normal_dev * normal_dev, axis=0)) + lax.optimization_barrier(jnp.sum(trial_stress[3:] * trial_stress[3:], axis=0))
    shear_stress = jnp.sqrt(second)
    yield_stress = cohesion + FRICTION * jnp.maximum(-pressure, 0.0)
    factor = yield_stress / jnp.maximum(shear_stress, yield_stress)
    return jnp.concatenate([pressure[None] + factor[None] * normal_dev, factor[None] * trial_stress[3:]], axis=0)

def advance_bulk(velocity, stress, traction, interface_velocity, cohesion, widen):
    padded_stress = widen(stress)
    forcing = jnp.stack([strike_diff(padded_stress[0]) + dip_diff(padded_stress[3]) + depth_diff(stress[4], traction[0]), strike_diff(padded_stress[3]) + dip_diff(padded_stress[1]) + depth_diff(stress[5], traction[1]), strike_diff(padded_stress[4]) + dip_diff(padded_stress[5]) + depth_diff(stress[2], traction[2])])
    velocity_new = velocity + COURANT * forcing
    padded_velocity = widen(velocity_new)
    strike_grad = strike_diff(padded_velocity)
    dip_grad = dip_diff(padded_velocity)
    depth_grad = jnp.stack([depth_diff(velocity_new[component], interface_velocity[component]) for component in range(3)])
    dilation = strike_grad[0] + dip_grad[1] + depth_grad[2]
    rates = jnp.stack([dilation + 2.0 * strike_grad[0], dilation + 2.0 * dip_grad[1], dilation + 2.0 * depth_grad[2], dip_grad[0] + strike_grad[1], depth_grad[0] + strike_grad[2], depth_grad[1] + dip_grad[2]])
    trial_stress = stress + COURANT * rates
    return (velocity_new, yield_limit(trial_stress, cohesion))

def wrap_pad(fields):
    return jnp.pad(fields, ((0, 0), (0, 0), (1, 1), (1, 1)), mode='wrap')

def reference(interface_velocity, history, kernel, velocity, stress, cohesion):
    transform = jnp.fft.fft2(interface_velocity, axes=(1, 2), norm='ortho')
    spectrum = to_layout(transform).astype(jnp.float32)
    past_terms = jnp.einsum('hupks,hzcupks->zcupks', kernel[1:].astype(jnp.float32), history.astype(jnp.float32), precision=lax.Precision.HIGHEST)
    response = kernel[0][None, None] * spectrum + past_terms
    traction = jnp.real(jnp.fft.ifft2(from_layout(response), axes=(1, 2), norm='ortho')).astype(jnp.float32)
    velocity_new, stress_new = advance_bulk(velocity, stress, traction, interface_velocity, cohesion, wrap_pad)
    return (velocity_new, stress_new)
```

```python
from functools import partial
import math

import jax
import jax.numpy as jnp
import ml_dtypes
import numpy as np
from jax import lax
from jax.experimental import pallas as pl
from jax.experimental.pallas import tpu as pltpu
from jax.sharding import PartitionSpec as P

COURANT = 0.3
FRICTION = 0.6
NP_, NQ = 32, 64
NJ = 16
NF = 512
SCALE = 1.0 / 2048.0
VMEM = pl.BlockSpec(memory_space=pltpu.VMEM)
PARAMS = pltpu.CompilerParams(vmem_limit_bytes=48 * 1024 * 1024)


def split_table(table):
    high = table.astype(ml_dtypes.bfloat16)
    low = (table - high.astype(np.float64)).astype(ml_dtypes.bfloat16)
    return high, low


def angles(rows, cols, length):
    return 2.0 * np.pi / length * ((rows[:, None] * cols[None, :]) % length)


def strike_tables():
    theta = angles(np.arange(32), np.arange(32), 32)
    cos, sin = np.cos(theta), np.sin(theta)
    high, low = split_table(np.concatenate([cos, -sin], axis=0))
    forward = np.concatenate([high, high, low], axis=1)
    high, low = split_table(np.concatenate([cos, -sin], axis=1))
    inverse = np.concatenate([high, high, low], axis=1)
    return forward, inverse


def strike_twiddle():
    theta = angles(np.arange(32), np.arange(64), 2048)
    theta = np.concatenate([theta, theta], axis=1)
    return np.stack([np.cos(theta), np.sin(theta)]).astype(np.float32)


def cell_tables():
    theta = angles(np.arange(64), np.arange(64), 64).reshape(64, 16, 4)
    cos, sin = np.cos(theta) * SCALE, np.sin(theta) * SCALE
    table = np.zeros((2, 2, 64, 16, 2, 2, 4))
    for h in range(2):
        table[0, h, :, :, 0, h] = cos
        table[1, h, :, :, 0, h] = sin
        table[0, h, :, :, 1, h] = -sin
        table[1, h, :, :, 1, h] = cos
    table = table.reshape(256, 256)
    return split_table(table), split_table(np.ascontiguousarray(table.T))


def dip_order():
    lane = np.arange(NF)
    return 16 * (lane % 32) + lane // 32


def dip_tables():
    theta = angles(np.arange(NF), dip_order(), NF)
    forward = split_table(np.concatenate([np.cos(theta), np.sin(theta)], axis=1))
    inverse = split_table(np.concatenate([np.cos(theta).T, np.sin(theta).T], axis=1))
    return forward, inverse


def dip_twiddle():
    theta = angles(np.arange(4), dip_order(), 2048).reshape(2, 2, 1, NF)
    theta = np.broadcast_to(theta, (2, 2, 4, NF)).reshape(2, 8, NF)
    return np.stack([np.cos(theta), np.sin(theta)], axis=1).astype(np.float32)


def halves(value):
    high = value.astype(jnp.bfloat16)
    low = (value - high.astype(jnp.float32)).astype(jnp.bfloat16)
    return high, low


def dot(a, b):
    return jnp.dot(a, b, preferred_element_type=jnp.float32)


def stacked_dot(table, value):
    high, low = halves(value)
    return dot(table, jnp.concatenate([high, low, high], axis=0))


def rows_dot(value, table_high, table_low):
    rows = value.shape[0]
    high, low = halves(value)
    both = dot(jnp.concatenate([high, low], axis=0), table_high)
    return both[:rows] + both[rows:] + dot(high, table_low)


def roll(value, shift, axis):
    return pltpu.roll(value, shift % value.shape[axis], axis)


def lane_of(shape):
    return lax.broadcasted_iota(jnp.int32, shape, len(shape) - 1)


def row_of(shape):
    return lax.broadcasted_iota(jnp.int32, shape, len(shape) - 2)


def block_transpose(parts):
    parts = list(parts)
    block = lane_of(parts[0].shape) // 16
    for step in (1, 2, 4):
        upper = (block // step) % 2 == 1
        for t in range(8):
            if (t // step) % 2 == 0:
                low, high = parts[t], parts[t + step]
                parts[t] = jnp.where(upper, roll(high, 16 * step, 1), low)
                parts[t + step] = jnp.where(upper, high, roll(low, -16 * step, 1))
    return parts


def scatter_kernel(iv_ref, out_ref, flipped_ref):
    for c in range(3):
        flipped_ref[...] = iv_ref[c].T
        for s in range(2):
            for h in range(2):
                out_ref[:, 2 * c + s, NQ * h : NQ * (h + 1)] = flipped_ref[
                    pl.ds(2 * s + h, 32, stride=4), :
                ]
    zero = jnp.zeros((32, 128), jnp.float32)
    out_ref[:, 6, :] = zero
    out_ref[:, 7, :] = zero


def strike_forward_kernel(in_ref, strike_ref, twiddle_ref, high_ref, low_ref, out_ref):
    value = jnp.concatenate([in_ref[:, m, :] for m in range(6)], axis=1)
    value = stacked_dot(strike_ref[...], value)
    cos, sin = twiddle_ref[0], twiddle_ref[1]
    rows = []
    for m in range(6):
        real = value[:32, 128 * m : 128 * (m + 1)]
        imag = value[32:, 128 * m : 128 * (m + 1)]
        rows.append(
            jnp.concatenate([real * cos + imag * sin, imag * cos - real * sin], axis=1)
        )
    value = rows_dot(jnp.concatenate(rows, axis=0), high_ref[...], low_ref[...])
    zero = jnp.zeros((32, 128), jnp.float32)
    for t in range(2):
        parts = [value[32 * m : 32 * (m + 1), 128 * t : 128 * (t + 1)] for m in range(6)]
        parts = block_transpose(parts + [zero, zero])
        for b in range(8):
            out_ref[32 * (8 * t + b) : 32 * (8 * t + b + 1), :] = parts[b]


def strike_inverse_kernel(in_ref, strike_ref, twiddle_ref, high_ref, low_ref, out_ref):
    columns = []
    for t in range(2):
        columns.append(
            block_transpose([in_ref[32 * (8 * t + b) : 32 * (8 * t + b + 1), :] for b in range(8)])
        )
    rows = [jnp.concatenate([columns[0][m], columns[1][m]], axis=1) for m in range(8)]
    value = rows_dot(jnp.concatenate(rows, axis=0), high_ref[...], low_ref[...])
    cos, sin = twiddle_ref[0], twiddle_ref[1]
    reals, imags = [], []
    for m in range(8):
        real = value[32 * m : 32 * (m + 1), :128]
        imag = value[32 * m : 32 * (m + 1), 128:]
        reals.append(real * cos - imag * sin)
        imags.append(imag * cos + real * sin)
    value = jnp.concatenate(
        [jnp.concatenate(reals, axis=1), jnp.concatenate(imags, axis=1)], axis=0
    )
    value = stacked_dot(strike_ref[...], value)
    parts = [value[:, 128 * m : 128 * (m + 1)] for m in range(8)]
    lane = lane_of((32, 128))
    last = parts[7]
    for m in range(6):
        before = roll(parts[m], 1, 0)
        after = roll(parts[m], -1, 0)
        for h in range(2):
            to = 64 + 2 * (2 * m + h)
            last = jnp.where(lane == to, roll(before, to - (NQ * h + 63), 1), last)
            last = jnp.where(lane == to + 1, roll(after, to + 1 - NQ * h, 1), last)
    parts[7] = last
    for m in range(8):
        out_ref[:, m, :] = parts[m]


def dip_kernel(
    in_ref, weight_ref, past_ref, twiddle_ref, fh_ref, fl_ref, ih_ref, il_ref, out_ref
):
    flipped = in_ref[...].T[:96]
    product = rows_dot(flipped, fh_ref[...], fl_ref[...])
    top = row_of((8, NF)) < 4
    sign = jnp.where(top, 1.0, -1.0).astype(jnp.float32)
    early = lane_of((8, NF)) % 32 < 16
    inverse_rows = []
    for c in range(3):
        even, odd = [], []
        turned = []
        for s in range(2):
            at = 32 * c + 16 * s
            real = product[at : at + 8, :NF] + product[at + 8 : at + 16, NF:]
            imag = product[at + 8 : at + 16, :NF] - product[at : at + 8, NF:]
            cos, sin = twiddle_ref[s, 0], twiddle_ref[s, 1]
            turned.append((real * cos + imag * sin, imag * cos - real * sin))
        even = [turned[0][ri] + turned[1][ri] for ri in range(2)]
        odd = [turned[0][ri] - turned[1][ri] for ri in range(2)]
        odd = [jnp.where(top, odd[0], odd[1]), jnp.where(top, odd[1], -odd[0])]
        response = []
        for parity, value in enumerate((even, odd)):
            spectrum = [roll(part, 4, 0) + sign * part for part in value]
            response.append(
                [
                    weight_ref[parity] * spectrum[ri] + past_ref[c, parity, ri]
                    for ri in range(2)
                ]
            )
        response = [[roll(part, 4, 0) + sign * part for part in pair] for pair in response]
        even = response[0]
        odd = [
            jnp.where(top, response[1][0], -response[1][1]),
            jnp.where(top, response[1][1], response[1][0]),
        ]
        for s in range(2):
            if s == 0:
                real, imag = even[0] + odd[0], even[1] + odd[1]
            else:
                real, imag = even[0] - odd[0], even[1] - odd[1]
            cos, sin = twiddle_ref[s, 0], twiddle_ref[s, 1]
            inverse_rows += [real * cos - imag * sin, imag * cos + real * sin]
    product = rows_dot(jnp.concatenate(inverse_rows, axis=0), ih_ref[...], il_ref[...])
    groups = []
    for c in range(3):
        for s in range(2):
            at = 32 * c + 16 * s
            groups.append(product[at : at + 8, :NF] - product[at + 8 : at + 16, NF:])
            groups.append(product[at + 8 : at + 16, :NF] + product[at : at + 8, NF:])
    edges = []
    for c in range(3):
        for ri in range(2):
            before = roll(roll(groups[4 * c + 2 + ri], 4, 0), 1, 1)
            after = roll(groups[4 * c + ri], -1, 1)
            edges.append(jnp.where(early, before, after))
    for ri in range(2):
        groups.append(jnp.where(top, edges[ri], roll(edges[2 + ri], 4, 0)))
    for ri in range(2):
        groups.append(jnp.where(top, edges[4 + ri], 0.0))
    out_ref[...] = jnp.concatenate(groups, axis=0).T


def past_kernel(kernel_ref, history_ref, out_ref):
    for a in range(4):
        weights = [kernel_ref[h + 1, a, 0] for h in range(6)]
        for z in range(2):
            for c in range(3):
                total = weights[0] * history_ref[0, z, c, a, 0]
                for h in range(1, 6):
                    total = total + weights[h] * history_ref[h, z, c, a, 0]
                out_ref[z, c, a] = total


def edge_kernel(fields_ref, xlo_ref, xhi_ref, ylo_ref, yhi_ref, *, across, along):
    pad = jnp.zeros((4, 128), jnp.float32)
    xlo, xhi = [], []
    lane = lane_of((64, 128))
    ylo = jnp.zeros((64, 128), jnp.float32)
    yhi = jnp.zeros((64, 128), jnp.float32)
    for n in range(3):
        for z in range(4):
            field = fields_ref[across[n], z]
            xlo.append(field[0:1])
            xhi.append(field[63:64])
            field = fields_ref[along[n], z]
            to = 4 * n + z
            ylo = jnp.where(lane == to, roll(field, to, 1), ylo)
            yhi = jnp.where(lane == to, roll(field, to - 127, 1), yhi)
    xlo_ref[...] = jnp.concatenate(xlo + [pad], axis=0)
    xhi_ref[...] = jnp.concatenate(xhi + [pad], axis=0)
    ylo_ref[...] = ylo
    yhi_ref[...] = yhi


def strike_diff(field, low, high):
    row = row_of(field.shape)
    before = jnp.where(row == 0, low, roll(field, 1, 0))
    after = jnp.where(row == 63, high, roll(field, -1, 0))
    return 0.5 * (after - before)


def dip_diff(field, low, high, to):
    lane = lane_of(field.shape)
    before = jnp.where(lane == 0, roll(low, -to, 1), roll(field, 1, 1))
    after = jnp.where(lane == 127, roll(high, 127 - to, 1), roll(field, -1, 1))
    return 0.5 * (after - before)


def velocity_kernel(velocity_ref, stress_ref, xlo_ref, xhi_ref, ylo_ref, yhi_ref, out_ref):
    across, along, deep = (0, 3, 4), (3, 1, 5), (4, 5, 2)
    ylo, yhi = ylo_ref[...], yhi_ref[...]
    for n in range(3):
        for z in range(4):
            at = 4 * n + z
            total = strike_diff(
                stress_ref[across[n], z], xlo_ref[at : at + 1], xhi_ref[at : at + 1]
            ) + dip_diff(stress_ref[along[n], z], ylo, yhi, at)
            if z < 3:
                total = total + 0.5 * stress_ref[deep[n], z + 1]
            if z > 0:
                total = total - 0.5 * stress_ref[deep[n], z - 1]
            out_ref[n, z] = velocity_ref[n, z] + COURANT * total


def slab_kernel(
    in_ref, before_ref, stress_ref, cohesion_ref, iv_ref,
    xlo_ref, xhi_ref, ylo_ref, yhi_ref,
    velocity_ref, out_ref, flipped_ref, edge_ref,
):
    last = in_ref[:, 7, :]
    xlo, xhi = [], []
    half = lane_of((32, 128)) < 64
    edge_ref[...] = jnp.zeros((128, 128), jnp.float32)
    for c in range(3):
        for s in range(2):
            for h in range(2):
                to = pl.ds(2 * s + h, 32, stride=4)
                piece = in_ref[:, 2 * c + s, :]
                piece = roll(piece, 64, 1) if h else piece
                shifted = roll(last, -2 * (4 * c + 2 * s + h), 1)
                flipped_ref[to, :] = jnp.where(half, piece, shifted)
        m, h = 6 + c // 2, c % 2
        edge_ref[4 * c : 4 * c + 1, 0:64] = in_ref[0, m : m + 1, NQ * h : NQ * (h + 1)]
        edge_ref[12 + 4 * c : 13 + 4 * c, 0:64] = in_ref[31, m : m + 1, NQ * h : NQ * (h + 1)]
        traction = flipped_ref[...].T
        velocity_ref[c, 0] = before_ref[c, 0] - 0.5 * COURANT * traction[:64]
        xlo.append(traction[64:65])
        xhi.append(traction[65:66])
        for z in range(1, 4):
            velocity_ref[c, z] = before_ref[c, z]
    edges = edge_ref[...].T[:64]
    lane = lane_of((64, 128))
    ylo = ylo_ref[...] - 0.5 * COURANT * jnp.where(lane < 12, edges, 0.0)
    yhi = yhi_ref[...] - 0.5 * COURANT * jnp.where(lane < 12, roll(edges, -12, 1), 0.0)
    for z in range(4):
        dx, dy, dz = [], [], []
        for c in range(3):
            field = velocity_ref[c, z]
            at = 4 * c + z
            low, high = xlo_ref[at : at + 1], xhi_ref[at : at + 1]
            if z == 0:
                low = low - 0.5 * COURANT * xlo[c]
                high = high - 0.5 * COURANT * xhi[c]
            dx.append(strike_diff(field, low, high))
            dy.append(dip_diff(field, ylo, yhi, at))
            under = iv_ref[c] if z == 0 else velocity_ref[c, z - 1]
            if z < 3:
                dz.append(0.5 * (velocity_ref[c, z + 1] - under))
            else:
                dz.append(-0.5 * under)
        dilation = dx[0] + dy[1] + dz[2]
        rates = [
            dilation + 2.0 * dx[0],
            dilation + 2.0 * dy[1],
            dilation + 2.0 * dz[2],
            dy[0] + dx[1],
            dz[0] + dx[2],
            dz[1] + dy[2],
        ]
        trial = [stress_ref[n, z] + COURANT * rates[n] for n in range(6)]
        pressure = (trial[0] + trial[1] + trial[2]) * (1.0 / 3.0)
        normal = [trial[n] - pressure for n in range(3)]
        second = 0.5 * (
            normal[0] * normal[0] + normal[1] * normal[1] + normal[2] * normal[2]
        ) + (trial[3] * trial[3] + trial[4] * trial[4] + trial[5] * trial[5])
        shear = jnp.sqrt(second)
        limit = cohesion_ref[z] + FRICTION * jnp.maximum(-pressure, 0.0)
        factor = limit / jnp.maximum(shear, limit)
        for n in range(3):
            out_ref[n, z] = pressure + factor * normal[n]
            out_ref[3 + n, z] = factor * trial[3 + n]


def f32(*shape):
    return jax.ShapeDtypeStruct(shape, jnp.float32)


def call(kernel, out_shape, arguments, scratch=()):
    many = isinstance(out_shape, tuple)
    return pl.pallas_call(
        kernel,
        out_shape=out_shape,
        in_specs=[VMEM] * len(arguments),
        out_specs=(VMEM,) * len(out_shape) if many else VMEM,
        scratch_shapes=list(scratch),
        compiler_params=PARAMS,
    )(*arguments)


def scatter(iv):
    return call(scatter_kernel, f32(32, 8, 128), (iv,), [pltpu.VMEM((128, 64), jnp.float32)])


def strike_forward(arrived):
    forward, _ = strike_tables()
    (high, low), _ = cell_tables()
    return call(
        strike_forward_kernel, f32(512, 128), (arrived, forward, strike_twiddle(), high, low)
    )


def strike_inverse(arrived):
    _, inverse = strike_tables()
    _, (high, low) = cell_tables()
    return call(
        strike_inverse_kernel, f32(32, 8, 128), (arrived, inverse, strike_twiddle(), high, low)
    )


def dip(arrived, weight, past):
    forward, inverse = dip_tables()
    return call(
        dip_kernel, f32(512, 128), (arrived, weight, past, dip_twiddle(), *forward, *inverse)
    )


def mode_order(value):
    lead = value.shape[:-3]
    n = len(lead)
    value = value.reshape(*lead, 4, 16, 2, 2, 32)
    value = jnp.transpose(value, (*range(n), n + 3, n + 2, n, n + 1, n + 4))
    return value.reshape(*lead, 2, 8, NF)


def past_terms(kernel, history):
    past = call(past_kernel, f32(2, 3, 4, 16, 128), (kernel, history))
    past = jnp.moveaxis(mode_order(past), 0, 2)
    return mode_order(kernel[0, :, 0]), past


def edges(fields, across, along):
    return call(
        partial(edge_kernel, across=across, along=along),
        (f32(16, 128), f32(16, 128), f32(64, 128), f32(64, 128)),
        (fields,),
    )


def velocity_before(velocity, stress, halo):
    return call(velocity_kernel, f32(3, 4, 64, 128), (velocity, stress, *halo))


def slab(arrived, before, stress, cohesion, iv, halo):
    return call(
        slab_kernel,
        (f32(3, 4, 64, 128), f32(6, 4, 64, 128)),
        (arrived, before, stress, cohesion, iv, *halo),
        [pltpu.VMEM((128, 128), jnp.float32), pltpu.VMEM((128, 128), jnp.float32)],
    )


def exchange(xlo, xhi, ylo, yhi):
    def shift(value, axis, step):
        count = lax.axis_size(axis)
        return lax.ppermute(value, axis, [(i, (i + step) % count) for i in range(count)])

    return (shift(xhi, "bx", 1), shift(xlo, "bx", -1), shift(yhi, "by", 1), shift(ylo, "by", -1))


def strike_swap(value):
    return lax.all_to_all(value, "bx", split_axis=0, concat_axis=0, tiled=True)


def whole_swap(value):
    value = value.reshape(512, 1, 128)
    value = lax.all_to_all(value, ("by", "bx"), split_axis=0, concat_axis=0, tiled=True)
    return value.reshape(512, 128)


def local(interface_velocity, history, kernel, velocity, stress, cohesion):
    arrived = strike_swap(scatter(interface_velocity))
    weight, past = past_terms(kernel, history)
    stress_halo = exchange(*edges(stress, (0, 3, 4), (3, 1, 5)))
    arrived = whole_swap(strike_forward(arrived))
    before = velocity_before(velocity, stress, stress_halo)
    halo = exchange(*edges(before, (0, 1, 2), (0, 1, 2)))
    arrived = whole_swap(dip(arrived, weight, past))
    arrived = strike_swap(strike_inverse(arrived))
    return slab(arrived, before, stress, cohesion, interface_velocity, halo)


def solution(mesh):
    return jax.shard_map(
        local,
        mesh=mesh,
        in_specs=(
            P(None, "bx", "by"),
            P(None, None, None, "by", "bx", None, None),
            P(None, "by", "bx", None, None),
            P(None, None, "bx", "by"),
            P(None, None, "bx", "by"),
            P(None, "bx", "by"),
        ),
        out_specs=(P(None, None, "bx", "by"), P(None, None, "bx", "by")),
        check_vma=False,
    )
```

```python
import jax
import jax.numpy as jnp
import ml_dtypes
import numpy as np
from jax import lax
from jax.experimental import pallas as pl
from jax.experimental.pallas import tpu as pltpu
from jax.sharding import PartitionSpec as P

COURANT = 0.3
FRICTION = 0.6
NP_, NQ = 32, 64
NJ = 16
NF = 512
SCALE = 1.0 / 2048.0
VMEM = pl.BlockSpec(memory_space=pltpu.VMEM)
PARAMS = pltpu.CompilerParams(vmem_limit_bytes=16 * 1024 * 1024)


def split_table(table):
    high = table.astype(ml_dtypes.bfloat16)
    low = (table - high.astype(np.float64)).astype(ml_dtypes.bfloat16)
    return high, low


def angles(rows, cols, length):
    return 2.0 * np.pi / length * ((rows[:, None] * cols[None, :]) % length)


def strike_tables():
    theta = angles(np.arange(32), np.arange(32), 32)
    cos, sin = np.cos(theta), np.sin(theta)
    high, low = split_table(np.concatenate([cos, -sin], axis=0))
    forward = np.concatenate([high, high, low], axis=1)
    high, low = split_table(np.concatenate([cos, -sin], axis=1))
    inverse = np.concatenate([high, high, low], axis=1)
    return forward, inverse


def strike_twiddle():
    theta = angles(np.arange(32), np.arange(64), 2048)
    theta = np.concatenate([theta, theta], axis=1)
    return np.stack([np.cos(theta), np.sin(theta)]).astype(np.float32)


def cell_tables():
    theta = angles(np.arange(64), np.arange(64), 64).reshape(64, 16, 4)
    cos, sin = np.cos(theta) * SCALE, np.sin(theta) * SCALE
    table = np.zeros((2, 2, 64, 16, 2, 2, 4))
    for h in range(2):
        table[0, h, :, :, 0, h] = cos
        table[1, h, :, :, 0, h] = sin
        table[0, h, :, :, 1, h] = -sin
        table[1, h, :, :, 1, h] = cos
    table = table.reshape(256, 256)
    return split_table(table), split_table(np.ascontiguousarray(table.T))


def dip_order():
    lane = np.arange(128)
    return 4 * (lane % 32) + lane // 32


def dip_tables():
    theta = angles(np.arange(128), dip_order(), 128)
    forward = np.concatenate([np.cos(theta), np.sin(theta)], axis=1)
    inverse = np.concatenate([np.cos(theta).T, np.sin(theta).T], axis=1)
    return split_table(forward) + split_table(inverse)


def dip_inner_twiddle():
    theta = angles(np.arange(4), np.arange(128), 512)
    return np.stack([np.cos(theta), np.sin(theta)], axis=1).astype(np.float32)


def dip_twiddle():
    f = (4 * dip_order()[None, :] + np.arange(4)[:, None]).reshape(NF)
    theta = angles(np.arange(4), f, 2048).reshape(2, 2, 1, NF)
    theta = np.broadcast_to(theta, (2, 2, 4, NF)).reshape(2, 8, NF)
    return np.stack([np.cos(theta), np.sin(theta)], axis=1).astype(np.float32)


def halves(value):
    high = value.astype(jnp.bfloat16)
    low = (value - high.astype(jnp.float32)).astype(jnp.bfloat16)
    return high, low


def dot(a, b):
    return jnp.dot(a, b, preferred_element_type=jnp.float32)


def stacked_dot(table, value):
    high, low = halves(value)
    return dot(table, jnp.concatenate([high, low, high], axis=0))


def rows_dot(value, table_high, table_low):
    rows = value.shape[0]
    high, low = halves(value)
    both = dot(jnp.concatenate([high, low], axis=0), table_high)
    return both[:rows] + both[rows:] + dot(high, table_low)


def radix_four(values, sign):
    (r0, i0), (r1, i1), (r2, i2), (r3, i3) = values
    ar, ai, br, bi = r0 + r2, i0 + i2, r0 - r2, i0 - i2
    cr, ci, dr, di = r1 + r3, i1 + i3, sign * (r1 - r3), sign * (i1 - i3)
    return [
        (ar + cr, ai + ci),
        (br - di, bi + dr),
        (ar - cr, ai - ci),
        (br + di, bi - dr),
    ]


def turn(real, imag, cos, sin, sign):
    if sign > 0:
        return real * cos - imag * sin, imag * cos + real * sin
    return real * cos + imag * sin, imag * cos - real * sin


def dip_transform(values, high, low, sign):
    stacked = jnp.concatenate([part for pair in values for part in pair], axis=0)
    product = rows_dot(stacked, high, low)
    out = []
    for n in range(4):
        real, imag = product[96 * n : 96 * n + 48], product[96 * n + 48 : 96 * (n + 1)]
        out.append(
            (
                real[:, :128] - sign * imag[:, 128:],
                imag[:, :128] + sign * real[:, 128:],
            )
        )
    return out


def roll(value, shift, axis):
    return pltpu.roll(value, shift % value.shape[axis], axis)


def lane_of(shape):
    return lax.broadcasted_iota(jnp.int32, shape, len(shape) - 1)


def row_of(shape):
    return lax.broadcasted_iota(jnp.int32, shape, len(shape) - 2)


def block_transpose(parts):
    parts = list(parts)
    block = lane_of(parts[0].shape) // 16
    for step in (1, 2, 4):
        upper = (block // step) % 2 == 1
        for t in range(8):
            if (t // step) % 2 == 0:
                low, high = parts[t], parts[t + step]
                parts[t] = jnp.where(upper, roll(high, 16 * step, 1), low)
                parts[t + step] = jnp.where(upper, high, roll(low, -16 * step, 1))
    return parts


def scatter_kernel(iv_ref, out_ref, flipped_ref):
    for c in range(3):
        flipped_ref[...] = iv_ref[c].T
        for s in range(2):
            for h in range(2):
                out_ref[:, 2 * c + s, NQ * h : NQ * (h + 1)] = flipped_ref[
                    pl.ds(2 * s + h, 32, stride=4), :
                ]
    zero = jnp.zeros((32, 128), jnp.float32)
    out_ref[:, 6, :] = zero
    out_ref[:, 7, :] = zero


def strike_forward_kernel(
    in_ref, strike_ref, twiddle_ref, high_ref, low_ref, after_ref, also_ref, out_ref
):
    value = jnp.concatenate([in_ref[:, m, :] for m in range(6)], axis=1)
    value = stacked_dot(strike_ref[...], value)
    cos, sin = twiddle_ref[0], twiddle_ref[1]
    rows = []
    for m in range(6):
        real = value[:32, 128 * m : 128 * (m + 1)]
        imag = value[32:, 128 * m : 128 * (m + 1)]
        rows.append(
            jnp.concatenate([real * cos + imag * sin, imag * cos - real * sin], axis=1)
        )
    value = rows_dot(jnp.concatenate(rows, axis=0), high_ref[...], low_ref[...])
    zero = jnp.zeros((32, 128), jnp.float32)
    for t in range(2):
        parts = [value[32 * m : 32 * (m + 1), 128 * t : 128 * (t + 1)] for m in range(6)]
        parts = block_transpose(parts + [zero, zero])
        for b in range(8):
            out_ref[32 * (8 * t + b) : 32 * (8 * t + b + 1), :] = parts[b]


def strike_inverse_kernel(
    in_ref, strike_ref, twiddle_ref, high_ref, low_ref, after_ref, also_ref, out_ref
):
    columns = []
    for t in range(2):
        columns.append(
            block_transpose([in_ref[32 * (8 * t + b) : 32 * (8 * t + b + 1), :] for b in range(8)])
        )
    rows = [jnp.concatenate([columns[0][m], columns[1][m]], axis=1) for m in range(8)]
    value = rows_dot(jnp.concatenate(rows, axis=0), high_ref[...], low_ref[...])
    cos, sin = twiddle_ref[0], twiddle_ref[1]
    reals, imags = [], []
    for m in range(8):
        real = value[32 * m : 32 * (m + 1), :128]
        imag = value[32 * m : 32 * (m + 1), 128:]
        reals.append(real * cos - imag * sin)
        imags.append(imag * cos + real * sin)
    value = jnp.concatenate(
        [jnp.concatenate(reals, axis=1), jnp.concatenate(imags, axis=1)], axis=0
    )
    value = stacked_dot(strike_ref[...], value)
    parts = [value[:, 128 * m : 128 * (m + 1)] for m in range(8)]
    lane = lane_of((32, 128))
    last = parts[7]
    for m in range(6):
        before = roll(parts[m], 1, 0)
        after = roll(parts[m], -1, 0)
        for h in range(2):
            to = 64 + 2 * (2 * m + h)
            last = jnp.where(lane == to, roll(before, to - (NQ * h + 63), 1), last)
            last = jnp.where(lane == to + 1, roll(after, to + 1 - NQ * h, 1), last)
    parts[7] = last
    for m in range(8):
        out_ref[:, m, :] = parts[m]


def dip_kernel(
    in_ref, weight_ref, past_ref, twiddle_ref, inner_ref,
    fh_ref, fl_ref, ih_ref, il_ref, after_ref, also_ref, out_ref,
):
    flipped = in_ref[...].T
    values = []
    for v in range(4):
        lanes = slice(128 * v, 128 * (v + 1))
        values.append(
            [
                jnp.concatenate(
                    [flipped[16 * m + 8 * ri : 16 * m + 8 * ri + 8, lanes] for m in range(6)],
                    axis=0,
                )
                for ri in range(2)
            ]
        )
    inner = [(inner_ref[b, 0:1, :], inner_ref[b, 1:2, :]) for b in range(4)]
    values = radix_four(values, -1)
    values = [turn(*values[b], *inner[b], -1) for b in range(4)]
    values = dip_transform(values, fh_ref[...], fl_ref[...], -1)
    real = jnp.concatenate([pair[0] for pair in values], axis=1)
    imag = jnp.concatenate([pair[1] for pair in values], axis=1)
    top = row_of((8, NF)) < 4
    sign = jnp.where(top, 1.0, -1.0).astype(jnp.float32)
    reals, imags = [], []
    for c in range(3):
        turned = []
        for s in range(2):
            rows = slice(16 * c + 8 * s, 16 * c + 8 * s + 8)
            turned.append(turn(real[rows], imag[rows], twiddle_ref[s, 0], twiddle_ref[s, 1], -1))
        even = [turned[0][ri] + turned[1][ri] for ri in range(2)]
        odd = [turned[0][ri] - turned[1][ri] for ri in range(2)]
        odd = [jnp.where(top, odd[0], odd[1]), jnp.where(top, odd[1], -odd[0])]
        response = []
        for parity, value in enumerate((even, odd)):
            spectrum = [roll(part, 4, 0) + sign * part for part in value]
            response.append(
                [
                    weight_ref[parity] * spectrum[ri] + past_ref[c, parity, ri]
                    for ri in range(2)
                ]
            )
        response = [[roll(part, 4, 0) + sign * part for part in pair] for pair in response]
        even = response[0]
        odd = [
            jnp.where(top, response[1][0], -response[1][1]),
            jnp.where(top, response[1][1], response[1][0]),
        ]
        for s in range(2):
            pair = [even[ri] + odd[ri] if s == 0 else even[ri] - odd[ri] for ri in range(2)]
            pair = turn(*pair, twiddle_ref[s, 0], twiddle_ref[s, 1], 1)
            reals.append(pair[0])
            imags.append(pair[1])
    real, imag = jnp.concatenate(reals, axis=0), jnp.concatenate(imags, axis=0)
    values = [
        (real[:, 128 * b : 128 * (b + 1)], imag[:, 128 * b : 128 * (b + 1)]) for b in range(4)
    ]
    values = dip_transform(values, ih_ref[...], il_ref[...], 1)
    values = [turn(*values[b], *inner[b], 1) for b in range(4)]
    values = radix_four(values, 1)
    real = jnp.concatenate([pair[0] for pair in values], axis=1)
    imag = jnp.concatenate([pair[1] for pair in values], axis=1)
    groups = []
    for m in range(6):
        groups += [real[8 * m : 8 * m + 8], imag[8 * m : 8 * m + 8]]
    early = lane_of((8, NF)) % 32 < 16
    edges = []
    for c in range(3):
        for ri in range(2):
            before = roll(roll(groups[4 * c + 2 + ri], 4, 0), 1, 1)
            after = roll(groups[4 * c + ri], -1, 1)
            edges.append(jnp.where(early, before, after))
    for ri in range(2):
        groups.append(jnp.where(top, edges[ri], roll(edges[2 + ri], 4, 0)))
    for ri in range(2):
        groups.append(jnp.where(top, edges[4 + ri], 0.0))
    out_ref[...] = jnp.concatenate(groups, axis=0).T


def mode_groups(tiles, rows_ref):
    for a in range(4):
        rows_ref[:, a, :] = tiles[a]
        rows_ref[:, 4 + a, :] = tiles[a]
    block = lane_of((8, 128)) // 32
    top = row_of((8, 128)) < 4
    columns = []
    for t in range(4):
        parts = [rows_ref[4 * n + t] for n in range(4)]
        for step in (1, 2):
            upper = (block // step) % 2 == 1
            for n in range(4):
                if (n // step) % 2 == 0:
                    low, high = parts[n], parts[n + step]
                    parts[n] = jnp.where(upper, roll(high, 32 * step, 1), low)
                    parts[n + step] = jnp.where(upper, high, roll(low, -32 * step, 1))
        columns.append([jnp.where(top, parts[n], parts[2 + n]) for n in range(2)])
    return [jnp.concatenate([column[n] for column in columns], axis=1) for n in range(2)]


def past_kernel(kernel_ref, history_ref, weight_ref, out_ref, rows_ref):
    groups = mode_groups([kernel_ref[0, a, 0] for a in range(4)], rows_ref.at[6])
    for parity in range(2):
        weight_ref[parity] = groups[parity]
    for z in range(2):
        for c in range(3):
            tiles = []
            for a in range(4):
                total = kernel_ref[1, a, 0] * history_ref[0, z, c, a, 0]
                for h in range(1, 6):
                    total = total + kernel_ref[h + 1, a, 0] * history_ref[h, z, c, a, 0]
                tiles.append(total)
            groups = mode_groups(tiles, rows_ref.at[3 * z + c])
            for parity in range(2):
                out_ref[c, parity, z] = groups[parity]


def strike_edges(fields_ref, chosen):
    pad = jnp.zeros((4, 128), jnp.float32)
    low = [fields_ref[n, z, 0:1, :] for n in chosen for z in range(4)]
    high = [fields_ref[n, z, 63:64, :] for n in chosen for z in range(4)]
    return jnp.concatenate(low + [pad], axis=0), jnp.concatenate(high + [pad], axis=0)


def dip_edges(fields_ref, chosen):
    lane = lane_of((64, 128))
    low = jnp.zeros((64, 128), jnp.float32)
    high = jnp.zeros((64, 128), jnp.float32)
    for i, n in enumerate(chosen):
        for z in range(4):
            to = 4 * i + z
            low = jnp.where(lane == to, roll(fields_ref[n, z], to, 1), low)
            high = jnp.where(lane == to, roll(fields_ref[n, z], to - 127, 1), high)
    return low, high


def strike_edge_kernel(fields_ref, low_ref, high_ref):
    low_ref[...], high_ref[...] = strike_edges(fields_ref, (0, 3, 4))


def dip_edge_kernel(fields_ref, after_ref, low_ref, high_ref):
    low_ref[...], high_ref[...] = dip_edges(fields_ref, (3, 1, 5))


def hold_kernel(low_ref, high_ref, after_ref, low_out_ref, high_out_ref):
    low_out_ref[...] = low_ref[...]
    high_out_ref[...] = high_ref[...]


def strike_diff(field, low, high):
    row = row_of(field.shape)
    before = jnp.where(row == 0, low, roll(field, 1, 0))
    after = jnp.where(row == 63, high, roll(field, -1, 0))
    return 0.5 * (after - before)


def dip_diff(field, low, high, to):
    lane = lane_of(field.shape)
    before = jnp.where(lane == 0, roll(low, -to, 1), roll(field, 1, 1))
    after = jnp.where(lane == 127, roll(high, 127 - to, 1), roll(field, -1, 1))
    return 0.5 * (after - before)


def velocity_kernel(
    velocity_ref, stress_ref, xlo_ref, xhi_ref, ylo_ref, yhi_ref,
    out_ref, xlo_out_ref, xhi_out_ref, ylo_out_ref, yhi_out_ref,
):
    across, along, deep = (0, 3, 4), (3, 1, 5), (4, 5, 2)
    ylo, yhi = ylo_ref[...], yhi_ref[...]
    for n in range(3):
        for z in range(4):
            at = 4 * n + z
            total = strike_diff(
                stress_ref[across[n], z], xlo_ref[at : at + 1], xhi_ref[at : at + 1]
            ) + dip_diff(stress_ref[along[n], z], ylo, yhi, at)
            if z < 3:
                total = total + 0.5 * stress_ref[deep[n], z + 1]
            if z > 0:
                total = total - 0.5 * stress_ref[deep[n], z - 1]
            out_ref[n, z] = velocity_ref[n, z] + COURANT * total
    xlo_out_ref[...], xhi_out_ref[...] = strike_edges(out_ref, (0, 1, 2))
    ylo_out_ref[...], yhi_out_ref[...] = dip_edges(out_ref, (0, 1, 2))


def slab_kernel(
    in_ref, before_ref, stress_ref, cohesion_ref, iv_ref,
    xlo_ref, xhi_ref, ylo_ref, yhi_ref,
    velocity_ref, out_ref, flipped_ref, edge_ref,
):
    last = in_ref[:, 7, :]
    xlo, xhi = [], []
    half = lane_of((32, 128)) < 64
    edge_ref[...] = jnp.zeros((128, 128), jnp.float32)
    for c in range(3):
        for s in range(2):
            for h in range(2):
                to = pl.ds(2 * s + h, 32, stride=4)
                piece = in_ref[:, 2 * c + s, :]
                piece = roll(piece, 64, 1) if h else piece
                shifted = roll(last, -2 * (4 * c + 2 * s + h), 1)
                flipped_ref[to, :] = jnp.where(half, piece, shifted)
        m, h = 6 + c // 2, c % 2
        edge_ref[4 * c : 4 * c + 1, 0:64] = in_ref[0, m : m + 1, NQ * h : NQ * (h + 1)]
        edge_ref[12 + 4 * c : 13 + 4 * c, 0:64] = in_ref[31, m : m + 1, NQ * h : NQ * (h + 1)]
        traction = flipped_ref[...].T
        velocity_ref[c, 0] = before_ref[c, 0] - 0.5 * COURANT * traction[:64]
        xlo.append(traction[64:65])
        xhi.append(traction[65:66])
        for z in range(1, 4):
            velocity_ref[c, z] = before_ref[c, z]
    edges = edge_ref[...].T[:64]
    lane = lane_of((64, 128))
    ylo = ylo_ref[...] - 0.5 * COURANT * jnp.where(lane < 12, edges, 0.0)
    yhi = yhi_ref[...] - 0.5 * COURANT * jnp.where(lane < 12, roll(edges, -12, 1), 0.0)
    for z in range(4):
        dx, dy, dz = [], [], []
        for c in range(3):
            field = velocity_ref[c, z]
            at = 4 * c + z
            low, high = xlo_ref[at : at + 1], xhi_ref[at : at + 1]
            if z == 0:
                low = low - 0.5 * COURANT * xlo[c]
                high = high - 0.5 * COURANT * xhi[c]
            dx.append(strike_diff(field, low, high))
            dy.append(dip_diff(field, ylo, yhi, at))
            under = iv_ref[c] if z == 0 else velocity_ref[c, z - 1]
            if z < 3:
                dz.append(0.5 * (velocity_ref[c, z + 1] - under))
            else:
                dz.append(-0.5 * under)
        dilation = dx[0] + dy[1] + dz[2]
        rates = [
            dilation + 2.0 * dx[0],
            dilation + 2.0 * dy[1],
            dilation + 2.0 * dz[2],
            dy[0] + dx[1],
            dz[0] + dx[2],
            dz[1] + dy[2],
        ]
        trial = [stress_ref[n, z] + COURANT * rates[n] for n in range(6)]
        pressure = (trial[0] + trial[1] + trial[2]) * (1.0 / 3.0)
        normal = [trial[n] - pressure for n in range(3)]
        second = 0.5 * (
            normal[0] * normal[0] + normal[1] * normal[1] + normal[2] * normal[2]
        ) + (trial[3] * trial[3] + trial[4] * trial[4] + trial[5] * trial[5])
        shear = jnp.sqrt(second)
        limit = cohesion_ref[z] + FRICTION * jnp.maximum(-pressure, 0.0)
        factor = limit / jnp.maximum(shear, limit)
        for n in range(3):
            out_ref[n, z] = pressure + factor * normal[n]
            out_ref[3 + n, z] = factor * trial[3 + n]


def f32(*shape):
    return jax.ShapeDtypeStruct(shape, jnp.float32)


def call(kernel, out_shape, arguments, after=(), scratch=()):
    many = isinstance(out_shape, tuple)
    return pl.pallas_call(
        kernel,
        out_shape=out_shape,
        in_specs=[VMEM] * len(arguments) + [pl.BlockSpec(memory_space=pl.ANY)] * len(after),
        out_specs=(VMEM,) * len(out_shape) if many else VMEM,
        scratch_shapes=list(scratch),
        compiler_params=PARAMS,
    )(*arguments, *after)


def scatter(iv):
    return call(
        scatter_kernel, f32(32, 8, 128), (iv,), scratch=[pltpu.VMEM((128, 64), jnp.float32)]
    )


def strike_forward(arrived, after):
    forward, _ = strike_tables()
    (high, low), _ = cell_tables()
    arguments = (arrived, forward, strike_twiddle(), high, low)
    return call(strike_forward_kernel, f32(512, 128), arguments, after)


def strike_inverse(arrived, after):
    _, inverse = strike_tables()
    _, (high, low) = cell_tables()
    arguments = (arrived, inverse, strike_twiddle(), high, low)
    return call(strike_inverse_kernel, f32(32, 8, 128), arguments, after)


def dip(arrived, weight, past, after):
    tables = (dip_twiddle(), dip_inner_twiddle(), *dip_tables())
    arguments = (arrived, weight, past, *tables)
    return call(dip_kernel, f32(512, 128), arguments, after)


def past_terms(kernel, history):
    return call(
        past_kernel,
        (f32(2, 8, NF), f32(3, 2, 2, 8, NF)),
        (kernel, history),
        scratch=[pltpu.VMEM((7, 16, 8, 128), jnp.float32)],
    )


def stress_strike_edges(stress):
    return call(strike_edge_kernel, (f32(16, 128),) * 2, (stress,))


def stress_dip_edges(stress, after):
    return call(dip_edge_kernel, (f32(64, 128),) * 2, (stress,), (after,))


def hold(low, high, after):
    return call(hold_kernel, (f32(*low.shape),) * 2, (low, high), (after,))


def velocity_before(velocity, stress, halo):
    return call(
        velocity_kernel,
        (f32(3, 4, 64, 128), f32(16, 128), f32(16, 128), f32(64, 128), f32(64, 128)),
        (velocity, stress, *halo),
    )


def slab(arrived, before, stress, cohesion, iv, halo):
    return call(
        slab_kernel,
        (f32(3, 4, 64, 128), f32(6, 4, 64, 128)),
        (arrived, before, stress, cohesion, iv, *halo),
        scratch=[pltpu.VMEM((128, 128), jnp.float32), pltpu.VMEM((128, 128), jnp.float32)],
    )


def exchange(axis, low, high):
    count = lax.axis_size(axis)
    return (
        lax.ppermute(high, axis, [(i, (i + 1) % count) for i in range(count)]),
        lax.ppermute(low, axis, [(i, (i - 1) % count) for i in range(count)]),
    )


def strike_swap(value):
    return lax.all_to_all(value, "bx", split_axis=0, concat_axis=0, tiled=True)


def whole_swap(value):
    value = value.reshape(512, 1, 128)
    value = lax.all_to_all(value, ("by", "bx"), split_axis=0, concat_axis=0, tiled=True)
    return value.reshape(512, 128)


def local(interface_velocity, history, kernel, velocity, stress, cohesion):
    arrived = strike_swap(scatter(interface_velocity))
    strike_halo = exchange("bx", *stress_strike_edges(stress))
    sent = strike_forward(arrived, strike_halo)
    arrived = whole_swap(sent)
    dip_halo = exchange("by", *stress_dip_edges(stress, sent))
    weight, past = past_terms(kernel, history)
    sent = dip(arrived, weight, past, dip_halo)
    arrived = whole_swap(sent)
    before, *edges = velocity_before(velocity, stress, (*strike_halo, *dip_halo))
    strike_halo = exchange("bx", *hold(edges[0], edges[1], sent))
    sent = strike_inverse(arrived, strike_halo)
    arrived = strike_swap(sent)
    dip_halo = exchange("by", *hold(edges[2], edges[3], sent))
    return slab(
        arrived, before, stress, cohesion, interface_velocity, (*strike_halo, *dip_halo)
    )


def solution(mesh):
    return jax.shard_map(
        local,
        mesh=mesh,
        in_specs=(
            P(None, "bx", "by"),
            P(None, None, None, "by", "bx", None, None),
            P(None, "by", "bx", None, None),
            P(None, None, "bx", "by"),
            P(None, None, "bx", "by"),
            P(None, "bx", "by"),
        ),
        out_specs=(P(None, None, "bx", "by"), P(None, None, "bx", "by")),
        check_vma=False,
    )
```

```python
import jax
import jax.numpy as jnp
import ml_dtypes
import numpy as np
from jax import lax
from jax.experimental import pallas as pl
from jax.experimental.pallas import tpu as pltpu
from jax.sharding import PartitionSpec as P

COURANT = 0.3
FRICTION = 0.6
NP_, NQ = 32, 64
NJ = 16
NF = 512
SCALE = 1.0 / 2048.0
VMEM = pl.BlockSpec(memory_space=pltpu.VMEM)
PARAMS = pltpu.CompilerParams(vmem_limit_bytes=16 * 1024 * 1024)


def split_table(table):
    high = table.astype(ml_dtypes.bfloat16)
    low = (table - high.astype(np.float64)).astype(ml_dtypes.bfloat16)
    return high, low


def angles(rows, cols, length):
    return 2.0 * np.pi / length * ((rows[:, None] * cols[None, :]) % length)


def strike_tables():
    theta = angles(np.arange(32), np.arange(32), 32)
    cos, sin = np.cos(theta), np.sin(theta)
    high, low = split_table(np.concatenate([cos, -sin], axis=0))
    forward = np.concatenate([high, high, low], axis=1)
    high, low = split_table(np.concatenate([cos, -sin], axis=1))
    inverse = np.concatenate([high, high, low], axis=1)
    return forward, inverse


def strike_twiddle():
    theta = angles(np.arange(32), np.arange(64), 2048)
    theta = np.concatenate([theta, theta], axis=1)
    return np.stack([np.cos(theta), np.sin(theta)]).astype(np.float32)


def cell_tables():
    theta = angles(np.arange(64), np.arange(64), 64).reshape(64, 16, 4)
    cos, sin = np.cos(theta) * SCALE, np.sin(theta) * SCALE
    table = np.zeros((2, 2, 64, 16, 2, 2, 4))
    for h in range(2):
        table[0, h, :, :, 0, h] = cos
        table[1, h, :, :, 0, h] = sin
        table[0, h, :, :, 1, h] = -sin
        table[1, h, :, :, 1, h] = cos
    table = table.reshape(256, 256)
    return split_table(table), split_table(np.ascontiguousarray(table.T))


def dip_order():
    lane = np.arange(128)
    return 4 * (lane % 32) + lane // 32


def dip_tables():
    theta = angles(np.arange(128), dip_order(), 128)
    forward = np.concatenate([np.cos(theta), np.sin(theta)], axis=1)
    inverse = np.concatenate([np.cos(theta).T, np.sin(theta).T], axis=1)
    return split_table(forward) + split_table(inverse)


def dip_inner_twiddle():
    theta = angles(np.arange(4), np.arange(128), 512)
    return np.stack([np.cos(theta), np.sin(theta)], axis=1).astype(np.float32)


def dip_twiddle():
    f = (4 * dip_order()[None, :] + np.arange(4)[:, None]).reshape(NF)
    theta = angles(np.arange(4), f, 2048).reshape(2, 2, 1, NF)
    theta = np.broadcast_to(theta, (2, 2, 4, NF)).reshape(2, 8, NF)
    return np.stack([np.cos(theta), np.sin(theta)], axis=1).astype(np.float32)


def halves(value):
    high = value.astype(jnp.bfloat16)
    low = (value - high.astype(jnp.float32)).astype(jnp.bfloat16)
    return high, low


def dot(a, b):
    return jnp.dot(a, b, preferred_element_type=jnp.float32)


def stacked_dot(table, value):
    high, low = halves(value)
    return dot(table, jnp.concatenate([high, low, high], axis=0))


def rows_dot(value, table_high, table_low):
    rows = value.shape[0]
    high, low = halves(value)
    both = dot(jnp.concatenate([high, low], axis=0), table_high)
    return both[:rows] + both[rows:] + dot(high, table_low)


def radix_four(values, sign):
    (r0, i0), (r1, i1), (r2, i2), (r3, i3) = values
    ar, ai, br, bi = r0 + r2, i0 + i2, r0 - r2, i0 - i2
    cr, ci, dr, di = r1 + r3, i1 + i3, sign * (r1 - r3), sign * (i1 - i3)
    return [
        (ar + cr, ai + ci),
        (br - di, bi + dr),
        (ar - cr, ai - ci),
        (br + di, bi - dr),
    ]


def turn(real, imag, cos, sin, sign):
    if sign > 0:
        return real * cos - imag * sin, imag * cos + real * sin
    return real * cos + imag * sin, imag * cos - real * sin


def dip_transform(values, high, low, sign):
    stacked = jnp.concatenate([part for pair in values for part in pair], axis=0)
    product = rows_dot(stacked, high, low)
    out = []
    for n in range(4):
        real, imag = product[96 * n : 96 * n + 48], product[96 * n + 48 : 96 * (n + 1)]
        out.append(
            (
                real[:, :128] - sign * imag[:, 128:],
                imag[:, :128] + sign * real[:, 128:],
            )
        )
    return out


def roll(value, shift, axis):
    return pltpu.roll(value, shift % value.shape[axis], axis)


def lane_of(shape):
    return lax.broadcasted_iota(jnp.int32, shape, len(shape) - 1)


def row_of(shape):
    return lax.broadcasted_iota(jnp.int32, shape, len(shape) - 2)


def block_transpose(parts):
    parts = list(parts)
    block = lane_of(parts[0].shape) // 16
    for step in (1, 2, 4):
        upper = (block // step) % 2 == 1
        for t in range(8):
            if (t // step) % 2 == 0:
                low, high = parts[t], parts[t + step]
                parts[t] = jnp.where(upper, roll(high, 16 * step, 1), low)
                parts[t + step] = jnp.where(upper, high, roll(low, -16 * step, 1))
    return parts


def scatter_kernel(iv_ref, after_ref, out_ref, flipped_ref):
    for c in range(3):
        flipped_ref[...] = iv_ref[c].T
        for s in range(2):
            for h in range(2):
                out_ref[:, 2 * c + s, NQ * h : NQ * (h + 1)] = flipped_ref[
                    pl.ds(2 * s + h, 32, stride=4), :
                ]
    zero = jnp.zeros((32, 128), jnp.float32)
    out_ref[:, 6, :] = zero
    out_ref[:, 7, :] = zero


def strike_forward_kernel(
    in_ref, strike_ref, twiddle_ref, high_ref, low_ref, after_ref, also_ref, out_ref
):
    value = jnp.concatenate([in_ref[:, m, :] for m in range(6)], axis=1)
    value = stacked_dot(strike_ref[...], value)
    cos, sin = twiddle_ref[0], twiddle_ref[1]
    rows = []
    for m in range(6):
        real = value[:32, 128 * m : 128 * (m + 1)]
        imag = value[32:, 128 * m : 128 * (m + 1)]
        rows.append(
            jnp.concatenate([real * cos + imag * sin, imag * cos - real * sin], axis=1)
        )
    value = rows_dot(jnp.concatenate(rows, axis=0), high_ref[...], low_ref[...])
    zero = jnp.zeros((32, 128), jnp.float32)
    for t in range(2):
        parts = [value[32 * m : 32 * (m + 1), 128 * t : 128 * (t + 1)] for m in range(6)]
        parts = block_transpose(parts + [zero, zero])
        for b in range(8):
            out_ref[32 * (8 * t + b) : 32 * (8 * t + b + 1), :] = parts[b]


def strike_inverse_kernel(
    in_ref, strike_ref, twiddle_ref, high_ref, low_ref, out_ref
):
    columns = []
    for t in range(2):
        columns.append(
            block_transpose([in_ref[32 * (8 * t + b) : 32 * (8 * t + b + 1), :] for b in range(8)])
        )
    rows = [jnp.concatenate([columns[0][m], columns[1][m]], axis=1) for m in range(8)]
    value = rows_dot(jnp.concatenate(rows, axis=0), high_ref[...], low_ref[...])
    cos, sin = twiddle_ref[0], twiddle_ref[1]
    reals, imags = [], []
    for m in range(8):
        real = value[32 * m : 32 * (m + 1), :128]
        imag = value[32 * m : 32 * (m + 1), 128:]
        reals.append(real * cos - imag * sin)
        imags.append(imag * cos + real * sin)
    value = jnp.concatenate(
        [jnp.concatenate(reals, axis=1), jnp.concatenate(imags, axis=1)], axis=0
    )
    value = stacked_dot(strike_ref[...], value)
    parts = [value[:, 128 * m : 128 * (m + 1)] for m in range(8)]
    lane = lane_of((32, 128))
    last = parts[7]
    for m in range(6):
        before = roll(parts[m], 1, 0)
        after = roll(parts[m], -1, 0)
        for h in range(2):
            to = 64 + 2 * (2 * m + h)
            last = jnp.where(lane == to, roll(before, to - (NQ * h + 63), 1), last)
            last = jnp.where(lane == to + 1, roll(after, to + 1 - NQ * h, 1), last)
    parts[7] = last
    for m in range(8):
        out_ref[:, m, :] = parts[m]


def dip_kernel(
    in_ref, weight_ref, past_ref, twiddle_ref, inner_ref,
    fh_ref, fl_ref, ih_ref, il_ref, after_ref, also_ref, out_ref,
):
    flipped = in_ref[...].T
    values = []
    for v in range(4):
        lanes = slice(128 * v, 128 * (v + 1))
        values.append(
            [
                jnp.concatenate(
                    [flipped[16 * m + 8 * ri : 16 * m + 8 * ri + 8, lanes] for m in range(6)],
                    axis=0,
                )
                for ri in range(2)
            ]
        )
    inner = [(inner_ref[b, 0:1, :], inner_ref[b, 1:2, :]) for b in range(4)]
    values = radix_four(values, -1)
    values = [turn(*values[b], *inner[b], -1) for b in range(4)]
    values = dip_transform(values, fh_ref[...], fl_ref[...], -1)
    real = jnp.concatenate([pair[0] for pair in values], axis=1)
    imag = jnp.concatenate([pair[1] for pair in values], axis=1)
    top = row_of((8, NF)) < 4
    sign = jnp.where(top, 1.0, -1.0).astype(jnp.float32)
    reals, imags = [], []
    for c in range(3):
        turned = []
        for s in range(2):
            rows = slice(16 * c + 8 * s, 16 * c + 8 * s + 8)
            turned.append(turn(real[rows], imag[rows], twiddle_ref[s, 0], twiddle_ref[s, 1], -1))
        even = [turned[0][ri] + turned[1][ri] for ri in range(2)]
        odd = [turned[0][ri] - turned[1][ri] for ri in range(2)]
        odd = [jnp.where(top, odd[0], odd[1]), jnp.where(top, odd[1], -odd[0])]
        response = []
        for parity, value in enumerate((even, odd)):
            spectrum = [roll(part, 4, 0) + sign * part for part in value]
            response.append(
                [
                    weight_ref[parity] * spectrum[ri] + past_ref[c, parity, ri]
                    for ri in range(2)
                ]
            )
        response = [[roll(part, 4, 0) + sign * part for part in pair] for pair in response]
        even = response[0]
        odd = [
            jnp.where(top, response[1][0], -response[1][1]),
            jnp.where(top, response[1][1], response[1][0]),
        ]
        for s in range(2):
            pair = [even[ri] + odd[ri] if s == 0 else even[ri] - odd[ri] for ri in range(2)]
            pair = turn(*pair, twiddle_ref[s, 0], twiddle_ref[s, 1], 1)
            reals.append(pair[0])
            imags.append(pair[1])
    real, imag = jnp.concatenate(reals, axis=0), jnp.concatenate(imags, axis=0)
    values = [
        (real[:, 128 * b : 128 * (b + 1)], imag[:, 128 * b : 128 * (b + 1)]) for b in range(4)
    ]
    values = dip_transform(values, ih_ref[...], il_ref[...], 1)
    values = [turn(*values[b], *inner[b], 1) for b in range(4)]
    values = radix_four(values, 1)
    real = jnp.concatenate([pair[0] for pair in values], axis=1)
    imag = jnp.concatenate([pair[1] for pair in values], axis=1)
    groups = []
    for m in range(6):
        groups += [real[8 * m : 8 * m + 8], imag[8 * m : 8 * m + 8]]
    early = lane_of((8, NF)) % 32 < 16
    edges = []
    for c in range(3):
        for ri in range(2):
            before = roll(roll(groups[4 * c + 2 + ri], 4, 0), 1, 1)
            after = roll(groups[4 * c + ri], -1, 1)
            edges.append(jnp.where(early, before, after))
    for ri in range(2):
        groups.append(jnp.where(top, edges[ri], roll(edges[2 + ri], 4, 0)))
    for ri in range(2):
        groups.append(jnp.where(top, edges[4 + ri], 0.0))
    out_ref[...] = jnp.concatenate(groups, axis=0).T


def mode_groups(tiles, rows_ref):
    for a in range(4):
        rows_ref[:, a, :] = tiles[a]
        rows_ref[:, 4 + a, :] = tiles[a]
    block = lane_of((8, 128)) // 32
    top = row_of((8, 128)) < 4
    columns = []
    for t in range(4):
        parts = [rows_ref[4 * n + t] for n in range(4)]
        for step in (1, 2):
            upper = (block // step) % 2 == 1
            for n in range(4):
                if (n // step) % 2 == 0:
                    low, high = parts[n], parts[n + step]
                    parts[n] = jnp.where(upper, roll(high, 32 * step, 1), low)
                    parts[n + step] = jnp.where(upper, high, roll(low, -32 * step, 1))
        columns.append([jnp.where(top, parts[n], parts[2 + n]) for n in range(2)])
    return [jnp.concatenate([column[n] for column in columns], axis=1) for n in range(2)]


def past_kernel(kernel_ref, history_ref, weight_ref, out_ref, rows_ref):
    groups = mode_groups([kernel_ref[0, a, 0] for a in range(4)], rows_ref.at[6])
    for parity in range(2):
        weight_ref[parity] = groups[parity]
    for z in range(2):
        for c in range(3):
            tiles = []
            for a in range(4):
                total = kernel_ref[1, a, 0] * history_ref[0, z, c, a, 0]
                for h in range(1, 6):
                    total = total + kernel_ref[h + 1, a, 0] * history_ref[h, z, c, a, 0]
                tiles.append(total)
            groups = mode_groups(tiles, rows_ref.at[3 * z + c])
            for parity in range(2):
                out_ref[c, parity, z] = groups[parity]


ACROSS, ALONG, DEEP = (0, 3, 4), (3, 1, 5), (4, 5, 2)
STEP = 0.5 * COURANT


def pack_columns(stress_ref, part_ref, side):
    lane = lane_of((64, 128))
    total = jnp.zeros((64, 128), jnp.float32)
    for n in range(3):
        for z in range(4):
            fields = (stress_ref[ALONG[n], z], part_ref[n, z], stress_ref[ACROSS[n], z])
            for i in range(3):
                to = 12 * i + 4 * n + z
                total = jnp.where(lane == to, roll(fields[i], to - side, 1), total)
    return total


def part_kernel(velocity_ref, stress_ref, part_ref, low_ref, high_ref):
    row, lane = row_of((64, 128)), lane_of((64, 128))
    for n in range(3):
        for z in range(4):
            across, along = stress_ref[ACROSS[n], z], stress_ref[ALONG[n], z]
            total = jnp.where(row == 63, 0.0, roll(across, -1, 0))
            total = total - jnp.where(row == 0, 0.0, roll(across, 1, 0))
            total = total + jnp.where(lane == 127, 0.0, roll(along, -1, 1))
            total = total - jnp.where(lane == 0, 0.0, roll(along, 1, 1))
            if z < 3:
                total = total + stress_ref[DEEP[n], z + 1]
            if z > 0:
                total = total - stress_ref[DEEP[n], z - 1]
            part_ref[n, z] = velocity_ref[n, z] + STEP * total
    low_ref[...] = pack_columns(stress_ref, part_ref, 0)
    high_ref[...] = pack_columns(stress_ref, part_ref, 127)


def column_kernel(part_ref, stress_ref, ylo_ref, yhi_ref, out_ref, low_ref, high_ref):
    lane = lane_of((64, 128))
    ylo, yhi = ylo_ref[...], yhi_ref[...]
    edges = [[], []]
    for n in range(3):
        for z in range(4):
            at = 4 * n + z
            field = part_ref[n, z]
            field = field - jnp.where(lane == 0, STEP * roll(ylo, -at, 1), 0.0)
            field = field + jnp.where(lane == 127, STEP * roll(yhi, 127 - at, 1), 0.0)
            out_ref[n, z] = field
            edges[0].append(field[0:1])
            edges[1].append(field[63:64])
    pad = jnp.zeros((6, 128), jnp.float32)
    for i, ref in enumerate((low_ref, high_ref)):
        at = 63 * i
        rows = [stress_ref[ACROSS[n], z, at : at + 1, :] for n in range(3) for z in range(4)]
        rows += edges[i] + [ylo[at : at + 1], yhi[at : at + 1], pad]
        ref[...] = jnp.concatenate(rows, axis=0)


def row_kernel(
    part_ref, xlo_ref, xhi_ref, ylo_ref, yhi_ref,
    own_xlo_ref, own_xhi_ref, own_ylo_ref, own_yhi_ref, after_ref,
    out_ref, vxlo_ref, vxhi_ref, vylo_ref, vyhi_ref,
):
    row = row_of((64, 128))
    for n in range(3):
        for z in range(4):
            at = 4 * n + z
            field = part_ref[n, z]
            field = field - jnp.where(row == 0, STEP * xlo_ref[at : at + 1, :], 0.0)
            field = field + jnp.where(row == 63, STEP * xhi_ref[at : at + 1, :], 0.0)
            out_ref[n, z] = field
    vxlo_ref[...] = xlo_ref[12:28, :] + STEP * own_xlo_ref[0:16, :]
    vxhi_ref[...] = xhi_ref[12:28, :] - STEP * own_xhi_ref[0:16, :]
    for side, ref in enumerate((vylo_ref, vyhi_ref)):
        corner = jnp.where(row == 63, STEP * xhi_ref[24 + side : 25 + side, :], 0.0)
        corner = corner - jnp.where(row == 0, STEP * xlo_ref[24 + side : 25 + side, :], 0.0)
        if side == 0:
            columns = roll(ylo_ref[...], -12, 1) + STEP * own_ylo_ref[...]
        else:
            columns = roll(yhi_ref[...], -12, 1) - STEP * own_yhi_ref[...]
        ref[...] = columns + roll(corner, -24, 1)


def strike_diff(field, low, high):
    row = row_of(field.shape)
    before = jnp.where(row == 0, low, roll(field, 1, 0))
    after = jnp.where(row == 63, high, roll(field, -1, 0))
    return 0.5 * (after - before)


def dip_diff(field, low, high, to):
    lane = lane_of(field.shape)
    before = jnp.where(lane == 0, roll(low, -to, 1), roll(field, 1, 1))
    after = jnp.where(lane == 127, roll(high, 127 - to, 1), roll(field, -1, 1))
    return 0.5 * (after - before)


def slab_kernel(
    in_ref, before_ref, stress_ref, cohesion_ref, iv_ref,
    xlo_ref, xhi_ref, ylo_ref, yhi_ref,
    velocity_ref, out_ref, flipped_ref, edge_ref,
):
    last = in_ref[:, 7, :]
    xlo, xhi = [], []
    half = lane_of((32, 128)) < 64
    edge_ref[...] = jnp.zeros((128, 128), jnp.float32)
    for c in range(3):
        for s in range(2):
            for h in range(2):
                to = pl.ds(2 * s + h, 32, stride=4)
                piece = in_ref[:, 2 * c + s, :]
                piece = roll(piece, 64, 1) if h else piece
                shifted = roll(last, -2 * (4 * c + 2 * s + h), 1)
                flipped_ref[to, :] = jnp.where(half, piece, shifted)
        m, h = 6 + c // 2, c % 2
        edge_ref[4 * c : 4 * c + 1, 0:64] = in_ref[0, m : m + 1, NQ * h : NQ * (h + 1)]
        edge_ref[12 + 4 * c : 13 + 4 * c, 0:64] = in_ref[31, m : m + 1, NQ * h : NQ * (h + 1)]
        traction = flipped_ref[...].T
        velocity_ref[c, 0] = before_ref[c, 0] - 0.5 * COURANT * traction[:64]
        xlo.append(traction[64:65])
        xhi.append(traction[65:66])
        for z in range(1, 4):
            velocity_ref[c, z] = before_ref[c, z]
    edges = edge_ref[...].T[:64]
    lane = lane_of((64, 128))
    ylo = ylo_ref[...] - 0.5 * COURANT * jnp.where(lane < 12, edges, 0.0)
    yhi = yhi_ref[...] - 0.5 * COURANT * jnp.where(lane < 12, roll(edges, -12, 1), 0.0)
    for z in range(4):
        dx, dy, dz = [], [], []
        for c in range(3):
            field = velocity_ref[c, z]
            at = 4 * c + z
            low, high = xlo_ref[at : at + 1], xhi_ref[at : at + 1]
            if z == 0:
                low = low - 0.5 * COURANT * xlo[c]
                high = high - 0.5 * COURANT * xhi[c]
            dx.append(strike_diff(field, low, high))
            dy.append(dip_diff(field, ylo, yhi, at))
            under = iv_ref[c] if z == 0 else velocity_ref[c, z - 1]
            if z < 3:
                dz.append(0.5 * (velocity_ref[c, z + 1] - under))
            else:
                dz.append(-0.5 * under)
        dilation = dx[0] + dy[1] + dz[2]
        rates = [
            dilation + 2.0 * dx[0],
            dilation + 2.0 * dy[1],
            dilation + 2.0 * dz[2],
            dy[0] + dx[1],
            dz[0] + dx[2],
            dz[1] + dy[2],
        ]
        trial = [stress_ref[n, z] + COURANT * rates[n] for n in range(6)]
        pressure = (trial[0] + trial[1] + trial[2]) * (1.0 / 3.0)
        normal = [trial[n] - pressure for n in range(3)]
        second = 0.5 * (
            normal[0] * normal[0] + normal[1] * normal[1] + normal[2] * normal[2]
        ) + (trial[3] * trial[3] + trial[4] * trial[4] + trial[5] * trial[5])
        shear = jnp.sqrt(second)
        limit = cohesion_ref[z] + FRICTION * jnp.maximum(-pressure, 0.0)
        factor = limit / jnp.maximum(shear, limit)
        for n in range(3):
            out_ref[n, z] = pressure + factor * normal[n]
            out_ref[3 + n, z] = factor * trial[3 + n]


def f32(*shape):
    return jax.ShapeDtypeStruct(shape, jnp.float32)


def call(kernel, out_shape, arguments, after=(), scratch=()):
    many = isinstance(out_shape, tuple)
    return pl.pallas_call(
        kernel,
        out_shape=out_shape,
        in_specs=[VMEM] * len(arguments) + [pl.BlockSpec(memory_space=pl.ANY)] * len(after),
        out_specs=(VMEM,) * len(out_shape) if many else VMEM,
        scratch_shapes=list(scratch),
        compiler_params=PARAMS,
    )(*arguments, *after)


def scatter(iv, after):
    scratch = [pltpu.VMEM((128, 64), jnp.float32)]
    return call(scatter_kernel, f32(32, 8, 128), (iv,), after, scratch)


def strike_forward(arrived, after):
    forward, _ = strike_tables()
    (high, low), _ = cell_tables()
    arguments = (arrived, forward, strike_twiddle(), high, low)
    return call(strike_forward_kernel, f32(512, 128), arguments, after)


def strike_inverse(arrived):
    _, inverse = strike_tables()
    _, (high, low) = cell_tables()
    arguments = (arrived, inverse, strike_twiddle(), high, low)
    return call(strike_inverse_kernel, f32(32, 8, 128), arguments)


def dip(arrived, weight, past, after):
    tables = (dip_twiddle(), dip_inner_twiddle(), *dip_tables())
    arguments = (arrived, weight, past, *tables)
    return call(dip_kernel, f32(512, 128), arguments, after)


def past_terms(kernel, history):
    return call(
        past_kernel,
        (f32(2, 8, NF), f32(3, 2, 2, 8, NF)),
        (kernel, history),
        scratch=[pltpu.VMEM((7, 16, 8, 128), jnp.float32)],
    )


def velocity_part(velocity, stress):
    return call(
        part_kernel,
        (f32(3, 4, 64, 128), f32(64, 128), f32(64, 128)),
        (velocity, stress),
    )


def velocity_columns(part, stress, halo):
    return call(
        column_kernel,
        (f32(3, 4, 64, 128), f32(32, 128), f32(32, 128)),
        (part, stress, *halo),
    )


def velocity_rows(part, halo, own, after):
    return call(
        row_kernel,
        (f32(3, 4, 64, 128), f32(16, 128), f32(16, 128), f32(64, 128), f32(64, 128)),
        (part, *halo, *own),
        (after,),
    )


def slab(arrived, before, stress, cohesion, iv, halo):
    return call(
        slab_kernel,
        (f32(3, 4, 64, 128), f32(6, 4, 64, 128)),
        (arrived, before, stress, cohesion, iv, *halo),
        scratch=[pltpu.VMEM((128, 128), jnp.float32), pltpu.VMEM((128, 128), jnp.float32)],
    )


def exchange(axis, low, high):
    count = lax.axis_size(axis)
    return (
        lax.ppermute(high, axis, [(i, (i + 1) % count) for i in range(count)]),
        lax.ppermute(low, axis, [(i, (i - 1) % count) for i in range(count)]),
    )


def strike_swap(value):
    return lax.all_to_all(value, "bx", split_axis=0, concat_axis=0, tiled=True)


def whole_swap(value):
    value = value.reshape(512, 1, 128)
    value = lax.all_to_all(value, ("by", "bx"), split_axis=0, concat_axis=0, tiled=True)
    return value.reshape(512, 128)


def local(interface_velocity, history, kernel, velocity, stress, cohesion):
    part, *own_columns = velocity_part(velocity, stress)
    columns = exchange("by", *own_columns)
    arrived = strike_swap(scatter(interface_velocity, (part,)))
    sent = strike_forward(arrived, columns)
    part, *own_rows = velocity_columns(part, stress, columns)
    rows = exchange("bx", *own_rows)
    arrived = whole_swap(sent)
    weight, past = past_terms(kernel, history)
    sent = dip(arrived, weight, past, rows)
    before, *halo = velocity_rows(part, (*rows, *columns), (*own_rows, *own_columns), sent)
    arrived = whole_swap(sent)
    arrived = strike_swap(strike_inverse(arrived))
    return slab(arrived, before, stress, cohesion, interface_velocity, halo)


def solution(mesh):
    return jax.shard_map(
        local,
        mesh=mesh,
        in_specs=(
            P(None, "bx", "by"),
            P(None, None, None, "by", "bx", None, None),
            P(None, "by", "bx", None, None),
            P(None, None, "bx", "by"),
            P(None, None, "bx", "by"),
            P(None, "bx", "by"),
        ),
        out_specs=(P(None, None, "bx", "by"), P(None, None, "bx", "by")),
        check_vma=False,
    )
```

```python
import jax
import jax.numpy as jnp
import numpy as np
from jax import lax
from jax.experimental import pallas as pl
from jax.experimental.pallas import tpu as pltpu
from jax.sharding import PartitionSpec as P

COURANT = 0.3
FRICTION = 0.6
NP_, NQ = 32, 64
NJ = 16
NF = 512
SCALE = 1.0 / 2048.0
VMEM = pl.BlockSpec(memory_space=pltpu.VMEM)
PARAMS = pltpu.CompilerParams(vmem_limit_bytes=16 * 1024 * 1024)


def angles(rows, cols, length):
    return 2.0 * np.pi / length * ((rows[:, None] * cols[None, :]) % length)


def stack(*tables):
    wide = [np.pad(table, ((0, 0), (0, 256 - table.shape[1]))) for table in tables]
    return np.concatenate(wide, axis=0).astype(np.float32)


def cell_table():
    theta = angles(np.arange(64), np.arange(64), 64).reshape(64, 16, 4)
    cos, sin = np.cos(theta) * SCALE, np.sin(theta) * SCALE
    table = np.zeros((2, 2, 64, 16, 2, 2, 4))
    for h in range(2):
        table[0, h, :, :, 0, h] = cos
        table[1, h, :, :, 0, h] = sin
        table[0, h, :, :, 1, h] = -sin
        table[1, h, :, :, 1, h] = cos
    return table.reshape(256, 256)


def strike_tables(inverse):
    theta = angles(np.arange(32), np.arange(32), 32)
    cos, sin = np.cos(theta), np.sin(theta)
    twiddle = angles(np.arange(32), np.arange(128) % 64, 2048)
    twiddle = np.concatenate([np.cos(twiddle), np.sin(twiddle)], axis=1)
    if inverse:
        return stack(cell_table().T, twiddle, np.concatenate([cos, -sin], axis=1))
    return stack(cell_table(), twiddle, np.concatenate([cos, -sin], axis=0))


def dip_order():
    lane = np.arange(128)
    return 4 * (lane % 32) + lane // 32


def dip_tables():
    theta = angles(np.arange(128), dip_order(), 128)
    forward = np.concatenate([np.cos(theta), np.sin(theta)], axis=1)
    inverse = np.concatenate([np.cos(theta).T, np.sin(theta).T], axis=1)
    theta = angles(np.arange(8), np.arange(128), 512)
    inner = np.concatenate([np.cos(theta), np.sin(theta)], axis=1)
    outer = []
    for b in range(4):
        for s in range(2):
            theta = angles(2 * s + np.arange(8) // 4, 4 * dip_order() + b, 2048)
            outer.append(np.concatenate([np.cos(theta), np.sin(theta)], axis=1))
    return stack(forward, inverse, inner, *outer)


def halves(value):
    high = value.astype(jnp.bfloat16)
    low = (value - high.astype(jnp.float32)).astype(jnp.bfloat16)
    return high, low


def dot(a, b):
    return jnp.dot(a, b, preferred_element_type=jnp.float32)


def stacked_dot(table, value):
    high, low = halves(value)
    table_high, table_low = halves(table)
    table = jnp.concatenate([table_high, table_high, table_low], axis=1)
    return dot(table, jnp.concatenate([high, low, high], axis=0))


def rows_dot(value, table):
    rows = value.shape[0]
    high, low = halves(value)
    table_high, table_low = halves(table)
    both = dot(jnp.concatenate([high, low], axis=0), table_high)
    return both[:rows] + both[rows:] + dot(high, table_low)


def radix_four(values, sign):
    (r0, i0), (r1, i1), (r2, i2), (r3, i3) = values
    ar, ai, br, bi = r0 + r2, i0 + i2, r0 - r2, i0 - i2
    cr, ci, dr, di = r1 + r3, i1 + i3, sign * (r1 - r3), sign * (i1 - i3)
    return [
        (ar + cr, ai + ci),
        (br - di, bi + dr),
        (ar - cr, ai - ci),
        (br + di, bi - dr),
    ]


def turn(real, imag, cos, sin, sign):
    if sign > 0:
        return real * cos - imag * sin, imag * cos + real * sin
    return real * cos + imag * sin, imag * cos - real * sin


def dip_transform(values, table, sign):
    stacked = jnp.concatenate([part for pair in values for part in pair], axis=0)
    product = rows_dot(stacked, table)
    out = []
    for n in range(4):
        real, imag = product[96 * n : 96 * n + 48], product[96 * n + 48 : 96 * (n + 1)]
        out.append(
            (
                real[:, :128] - sign * imag[:, 128:],
                imag[:, :128] + sign * real[:, 128:],
            )
        )
    return out


def roll(value, shift, axis):
    return pltpu.roll(value, shift % value.shape[axis], axis)


def lane_of(shape):
    return lax.broadcasted_iota(jnp.int32, shape, len(shape) - 1)


def row_of(shape):
    return lax.broadcasted_iota(jnp.int32, shape, len(shape) - 2)


def block_transpose(parts):
    parts = list(parts)
    block = lane_of(parts[0].shape) // 16
    for step in (1, 2, 4):
        upper = (block // step) % 2 == 1
        for t in range(8):
            if (t // step) % 2 == 0:
                low, high = parts[t], parts[t + step]
                parts[t] = jnp.where(upper, roll(high, 16 * step, 1), low)
                parts[t + step] = jnp.where(upper, high, roll(low, -16 * step, 1))
    return parts


def scatter_kernel(iv_ref, out_ref, flipped_ref):
    for c in range(3):
        flipped_ref[...] = iv_ref[c].T
        for s in range(2):
            for h in range(2):
                out_ref[:, 2 * c + s, NQ * h : NQ * (h + 1)] = flipped_ref[
                    pl.ds(2 * s + h, 32, stride=4), :
                ]
    zero = jnp.zeros((32, 128), jnp.float32)
    out_ref[:, 6, :] = zero
    out_ref[:, 7, :] = zero


def strike_forward_kernel(in_ref, table_ref, after_ref, also_ref, out_ref):
    value = jnp.concatenate([in_ref[:, m, :] for m in range(6)], axis=1)
    value = stacked_dot(table_ref[288:352, 0:32], value)
    cos, sin = table_ref[256:288, 0:128], table_ref[256:288, 128:256]
    rows = []
    for m in range(6):
        real = value[:32, 128 * m : 128 * (m + 1)]
        imag = value[32:, 128 * m : 128 * (m + 1)]
        rows.append(
            jnp.concatenate([real * cos + imag * sin, imag * cos - real * sin], axis=1)
        )
    value = rows_dot(jnp.concatenate(rows, axis=0), table_ref[0:256, :])
    zero = jnp.zeros((32, 128), jnp.float32)
    for t in range(2):
        parts = [value[32 * m : 32 * (m + 1), 128 * t : 128 * (t + 1)] for m in range(6)]
        parts = block_transpose(parts + [zero, zero])
        for b in range(8):
            out_ref[32 * (8 * t + b) : 32 * (8 * t + b + 1), :] = parts[b]


def strike_inverse_kernel(in_ref, table_ref, out_ref):
    columns = []
    for t in range(2):
        columns.append(
            block_transpose([in_ref[32 * (8 * t + b) : 32 * (8 * t + b + 1), :] for b in range(8)])
        )
    rows = [jnp.concatenate([columns[0][m], columns[1][m]], axis=1) for m in range(8)]
    value = rows_dot(jnp.concatenate(rows, axis=0), table_ref[0:256, :])
    cos, sin = table_ref[256:288, 0:128], table_ref[256:288, 128:256]
    reals, imags = [], []
    for m in range(8):
        real = value[32 * m : 32 * (m + 1), :128]
        imag = value[32 * m : 32 * (m + 1), 128:]
        reals.append(real * cos - imag * sin)
        imags.append(imag * cos + real * sin)
    value = jnp.concatenate(
        [jnp.concatenate(reals, axis=1), jnp.concatenate(imags, axis=1)], axis=0
    )
    value = stacked_dot(table_ref[288:320, 0:64], value)
    parts = [value[:, 128 * m : 128 * (m + 1)] for m in range(8)]
    lane = lane_of((32, 128))
    last = parts[7]
    for m in range(6):
        before = roll(parts[m], 1, 0)
        after = roll(parts[m], -1, 0)
        for h in range(2):
            to = 64 + 2 * (2 * m + h)
            last = jnp.where(lane == to, roll(before, to - (NQ * h + 63), 1), last)
            last = jnp.where(lane == to + 1, roll(after, to + 1 - NQ * h, 1), last)
    parts[7] = last
    for m in range(8):
        out_ref[:, m, :] = parts[m]


def dip_kernel(in_ref, weight_ref, past_ref, table_ref, after_ref, also_ref, out_ref):
    flipped = in_ref[...].T
    values = []
    for v in range(4):
        lanes = slice(128 * v, 128 * (v + 1))
        values.append(
            [
                jnp.concatenate(
                    [flipped[16 * m + 8 * ri : 16 * m + 8 * ri + 8, lanes] for m in range(6)],
                    axis=0,
                )
                for ri in range(2)
            ]
        )
    inner = [
        (table_ref[256 + b : 257 + b, 0:128], table_ref[256 + b : 257 + b, 128:256])
        for b in range(4)
    ]
    outer = []
    for s in range(2):
        at = [264 + 16 * b + 8 * s for b in range(4)]
        cos = jnp.concatenate([table_ref[n : n + 8, 0:128] for n in at], axis=1)
        outer.append((cos, jnp.concatenate([table_ref[n : n + 8, 128:256] for n in at], axis=1)))
    values = radix_four(values, -1)
    values = [turn(*values[b], *inner[b], -1) for b in range(4)]
    values = dip_transform(values, table_ref[0:128, :], -1)
    real = jnp.concatenate([pair[0] for pair in values], axis=1)
    imag = jnp.concatenate([pair[1] for pair in values], axis=1)
    top = row_of((8, NF)) < 4
    sign = jnp.where(top, 1.0, -1.0).astype(jnp.float32)
    reals, imags = [], []
    for c in range(3):
        turned = []
        for s in range(2):
            rows = slice(16 * c + 8 * s, 16 * c + 8 * s + 8)
            turned.append(turn(real[rows], imag[rows], *outer[s], -1))
        even = [turned[0][ri] + turned[1][ri] for ri in range(2)]
        odd = [turned[0][ri] - turned[1][ri] for ri in range(2)]
        odd = [jnp.where(top, odd[0], odd[1]), jnp.where(top, odd[1], -odd[0])]
        response = []
        for parity, value in enumerate((even, odd)):
            spectrum = [roll(part, 4, 0) + sign * part for part in value]
            response.append(
                [
                    weight_ref[parity] * spectrum[ri] + past_ref[c, parity, ri]
                    for ri in range(2)
                ]
            )
        response = [[roll(part, 4, 0) + sign * part for part in pair] for pair in response]
        even = response[0]
        odd = [
            jnp.where(top, response[1][0], -response[1][1]),
            jnp.where(top, response[1][1], response[1][0]),
        ]
        for s in range(2):
            pair = [even[ri] + odd[ri] if s == 0 else even[ri] - odd[ri] for ri in range(2)]
            pair = turn(*pair, *outer[s], 1)
            reals.append(pair[0])
            imags.append(pair[1])
    real, imag = jnp.concatenate(reals, axis=0), jnp.concatenate(imags, axis=0)
    values = [
        (real[:, 128 * b : 128 * (b + 1)], imag[:, 128 * b : 128 * (b + 1)]) for b in range(4)
    ]
    values = dip_transform(values, table_ref[128:256, :], 1)
    values = [turn(*values[b], *inner[b], 1) for b in range(4)]
    values = radix_four(values, 1)
    real = jnp.concatenate([pair[0] for pair in values], axis=1)
    imag = jnp.concatenate([pair[1] for pair in values], axis=1)
    groups = []
    for m in range(6):
        groups += [real[8 * m : 8 * m + 8], imag[8 * m : 8 * m + 8]]
    early = lane_of((8, NF)) % 32 < 16
    edges = []
    for c in range(3):
        for ri in range(2):
            before = roll(roll(groups[4 * c + 2 + ri], 4, 0), 1, 1)
            after = roll(groups[4 * c + ri], -1, 1)
            edges.append(jnp.where(early, before, after))
    for ri in range(2):
        groups.append(jnp.where(top, edges[ri], roll(edges[2 + ri], 4, 0)))
    for ri in range(2):
        groups.append(jnp.where(top, edges[4 + ri], 0.0))
    out_ref[...] = jnp.concatenate(groups, axis=0).T


def mode_groups(tiles, rows_ref):
    for a in range(4):
        rows_ref[:, a, :] = tiles[a]
        rows_ref[:, 4 + a, :] = tiles[a]
    block = lane_of((8, 128)) // 32
    top = row_of((8, 128)) < 4
    columns = []
    for t in range(4):
        parts = [rows_ref[4 * n + t] for n in range(4)]
        for step in (1, 2):
            upper = (block // step) % 2 == 1
            for n in range(4):
                if (n // step) % 2 == 0:
                    low, high = parts[n], parts[n + step]
                    parts[n] = jnp.where(upper, roll(high, 32 * step, 1), low)
                    parts[n + step] = jnp.where(upper, high, roll(low, -32 * step, 1))
        columns.append([jnp.where(top, parts[n], parts[2 + n]) for n in range(2)])
    return [jnp.concatenate([column[n] for column in columns], axis=1) for n in range(2)]


def past_kernel(
    kernel_hbm, history_hbm, weight_ref, out_ref, rows_ref, kernel_ref, history_ref, arrived
):
    first = pltpu.make_async_copy(kernel_hbm, kernel_ref, arrived.at[0])
    second = pltpu.make_async_copy(history_hbm, history_ref, arrived.at[1])
    first.start()
    second.start()
    first.wait()
    groups = mode_groups([kernel_ref[0, a, 0] for a in range(4)], rows_ref.at[6])
    for parity in range(2):
        weight_ref[parity] = groups[parity]
    second.wait()
    for z in range(2):
        for c in range(3):
            tiles = []
            for a in range(4):
                total = kernel_ref[1, a, 0] * history_ref[0, z, c, a, 0]
                for h in range(1, 6):
                    total = total + kernel_ref[h + 1, a, 0] * history_ref[h, z, c, a, 0]
                tiles.append(total)
            groups = mode_groups(tiles, rows_ref.at[3 * z + c])
            for parity in range(2):
                out_ref[c, parity, z] = groups[parity]


ACROSS, ALONG, DEEP = (0, 3, 4), (3, 1, 5), (4, 5, 2)
STEP = 0.5 * COURANT


def pack_columns(stress_ref, part_ref, side):
    lane = lane_of((64, 128))
    total = jnp.zeros((64, 128), jnp.float32)
    for n in range(3):
        for z in range(4):
            fields = (stress_ref[ALONG[n], z], part_ref[n, z], stress_ref[ACROSS[n], z])
            for i in range(3):
                to = 12 * i + 4 * n + z
                total = jnp.where(lane == to, roll(fields[i], to - side, 1), total)
    return total


def part_kernel(velocity_ref, stress_ref, part_ref, ylo_ref, yhi_ref, xlo_ref, xhi_ref):
    row, lane = row_of((64, 128)), lane_of((64, 128))
    for n in range(3):
        for z in range(4):
            across, along = stress_ref[ACROSS[n], z], stress_ref[ALONG[n], z]
            total = jnp.where(row == 63, 0.0, roll(across, -1, 0))
            total = total - jnp.where(row == 0, 0.0, roll(across, 1, 0))
            total = total + jnp.where(lane == 127, 0.0, roll(along, -1, 1))
            total = total - jnp.where(lane == 0, 0.0, roll(along, 1, 1))
            if z < 3:
                total = total + stress_ref[DEEP[n], z + 1]
            if z > 0:
                total = total - stress_ref[DEEP[n], z - 1]
            part_ref[n, z] = velocity_ref[n, z] + STEP * total
    ylo_ref[...] = pack_columns(stress_ref, part_ref, 0)
    yhi_ref[...] = pack_columns(stress_ref, part_ref, 127)
    pad = jnp.zeros((8, 128), jnp.float32)
    for at, ref in ((0, xlo_ref), (63, xhi_ref)):
        rows = [stress_ref[ACROSS[n], z, at : at + 1, :] for n in range(3) for z in range(4)]
        rows += [part_ref[n, z, at : at + 1, :] for n in range(3) for z in range(4)]
        ref[...] = jnp.concatenate(rows + [pad], axis=0)


def column_kernel(low_ref, high_ref, ylo_ref, yhi_ref, out_low_ref, out_high_ref):
    lane, row = lane_of((32, 128)), row_of((32, 128))
    for at, ref, out_ref in ((0, low_ref, out_low_ref), (63, high_ref, out_high_ref)):
        low = jnp.broadcast_to(ylo_ref[at : at + 1, :], (32, 128))
        high = jnp.broadcast_to(yhi_ref[at : at + 1, :], (32, 128))
        before = jnp.zeros((32, 128), jnp.float32)
        after = jnp.zeros((32, 128), jnp.float32)
        for n in range(12):
            before = jnp.where((row == 12 + n) & (lane == 0), roll(low, -n, 1), before)
            after = jnp.where((row == 12 + n) & (lane == 127), roll(high, 127 - n, 1), after)
        edge = ref[...] + STEP * (after - before)
        edge = jnp.where(row == 24, low, edge)
        out_ref[...] = jnp.where(row == 25, high, edge)


def row_kernel(
    part_ref, xlo_ref, xhi_ref, ylo_ref, yhi_ref,
    own_xlo_ref, own_xhi_ref, own_ylo_ref, own_yhi_ref, after_ref,
    out_ref, vxlo_ref, vxhi_ref, vylo_ref, vyhi_ref,
):
    row, lane = row_of((64, 128)), lane_of((64, 128))
    ylo, yhi = ylo_ref[...], yhi_ref[...]
    for n in range(3):
        for z in range(4):
            at = 4 * n + z
            field = part_ref[n, z]
            field = field - jnp.where(row == 0, STEP * xlo_ref[at : at + 1, :], 0.0)
            field = field + jnp.where(row == 63, STEP * xhi_ref[at : at + 1, :], 0.0)
            field = field - jnp.where(lane == 0, STEP * roll(ylo, -at, 1), 0.0)
            field = field + jnp.where(lane == 127, STEP * roll(yhi, 127 - at, 1), 0.0)
            out_ref[n, z] = field
    vxlo_ref[...] = xlo_ref[12:28, :] + STEP * own_xlo_ref[0:16, :]
    vxhi_ref[...] = xhi_ref[12:28, :] - STEP * own_xhi_ref[0:16, :]
    for side, ref in enumerate((vylo_ref, vyhi_ref)):
        corner = jnp.where(row == 63, STEP * xhi_ref[24 + side : 25 + side, :], 0.0)
        corner = corner - jnp.where(row == 0, STEP * xlo_ref[24 + side : 25 + side, :], 0.0)
        if side == 0:
            columns = roll(ylo, -12, 1) + STEP * own_ylo_ref[...]
        else:
            columns = roll(yhi, -12, 1) - STEP * own_yhi_ref[...]
        ref[...] = columns + roll(corner, -24, 1)


def strike_diff(field, low, high):
    row = row_of(field.shape)
    before = jnp.where(row == 0, low, roll(field, 1, 0))
    after = jnp.where(row == 63, high, roll(field, -1, 0))
    return 0.5 * (after - before)


def dip_diff(field, low, high, to):
    lane = lane_of(field.shape)
    before = jnp.where(lane == 0, roll(low, -to, 1), roll(field, 1, 1))
    after = jnp.where(lane == 127, roll(high, 127 - to, 1), roll(field, -1, 1))
    return 0.5 * (after - before)


def slab_kernel(
    in_ref, before_ref, stress_ref, cohesion_ref, iv_ref,
    xlo_ref, xhi_ref, ylo_ref, yhi_ref,
    velocity_ref, out_ref, flipped_ref, edge_ref,
):
    last = in_ref[:, 7, :]
    xlo, xhi = [], []
    half = lane_of((32, 128)) < 64
    edge_ref[...] = jnp.zeros((128, 128), jnp.float32)
    for c in range(3):
        for s in range(2):
            for h in range(2):
                to = pl.ds(2 * s + h, 32, stride=4)
                piece = in_ref[:, 2 * c + s, :]
                piece = roll(piece, 64, 1) if h else piece
                shifted = roll(last, -2 * (4 * c + 2 * s + h), 1)
                flipped_ref[to, :] = jnp.where(half, piece, shifted)
        m, h = 6 + c // 2, c % 2
        edge_ref[4 * c : 4 * c + 1, 0:64] = in_ref[0, m : m + 1, NQ * h : NQ * (h + 1)]
        edge_ref[12 + 4 * c : 13 + 4 * c, 0:64] = in_ref[31, m : m + 1, NQ * h : NQ * (h + 1)]
        traction = flipped_ref[...].T
        velocity_ref[c, 0] = before_ref[c, 0] - 0.5 * COURANT * traction[:64]
        xlo.append(traction[64:65])
        xhi.append(traction[65:66])
        for z in range(1, 4):
            velocity_ref[c, z] = before_ref[c, z]
    edges = edge_ref[...].T[:64]
    lane = lane_of((64, 128))
    ylo = ylo_ref[...] - 0.5 * COURANT * jnp.where(lane < 12, edges, 0.0)
    yhi = yhi_ref[...] - 0.5 * COURANT * jnp.where(lane < 12, roll(edges, -12, 1), 0.0)
    for z in range(4):
        dx, dy, dz = [], [], []
        for c in range(3):
            field = velocity_ref[c, z]
            at = 4 * c + z
            low, high = xlo_ref[at : at + 1], xhi_ref[at : at + 1]
            if z == 0:
                low = low - 0.5 * COURANT * xlo[c]
                high = high - 0.5 * COURANT * xhi[c]
            dx.append(strike_diff(field, low, high))
            dy.append(dip_diff(field, ylo, yhi, at))
            under = iv_ref[c] if z == 0 else velocity_ref[c, z - 1]
            if z < 3:
                dz.append(0.5 * (velocity_ref[c, z + 1] - under))
            else:
                dz.append(-0.5 * under)
        dilation = dx[0] + dy[1] + dz[2]
        rates = [
            dilation + 2.0 * dx[0],
            dilation + 2.0 * dy[1],
            dilation + 2.0 * dz[2],
            dy[0] + dx[1],
            dz[0] + dx[2],
            dz[1] + dy[2],
        ]
        trial = [stress_ref[n, z] + COURANT * rates[n] for n in range(6)]
        pressure = (trial[0] + trial[1] + trial[2]) * (1.0 / 3.0)
        normal = [trial[n] - pressure for n in range(3)]
        second = 0.5 * (
            normal[0] * normal[0] + normal[1] * normal[1] + normal[2] * normal[2]
        ) + (trial[3] * trial[3] + trial[4] * trial[4] + trial[5] * trial[5])
        shear = jnp.sqrt(second)
        limit = cohesion_ref[z] + FRICTION * jnp.maximum(-pressure, 0.0)
        factor = limit / jnp.maximum(shear, limit)
        for n in range(3):
            out_ref[n, z] = pressure + factor * normal[n]
            out_ref[3 + n, z] = factor * trial[3 + n]


def f32(*shape):
    return jax.ShapeDtypeStruct(shape, jnp.float32)


def call(kernel, out_shape, arguments, after=(), scratch=()):
    many = isinstance(out_shape, tuple)
    return pl.pallas_call(
        kernel,
        out_shape=out_shape,
        in_specs=[VMEM] * len(arguments) + [pl.BlockSpec(memory_space=pl.ANY)] * len(after),
        out_specs=(VMEM,) * len(out_shape) if many else VMEM,
        scratch_shapes=list(scratch),
        compiler_params=PARAMS,
    )(*arguments, *after)


def scatter(iv):
    scratch = [pltpu.VMEM((128, 64), jnp.float32)]
    return call(scatter_kernel, f32(32, 8, 128), (iv,), scratch=scratch)


def strike_forward(arrived, after):
    arguments = (arrived, strike_tables(False))
    return call(strike_forward_kernel, f32(512, 128), arguments, after)


def strike_inverse(arrived):
    return call(strike_inverse_kernel, f32(32, 8, 128), (arrived, strike_tables(True)))


def dip(arrived, weight, past, after):
    return call(dip_kernel, f32(512, 128), (arrived, weight, past, dip_tables()), after)


def past_terms(kernel, history):
    return call(
        past_kernel,
        (f32(2, 8, NF), f32(3, 2, 2, 8, NF)),
        (),
        (kernel, history),
        [
            pltpu.VMEM((7, 16, 8, 128), jnp.float32),
            pltpu.VMEM(kernel.shape, jnp.float32),
            pltpu.VMEM(history.shape, jnp.float32),
            pltpu.SemaphoreType.DMA((2,)),
        ],
    )


def velocity_part(velocity, stress):
    columns, rows = (f32(64, 128),) * 2, (f32(32, 128),) * 2
    return call(part_kernel, (f32(3, 4, 64, 128), *columns, *rows), (velocity, stress))


def velocity_columns(edges, halo):
    return call(column_kernel, (f32(32, 128),) * 2, (*edges, *halo))


def velocity_rows(part, halo, own, after):
    return call(
        row_kernel,
        (f32(3, 4, 64, 128), f32(16, 128), f32(16, 128), f32(64, 128), f32(64, 128)),
        (part, *halo, *own),
        (after,),
    )


def slab(arrived, before, stress, cohesion, iv, halo):
    return call(
        slab_kernel,
        (f32(3, 4, 64, 128), f32(6, 4, 64, 128)),
        (arrived, before, stress, cohesion, iv, *halo),
        scratch=[pltpu.VMEM((128, 128), jnp.float32), pltpu.VMEM((128, 128), jnp.float32)],
    )


def exchange(axis, low, high):
    count = lax.axis_size(axis)
    return (
        lax.ppermute(high, axis, [(i, (i + 1) % count) for i in range(count)]),
        lax.ppermute(low, axis, [(i, (i - 1) % count) for i in range(count)]),
    )


def strike_swap(value):
    return lax.all_to_all(value, "bx", split_axis=0, concat_axis=0, tiled=True)


def whole_swap(value):
    value = value.reshape(512, 1, 128)
    value = lax.all_to_all(value, ("by", "bx"), split_axis=0, concat_axis=0, tiled=True)
    return value.reshape(512, 128)


def local(interface_velocity, history, kernel, velocity, stress, cohesion):
    arrived = strike_swap(scatter(interface_velocity))
    part, *edges = velocity_part(velocity, stress)
    own_columns, own_rows = edges[:2], edges[2:]
    columns = exchange("by", *own_columns)
    sent = strike_forward(arrived, columns)
    rows = exchange("bx", *velocity_columns(own_rows, columns))
    arrived = whole_swap(sent)
    weight, past = past_terms(kernel, history)
    sent = dip(arrived, weight, past, rows)
    before, *halo = velocity_rows(part, (*rows, *columns), (*own_rows, *own_columns), sent)
    arrived = whole_swap(sent)
    arrived = strike_swap(strike_inverse(arrived))
    return slab(arrived, before, stress, cohesion, interface_velocity, halo)


def solution(mesh):
    return jax.shard_map(
        local,
        mesh=mesh,
        in_specs=(
            P(None, "bx", "by"),
            P(None, None, None, "by", "bx", None, None),
            P(None, "by", "bx", None, None),
            P(None, None, "bx", "by"),
            P(None, None, "bx", "by"),
            P(None, "bx", "by"),
        ),
        out_specs=(P(None, None, "bx", "by"), P(None, None, "bx", "by")),
        check_vma=False,
    )
```

```python
import jax
import jax.numpy as jnp
import numpy as np
from jax import lax
from jax.experimental import pallas as pl
from jax.experimental.pallas import tpu as pltpu
from jax.sharding import PartitionSpec as P

COURANT = 0.3
FRICTION = 0.6
NP_, NQ = 32, 64
NJ = 16
NF = 512
SCALE = 1.0 / 2048.0
VMEM = pl.BlockSpec(memory_space=pltpu.VMEM)
LONG = pl.CostEstimate(flops=30_000_000_000, bytes_accessed=20_000_000, transcendentals=0)
PARAMS = pltpu.CompilerParams(vmem_limit_bytes=16 * 1024 * 1024)


def angles(rows, cols, length):
    return 2.0 * np.pi / length * ((rows[:, None] * cols[None, :]) % length)


def stack(*tables):
    wide = [np.pad(table, ((0, 0), (0, 256 - table.shape[1]))) for table in tables]
    return np.concatenate(wide, axis=0).astype(np.float32)


def cell_table():
    theta = angles(np.arange(64), np.arange(64), 64).reshape(64, 16, 4)
    cos, sin = np.cos(theta) * SCALE, np.sin(theta) * SCALE
    table = np.zeros((2, 2, 64, 16, 2, 2, 4))
    for h in range(2):
        table[0, h, :, :, 0, h] = cos
        table[1, h, :, :, 0, h] = sin
        table[0, h, :, :, 1, h] = -sin
        table[1, h, :, :, 1, h] = cos
    return table.reshape(256, 256)


def strike_tables(inverse):
    theta = angles(np.arange(32), np.arange(32), 32)
    cos, sin = np.cos(theta), np.sin(theta)
    twiddle = angles(np.arange(32), np.arange(128) % 64, 2048)
    twiddle = np.concatenate([np.cos(twiddle), np.sin(twiddle)], axis=1)
    if inverse:
        return stack(cell_table().T, twiddle, np.concatenate([cos, -sin], axis=1))
    return stack(cell_table(), twiddle, np.concatenate([cos, -sin], axis=0))


def dip_order():
    lane = np.arange(128)
    return 4 * (lane % 32) + lane // 32


def dip_tables():
    theta = angles(np.arange(128), dip_order(), 128)
    forward = np.concatenate([np.cos(theta), np.sin(theta)], axis=1)
    inverse = np.concatenate([np.cos(theta).T, np.sin(theta).T], axis=1)
    theta = angles(np.arange(8), np.arange(128), 512)
    inner = np.concatenate([np.cos(theta), np.sin(theta)], axis=1)
    outer = []
    for b in range(4):
        for s in range(2):
            theta = angles(2 * s + np.arange(8) // 4, 4 * dip_order() + b, 2048)
            outer.append(np.concatenate([np.cos(theta), np.sin(theta)], axis=1))
    return stack(forward, inverse, inner, *outer)


def halves(value):
    high = value.astype(jnp.bfloat16)
    low = (value - high.astype(jnp.float32)).astype(jnp.bfloat16)
    return high, low


def dot(a, b):
    return jnp.dot(a, b, preferred_element_type=jnp.float32)


def stacked_dot(table, value):
    high, low = halves(value)
    table_high, table_low = halves(table)
    table = jnp.concatenate([table_high, table_high, table_low], axis=1)
    return dot(table, jnp.concatenate([high, low, high], axis=0))


def rows_dot(value, table):
    rows = value.shape[0]
    high, low = halves(value)
    table_high, table_low = halves(table)
    both = dot(jnp.concatenate([high, low], axis=0), table_high)
    return both[:rows] + both[rows:] + dot(high, table_low)


def radix_four(values, sign):
    (r0, i0), (r1, i1), (r2, i2), (r3, i3) = values
    ar, ai, br, bi = r0 + r2, i0 + i2, r0 - r2, i0 - i2
    cr, ci, dr, di = r1 + r3, i1 + i3, sign * (r1 - r3), sign * (i1 - i3)
    return [
        (ar + cr, ai + ci),
        (br - di, bi + dr),
        (ar - cr, ai - ci),
        (br + di, bi - dr),
    ]


def turn(real, imag, cos, sin, sign):
    if sign > 0:
        return real * cos - imag * sin, imag * cos + real * sin
    return real * cos + imag * sin, imag * cos - real * sin


def dip_transform(values, table, sign):
    stacked = jnp.concatenate([part for pair in values for part in pair], axis=0)
    product = rows_dot(stacked, table)
    out = []
    for n in range(4):
        real, imag = product[96 * n : 96 * n + 48], product[96 * n + 48 : 96 * (n + 1)]
        out.append(
            (
                real[:, :128] - sign * imag[:, 128:],
                imag[:, :128] + sign * real[:, 128:],
            )
        )
    return out


def roll(value, shift, axis):
    return pltpu.roll(value, shift % value.shape[axis], axis)


def lane_of(shape):
    return lax.broadcasted_iota(jnp.int32, shape, len(shape) - 1)


def row_of(shape):
    return lax.broadcasted_iota(jnp.int32, shape, len(shape) - 2)


def block_transpose(parts):
    parts = list(parts)
    block = lane_of(parts[0].shape) // 16
    for step in (1, 2, 4):
        upper = (block // step) % 2 == 1
        for t in range(8):
            if (t // step) % 2 == 0:
                low, high = parts[t], parts[t + step]
                parts[t] = jnp.where(upper, roll(high, 16 * step, 1), low)
                parts[t + step] = jnp.where(upper, high, roll(low, -16 * step, 1))
    return parts


def scatter_kernel(iv_ref, out_ref, flipped_ref):
    for c in range(3):
        flipped_ref[...] = iv_ref[c].T
        for s in range(2):
            for h in range(2):
                out_ref[:, 2 * c + s, NQ * h : NQ * (h + 1)] = flipped_ref[
                    pl.ds(2 * s + h, 32, stride=4), :
                ]
    zero = jnp.zeros((32, 128), jnp.float32)
    out_ref[:, 6, :] = zero
    out_ref[:, 7, :] = zero


def strike_forward_kernel(in_ref, table_ref, after_ref, also_ref, out_ref):
    value = jnp.concatenate([in_ref[:, m, :] for m in range(6)], axis=1)
    value = stacked_dot(table_ref[288:352, 0:32], value)
    cos, sin = table_ref[256:288, 0:128], table_ref[256:288, 128:256]
    rows = []
    for m in range(6):
        real = value[:32, 128 * m : 128 * (m + 1)]
        imag = value[32:, 128 * m : 128 * (m + 1)]
        rows.append(
            jnp.concatenate([real * cos + imag * sin, imag * cos - real * sin], axis=1)
        )
    value = rows_dot(jnp.concatenate(rows, axis=0), table_ref[0:256, :])
    zero = jnp.zeros((32, 128), jnp.float32)
    for t in range(2):
        parts = [value[32 * m : 32 * (m + 1), 128 * t : 128 * (t + 1)] for m in range(6)]
        parts = block_transpose(parts + [zero, zero])
        for b in range(8):
            out_ref[32 * (8 * t + b) : 32 * (8 * t + b + 1), :] = parts[b]


def strike_inverse_kernel(in_ref, table_ref, out_ref):
    columns = []
    for t in range(2):
        columns.append(
            block_transpose([in_ref[32 * (8 * t + b) : 32 * (8 * t + b + 1), :] for b in range(8)])
        )
    rows = [jnp.concatenate([columns[0][m], columns[1][m]], axis=1) for m in range(8)]
    value = rows_dot(jnp.concatenate(rows, axis=0), table_ref[0:256, :])
    cos, sin = table_ref[256:288, 0:128], table_ref[256:288, 128:256]
    reals, imags = [], []
    for m in range(8):
        real = value[32 * m : 32 * (m + 1), :128]
        imag = value[32 * m : 32 * (m + 1), 128:]
        reals.append(real * cos - imag * sin)
        imags.append(imag * cos + real * sin)
    value = jnp.concatenate(
        [jnp.concatenate(reals, axis=1), jnp.concatenate(imags, axis=1)], axis=0
    )
    value = stacked_dot(table_ref[288:320, 0:64], value)
    parts = [value[:, 128 * m : 128 * (m + 1)] for m in range(8)]
    lane = lane_of((32, 128))
    last = parts[7]
    for m in range(6):
        before = roll(parts[m], 1, 0)
        after = roll(parts[m], -1, 0)
        for h in range(2):
            to = 64 + 2 * (2 * m + h)
            last = jnp.where(lane == to, roll(before, to - (NQ * h + 63), 1), last)
            last = jnp.where(lane == to + 1, roll(after, to + 1 - NQ * h, 1), last)
    parts[7] = last
    for m in range(8):
        out_ref[:, m, :] = parts[m]


def dip_kernel(in_ref, weight_ref, past_ref, table_ref, after_ref, also_ref, out_ref):
    flipped = in_ref[...].T
    values = []
    for v in range(4):
        lanes = slice(128 * v, 128 * (v + 1))
        values.append(
            [
                jnp.concatenate(
                    [flipped[16 * m + 8 * ri : 16 * m + 8 * ri + 8, lanes] for m in range(6)],
                    axis=0,
                )
                for ri in range(2)
            ]
        )
    inner = [
        (table_ref[256 + b : 257 + b, 0:128], table_ref[256 + b : 257 + b, 128:256])
        for b in range(4)
    ]
    outer = []
    for s in range(2):
        at = [264 + 16 * b + 8 * s for b in range(4)]
        cos = jnp.concatenate([table_ref[n : n + 8, 0:128] for n in at], axis=1)
        outer.append((cos, jnp.concatenate([table_ref[n : n + 8, 128:256] for n in at], axis=1)))
    values = radix_four(values, -1)
    values = [turn(*values[b], *inner[b], -1) for b in range(4)]
    values = dip_transform(values, table_ref[0:128, :], -1)
    real = jnp.concatenate([pair[0] for pair in values], axis=1)
    imag = jnp.concatenate([pair[1] for pair in values], axis=1)
    top = row_of((8, NF)) < 4
    sign = jnp.where(top, 1.0, -1.0).astype(jnp.float32)
    reals, imags = [], []
    for c in range(3):
        turned = []
        for s in range(2):
            rows = slice(16 * c + 8 * s, 16 * c + 8 * s + 8)
            turned.append(turn(real[rows], imag[rows], *outer[s], -1))
        even = [turned[0][ri] + turned[1][ri] for ri in range(2)]
        odd = [turned[0][ri] - turned[1][ri] for ri in range(2)]
        odd = [jnp.where(top, odd[0], odd[1]), jnp.where(top, odd[1], -odd[0])]
        response = []
        for parity, value in enumerate((even, odd)):
            spectrum = [roll(part, 4, 0) + sign * part for part in value]
            response.append(
                [
                    weight_ref[parity] * spectrum[ri] + past_ref[c, parity, ri]
                    for ri in range(2)
                ]
            )
        response = [[roll(part, 4, 0) + sign * part for part in pair] for pair in response]
        even = response[0]
        odd = [
            jnp.where(top, response[1][0], -response[1][1]),
            jnp.where(top, response[1][1], response[1][0]),
        ]
        for s in range(2):
            pair = [even[ri] + odd[ri] if s == 0 else even[ri] - odd[ri] for ri in range(2)]
            pair = turn(*pair, *outer[s], 1)
            reals.append(pair[0])
            imags.append(pair[1])
    real, imag = jnp.concatenate(reals, axis=0), jnp.concatenate(imags, axis=0)
    values = [
        (real[:, 128 * b : 128 * (b + 1)], imag[:, 128 * b : 128 * (b + 1)]) for b in range(4)
    ]
    values = dip_transform(values, table_ref[128:256, :], 1)
    values = [turn(*values[b], *inner[b], 1) for b in range(4)]
    values = radix_four(values, 1)
    real = jnp.concatenate([pair[0] for pair in values], axis=1)
    imag = jnp.concatenate([pair[1] for pair in values], axis=1)
    groups = []
    for m in range(6):
        groups += [real[8 * m : 8 * m + 8], imag[8 * m : 8 * m + 8]]
    early = lane_of((8, NF)) % 32 < 16
    edges = []
    for c in range(3):
        for ri in range(2):
            before = roll(roll(groups[4 * c + 2 + ri], 4, 0), 1, 1)
            after = roll(groups[4 * c + ri], -1, 1)
            edges.append(jnp.where(early, before, after))
    for ri in range(2):
        groups.append(jnp.where(top, edges[ri], roll(edges[2 + ri], 4, 0)))
    for ri in range(2):
        groups.append(jnp.where(top, edges[4 + ri], 0.0))
    out_ref[...] = jnp.concatenate(groups, axis=0).T


def mode_groups(tiles, rows_ref):
    for a in range(4):
        rows_ref[:, a, :] = tiles[a]
        rows_ref[:, 4 + a, :] = tiles[a]
    block = lane_of((8, 128)) // 32
    top = row_of((8, 128)) < 4
    columns = []
    for t in range(4):
        parts = [rows_ref[4 * n + t] for n in range(4)]
        for step in (1, 2):
            upper = (block // step) % 2 == 1
            for n in range(4):
                if (n // step) % 2 == 0:
                    low, high = parts[n], parts[n + step]
                    parts[n] = jnp.where(upper, roll(high, 32 * step, 1), low)
                    parts[n + step] = jnp.where(upper, high, roll(low, -32 * step, 1))
        columns.append([jnp.where(top, parts[n], parts[2 + n]) for n in range(2)])
    return [jnp.concatenate([column[n] for column in columns], axis=1) for n in range(2)]


def past_kernel(
    kernel_hbm, history_hbm, weight_ref, out_ref, rows_ref, kernel_ref, history_ref, arrived
):
    first = pltpu.make_async_copy(kernel_hbm, kernel_ref, arrived.at[0])
    second = pltpu.make_async_copy(history_hbm, history_ref, arrived.at[1])
    first.start()
    second.start()
    first.wait()
    groups = mode_groups([kernel_ref[0, a, 0] for a in range(4)], rows_ref.at[6])
    for parity in range(2):
        weight_ref[parity] = groups[parity]
    second.wait()
    for z in range(2):
        for c in range(3):
            tiles = []
            for a in range(4):
                total = kernel_ref[1, a, 0] * history_ref[0, z, c, a, 0]
                for h in range(1, 6):
                    total = total + kernel_ref[h + 1, a, 0] * history_ref[h, z, c, a, 0]
                tiles.append(total)
            groups = mode_groups(tiles, rows_ref.at[3 * z + c])
            for parity in range(2):
                out_ref[c, parity, z] = groups[parity]


ACROSS, ALONG, DEEP = (0, 3, 4), (3, 1, 5), (4, 5, 2)
STEP = 0.5 * COURANT


def pack_columns(stress_ref, part_ref, side):
    lane = lane_of((64, 128))
    total = jnp.zeros((64, 128), jnp.float32)
    for n in range(3):
        for z in range(4):
            fields = (stress_ref[ALONG[n], z], part_ref[n, z], stress_ref[ACROSS[n], z])
            for i in range(3):
                to = 12 * i + 4 * n + z
                total = jnp.where(lane == to, roll(fields[i], to - side, 1), total)
    return total


def part_kernel(velocity_ref, stress_ref, part_ref, ylo_ref, yhi_ref, xlo_ref, xhi_ref):
    row, lane = row_of((64, 128)), lane_of((64, 128))
    for n in range(3):
        for z in range(4):
            across, along = stress_ref[ACROSS[n], z], stress_ref[ALONG[n], z]
            total = jnp.where(row == 63, 0.0, roll(across, -1, 0))
            total = total - jnp.where(row == 0, 0.0, roll(across, 1, 0))
            total = total + jnp.where(lane == 127, 0.0, roll(along, -1, 1))
            total = total - jnp.where(lane == 0, 0.0, roll(along, 1, 1))
            if z < 3:
                total = total + stress_ref[DEEP[n], z + 1]
            if z > 0:
                total = total - stress_ref[DEEP[n], z - 1]
            part_ref[n, z] = velocity_ref[n, z] + STEP * total
    ylo_ref[...] = pack_columns(stress_ref, part_ref, 0)
    yhi_ref[...] = pack_columns(stress_ref, part_ref, 127)
    pad = jnp.zeros((8, 128), jnp.float32)
    for at, ref in ((0, xlo_ref), (63, xhi_ref)):
        rows = [stress_ref[ACROSS[n], z, at : at + 1, :] for n in range(3) for z in range(4)]
        rows += [part_ref[n, z, at : at + 1, :] for n in range(3) for z in range(4)]
        ref[...] = jnp.concatenate(rows + [pad], axis=0)


def column_kernel(low_ref, high_ref, ylo_ref, yhi_ref, out_low_ref, out_high_ref):
    lane, row = lane_of((32, 128)), row_of((32, 128))
    for at, ref, out_ref in ((0, low_ref, out_low_ref), (63, high_ref, out_high_ref)):
        low = jnp.broadcast_to(ylo_ref[at : at + 1, :], (32, 128))
        high = jnp.broadcast_to(yhi_ref[at : at + 1, :], (32, 128))
        before = jnp.zeros((32, 128), jnp.float32)
        after = jnp.zeros((32, 128), jnp.float32)
        for n in range(12):
            before = jnp.where((row == 12 + n) & (lane == 0), roll(low, -n, 1), before)
            after = jnp.where((row == 12 + n) & (lane == 127), roll(high, 127 - n, 1), after)
        edge = ref[...] + STEP * (after - before)
        edge = jnp.where(row == 24, low, edge)
        out_ref[...] = jnp.where(row == 25, high, edge)


def row_kernel(
    part_ref, xlo_ref, xhi_ref, ylo_ref, yhi_ref,
    own_xlo_ref, own_xhi_ref, own_ylo_ref, own_yhi_ref,
    out_ref, vxlo_ref, vxhi_ref, vylo_ref, vyhi_ref,
):
    row, lane = row_of((64, 128)), lane_of((64, 128))
    ylo, yhi = ylo_ref[...], yhi_ref[...]
    for n in range(3):
        for z in range(4):
            at = 4 * n + z
            field = part_ref[n, z]
            field = field - jnp.where(row == 0, STEP * xlo_ref[at : at + 1, :], 0.0)
            field = field + jnp.where(row == 63, STEP * xhi_ref[at : at + 1, :], 0.0)
            field = field - jnp.where(lane == 0, STEP * roll(ylo, -at, 1), 0.0)
            field = field + jnp.where(lane == 127, STEP * roll(yhi, 127 - at, 1), 0.0)
            out_ref[n, z] = field
    vxlo_ref[...] = xlo_ref[12:28, :] + STEP * own_xlo_ref[0:16, :]
    vxhi_ref[...] = xhi_ref[12:28, :] - STEP * own_xhi_ref[0:16, :]
    for side, ref in enumerate((vylo_ref, vyhi_ref)):
        corner = jnp.where(row == 63, STEP * xhi_ref[24 + side : 25 + side, :], 0.0)
        corner = corner - jnp.where(row == 0, STEP * xlo_ref[24 + side : 25 + side, :], 0.0)
        if side == 0:
            columns = roll(ylo, -12, 1) + STEP * own_ylo_ref[...]
        else:
            columns = roll(yhi, -12, 1) - STEP * own_yhi_ref[...]
        ref[...] = columns + roll(corner, -24, 1)


def strike_diff(field, low, high):
    row = row_of(field.shape)
    before = jnp.where(row == 0, low, roll(field, 1, 0))
    after = jnp.where(row == 63, high, roll(field, -1, 0))
    return 0.5 * (after - before)


def dip_diff(field, low, high, to):
    lane = lane_of(field.shape)
    before = jnp.where(lane == 0, roll(low, -to, 1), roll(field, 1, 1))
    after = jnp.where(lane == 127, roll(high, 127 - to, 1), roll(field, -1, 1))
    return 0.5 * (after - before)


def slab_kernel(
    in_ref, before_ref, stress_ref, cohesion_ref, iv_ref,
    xlo_ref, xhi_ref, ylo_ref, yhi_ref,
    velocity_ref, out_ref, flipped_ref, edge_ref,
):
    last = in_ref[:, 7, :]
    xlo, xhi = [], []
    half = lane_of((32, 128)) < 64
    edge_ref[...] = jnp.zeros((128, 128), jnp.float32)
    for c in range(3):
        for s in range(2):
            for h in range(2):
                to = pl.ds(2 * s + h, 32, stride=4)
                piece = in_ref[:, 2 * c + s, :]
                piece = roll(piece, 64, 1) if h else piece
                shifted = roll(last, -2 * (4 * c + 2 * s + h), 1)
                flipped_ref[to, :] = jnp.where(half, piece, shifted)
        m, h = 6 + c // 2, c % 2
        edge_ref[4 * c : 4 * c + 1, 0:64] = in_ref[0, m : m + 1, NQ * h : NQ * (h + 1)]
        edge_ref[12 + 4 * c : 13 + 4 * c, 0:64] = in_ref[31, m : m + 1, NQ * h : NQ * (h + 1)]
        traction = flipped_ref[...].T
        velocity_ref[c, 0] = before_ref[c, 0] - 0.5 * COURANT * traction[:64]
        xlo.append(traction[64:65])
        xhi.append(traction[65:66])
        for z in range(1, 4):
            velocity_ref[c, z] = before_ref[c, z]
    edges = edge_ref[...].T[:64]
    lane = lane_of((64, 128))
    ylo = ylo_ref[...] - 0.5 * COURANT * jnp.where(lane < 12, edges, 0.0)
    yhi = yhi_ref[...] - 0.5 * COURANT * jnp.where(lane < 12, roll(edges, -12, 1), 0.0)
    for z in range(4):
        dx, dy, dz = [], [], []
        for c in range(3):
            field = velocity_ref[c, z]
            at = 4 * c + z
            low, high = xlo_ref[at : at + 1], xhi_ref[at : at + 1]
            if z == 0:
                low = low - 0.5 * COURANT * xlo[c]
                high = high - 0.5 * COURANT * xhi[c]
            dx.append(strike_diff(field, low, high))
            dy.append(dip_diff(field, ylo, yhi, at))
            under = iv_ref[c] if z == 0 else velocity_ref[c, z - 1]
            if z < 3:
                dz.append(0.5 * (velocity_ref[c, z + 1] - under))
            else:
                dz.append(-0.5 * under)
        dilation = dx[0] + dy[1] + dz[2]
        rates = [
            dilation + 2.0 * dx[0],
            dilation + 2.0 * dy[1],
            dilation + 2.0 * dz[2],
            dy[0] + dx[1],
            dz[0] + dx[2],
            dz[1] + dy[2],
        ]
        trial = [stress_ref[n, z] + COURANT * rates[n] for n in range(6)]
        pressure = (trial[0] + trial[1] + trial[2]) * (1.0 / 3.0)
        normal = [trial[n] - pressure for n in range(3)]
        second = 0.5 * (
            normal[0] * normal[0] + normal[1] * normal[1] + normal[2] * normal[2]
        ) + (trial[3] * trial[3] + trial[4] * trial[4] + trial[5] * trial[5])
        shear = jnp.sqrt(second)
        limit = cohesion_ref[z] + FRICTION * jnp.maximum(-pressure, 0.0)
        factor = limit / jnp.maximum(shear, limit)
        for n in range(3):
            out_ref[n, z] = pressure + factor * normal[n]
            out_ref[3 + n, z] = factor * trial[3 + n]


def f32(*shape):
    return jax.ShapeDtypeStruct(shape, jnp.float32)


def call(kernel, out_shape, arguments, after=(), scratch=(), cost=None):
    many = isinstance(out_shape, tuple)
    return pl.pallas_call(
        kernel,
        out_shape=out_shape,
        in_specs=[VMEM] * len(arguments) + [pl.BlockSpec(memory_space=pl.ANY)] * len(after),
        out_specs=(VMEM,) * len(out_shape) if many else VMEM,
        scratch_shapes=list(scratch),
        compiler_params=PARAMS,
        cost_estimate=cost,
    )(*arguments, *after)


def scatter(iv):
    scratch = [pltpu.VMEM((128, 64), jnp.float32)]
    return call(scatter_kernel, f32(32, 8, 128), (iv,), scratch=scratch)


def strike_forward(arrived, after):
    arguments = (arrived, strike_tables(False))
    return call(strike_forward_kernel, f32(512, 128), arguments, after)


def strike_inverse(arrived):
    return call(strike_inverse_kernel, f32(32, 8, 128), (arrived, strike_tables(True)))


def dip(arrived, weight, past, after):
    return call(dip_kernel, f32(512, 128), (arrived, weight, past, dip_tables()), after)


def past_terms(kernel, history):
    return call(
        past_kernel,
        (f32(2, 8, NF), f32(3, 2, 2, 8, NF)),
        (),
        (kernel, history),
        [
            pltpu.VMEM((7, 16, 8, 128), jnp.float32),
            pltpu.VMEM(kernel.shape, jnp.float32),
            pltpu.VMEM(history.shape, jnp.float32),
            pltpu.SemaphoreType.DMA((2,)),
        ],
    )


def velocity_part(velocity, stress):
    columns, rows = (f32(64, 128),) * 2, (f32(32, 128),) * 2
    return call(part_kernel, (f32(3, 4, 64, 128), *columns, *rows), (velocity, stress))


def velocity_columns(edges, halo):
    return call(column_kernel, (f32(32, 128),) * 2, (*edges, *halo), cost=LONG)


def velocity_rows(part, halo, own):
    return call(
        row_kernel,
        (f32(3, 4, 64, 128), f32(16, 128), f32(16, 128), f32(64, 128), f32(64, 128)),
        (part, *halo, *own),
        cost=LONG,
    )


def slab(arrived, before, stress, cohesion, iv, halo):
    return call(
        slab_kernel,
        (f32(3, 4, 64, 128), f32(6, 4, 64, 128)),
        (arrived, before, stress, cohesion, iv, *halo),
        scratch=[pltpu.VMEM((128, 128), jnp.float32), pltpu.VMEM((128, 128), jnp.float32)],
    )


def exchange(axis, low, high):
    count = lax.axis_size(axis)
    return (
        lax.ppermute(high, axis, [(i, (i + 1) % count) for i in range(count)]),
        lax.ppermute(low, axis, [(i, (i - 1) % count) for i in range(count)]),
    )


def strike_swap(value):
    return lax.all_to_all(value, "bx", split_axis=0, concat_axis=0, tiled=True)


def whole_swap(value):
    value = value.reshape(512, 1, 128)
    value = lax.all_to_all(value, ("by", "bx"), split_axis=0, concat_axis=0, tiled=True)
    return value.reshape(512, 128)


def local(interface_velocity, history, kernel, velocity, stress, cohesion):
    arrived = strike_swap(scatter(interface_velocity))
    part, *edges = velocity_part(velocity, stress)
    own_columns, own_rows = edges[:2], edges[2:]
    columns = exchange("by", *own_columns)
    edges = velocity_columns(own_rows, columns)
    sent = strike_forward(arrived, edges)
    rows = exchange("bx", *edges)
    before, *halo = velocity_rows(part, (*rows, *columns), (*own_rows, *own_columns))
    arrived = whole_swap(sent)
    weight, past = past_terms(kernel, history)
    sent = dip(arrived, weight, past, halo[:2])
    arrived = whole_swap(sent)
    arrived = strike_swap(strike_inverse(arrived))
    return slab(arrived, before, stress, cohesion, interface_velocity, halo)


def solution(mesh):
    return jax.shard_map(
        local,
        mesh=mesh,
        in_specs=(
            P(None, "bx", "by"),
            P(None, None, None, "by", "bx", None, None),
            P(None, "by", "bx", None, None),
            P(None, None, "bx", "by"),
            P(None, None, "bx", "by"),
            P(None, "bx", "by"),
        ),
        out_specs=(P(None, None, "bx", "by"), P(None, None, "bx", "by")),
        check_vma=False,
    )
```

```python
import jax
import jax.numpy as jnp
import numpy as np
from jax import lax
from jax.experimental import pallas as pl
from jax.experimental.pallas import tpu as pltpu
from jax.sharding import PartitionSpec as P

COURANT = 0.3
FRICTION = 0.6
NP_, NQ = 32, 64
NJ = 16
NF = 512
SCALE = 1.0 / 2048.0
VMEM = pl.BlockSpec(memory_space=pltpu.VMEM)
PARAMS = pltpu.CompilerParams(vmem_limit_bytes=16 * 1024 * 1024)


def angles(rows, cols, length):
    return 2.0 * np.pi / length * ((rows[:, None] * cols[None, :]) % length)


def stack(*tables):
    wide = [np.pad(table, ((0, 0), (0, 256 - table.shape[1]))) for table in tables]
    return np.concatenate(wide, axis=0).astype(np.float32)


def cell_table():
    theta = angles(np.arange(64), np.arange(64), 64).reshape(64, 16, 4)
    cos, sin = np.cos(theta) * SCALE, np.sin(theta) * SCALE
    table = np.zeros((2, 2, 64, 16, 2, 2, 4))
    for h in range(2):
        table[0, h, :, :, 0, h] = cos
        table[1, h, :, :, 0, h] = sin
        table[0, h, :, :, 1, h] = -sin
        table[1, h, :, :, 1, h] = cos
    return table.reshape(256, 256)


def strike_tables(inverse):
    theta = angles(np.arange(32), np.arange(32), 32)
    cos, sin = np.cos(theta), np.sin(theta)
    twiddle = angles(np.arange(32), np.arange(128) % 64, 2048)
    twiddle = np.concatenate([np.cos(twiddle), np.sin(twiddle)], axis=1)
    if inverse:
        return stack(cell_table().T, twiddle, np.concatenate([cos, -sin], axis=1))
    return stack(cell_table(), twiddle, np.concatenate([cos, -sin], axis=0))


def dip_order():
    lane = np.arange(128)
    return 4 * (lane % 32) + lane // 32


def dip_tables():
    theta = angles(np.arange(128), dip_order(), 128)
    forward = np.concatenate([np.cos(theta), np.sin(theta)], axis=1)
    inverse = np.concatenate([np.cos(theta).T, np.sin(theta).T], axis=1)
    theta = angles(np.arange(8), np.arange(128), 512)
    inner = np.concatenate([np.cos(theta), np.sin(theta)], axis=1)
    outer = []
    for b in range(4):
        for s in range(2):
            theta = angles(2 * s + np.arange(8) // 4, 4 * dip_order() + b, 2048)
            outer.append(np.concatenate([np.cos(theta), np.sin(theta)], axis=1))
    return stack(forward, inverse, inner, *outer)


def halves(value):
    high = value.astype(jnp.bfloat16)
    low = (value - high.astype(jnp.float32)).astype(jnp.bfloat16)
    return high, low


def dot(a, b):
    return jnp.dot(a, b, preferred_element_type=jnp.float32)


def stacked_dot(table, value):
    high, low = halves(value)
    table_high, table_low = halves(table)
    table = jnp.concatenate([table_high, table_high, table_low], axis=1)
    return dot(table, jnp.concatenate([high, low, high], axis=0))


def rows_dot(value, table):
    rows = value.shape[0]
    high, low = halves(value)
    table_high, table_low = halves(table)
    both = dot(jnp.concatenate([high, low], axis=0), table_high)
    return both[:rows] + both[rows:] + dot(high, table_low)


def radix_four(values, sign):
    (r0, i0), (r1, i1), (r2, i2), (r3, i3) = values
    ar, ai, br, bi = r0 + r2, i0 + i2, r0 - r2, i0 - i2
    cr, ci, dr, di = r1 + r3, i1 + i3, sign * (r1 - r3), sign * (i1 - i3)
    return [
        (ar + cr, ai + ci),
        (br - di, bi + dr),
        (ar - cr, ai - ci),
        (br + di, bi - dr),
    ]


def turn(real, imag, cos, sin, sign):
    if sign > 0:
        return real * cos - imag * sin, imag * cos + real * sin
    return real * cos + imag * sin, imag * cos - real * sin


def dip_transform(values, table, sign):
    stacked = jnp.concatenate([part for pair in values for part in pair], axis=0)
    product = rows_dot(stacked, table)
    out = []
    for n in range(4):
        real, imag = product[96 * n : 96 * n + 48], product[96 * n + 48 : 96 * (n + 1)]
        out.append(
            (
                real[:, :128] - sign * imag[:, 128:],
                imag[:, :128] + sign * real[:, 128:],
            )
        )
    return out


def roll(value, shift, axis):
    return pltpu.roll(value, shift % value.shape[axis], axis)


def lane_of(shape):
    return lax.broadcasted_iota(jnp.int32, shape, len(shape) - 1)


def row_of(shape):
    return lax.broadcasted_iota(jnp.int32, shape, len(shape) - 2)


def block_transpose(parts):
    parts = list(parts)
    block = lane_of(parts[0].shape) // 16
    for step in (1, 2, 4):
        upper = (block // step) % 2 == 1
        for t in range(8):
            if (t // step) % 2 == 0:
                low, high = parts[t], parts[t + step]
                parts[t] = jnp.where(upper, roll(high, 16 * step, 1), low)
                parts[t + step] = jnp.where(upper, high, roll(low, -16 * step, 1))
    return parts


def scatter_kernel(iv_ref, out_ref, flipped_ref):
    for c in range(3):
        flipped_ref[...] = iv_ref[c].T
        for s in range(2):
            for h in range(2):
                out_ref[:, 2 * c + s, NQ * h : NQ * (h + 1)] = flipped_ref[
                    pl.ds(2 * s + h, 32, stride=4), :
                ]
    zero = jnp.zeros((32, 128), jnp.float32)
    out_ref[:, 6, :] = zero
    out_ref[:, 7, :] = zero


def strike_forward_kernel(in_ref, table_ref, out_ref):
    value = jnp.concatenate([in_ref[:, m, :] for m in range(6)], axis=1)
    value = stacked_dot(table_ref[288:352, 0:32], value)
    cos, sin = table_ref[256:288, 0:128], table_ref[256:288, 128:256]
    rows = []
    for m in range(6):
        real = value[:32, 128 * m : 128 * (m + 1)]
        imag = value[32:, 128 * m : 128 * (m + 1)]
        rows.append(
            jnp.concatenate([real * cos + imag * sin, imag * cos - real * sin], axis=1)
        )
    value = rows_dot(jnp.concatenate(rows, axis=0), table_ref[0:256, :])
    zero = jnp.zeros((32, 128), jnp.float32)
    for t in range(2):
        parts = [value[32 * m : 32 * (m + 1), 128 * t : 128 * (t + 1)] for m in range(6)]
        parts = block_transpose(parts + [zero, zero])
        for b in range(8):
            out_ref[32 * (8 * t + b) : 32 * (8 * t + b + 1), :] = parts[b]


def strike_inverse_kernel(in_ref, table_ref, after_ref, also_ref, out_ref):
    columns = []
    for t in range(2):
        columns.append(
            block_transpose([in_ref[32 * (8 * t + b) : 32 * (8 * t + b + 1), :] for b in range(8)])
        )
    rows = [jnp.concatenate([columns[0][m], columns[1][m]], axis=1) for m in range(8)]
    value = rows_dot(jnp.concatenate(rows, axis=0), table_ref[0:256, :])
    cos, sin = table_ref[256:288, 0:128], table_ref[256:288, 128:256]
    reals, imags = [], []
    for m in range(8):
        real = value[32 * m : 32 * (m + 1), :128]
        imag = value[32 * m : 32 * (m + 1), 128:]
        reals.append(real * cos - imag * sin)
        imags.append(imag * cos + real * sin)
    value = jnp.concatenate(
        [jnp.concatenate(reals, axis=1), jnp.concatenate(imags, axis=1)], axis=0
    )
    value = stacked_dot(table_ref[288:320, 0:64], value)
    parts = [value[:, 128 * m : 128 * (m + 1)] for m in range(8)]
    lane = lane_of((32, 128))
    last = parts[7]
    for m in range(6):
        before = roll(parts[m], 1, 0)
        after = roll(parts[m], -1, 0)
        for h in range(2):
            to = 64 + 2 * (2 * m + h)
            last = jnp.where(lane == to, roll(before, to - (NQ * h + 63), 1), last)
            last = jnp.where(lane == to + 1, roll(after, to + 1 - NQ * h, 1), last)
    parts[7] = last
    for m in range(8):
        out_ref[:, m, :] = parts[m]


def dip_kernel(in_ref, weight_ref, past_ref, table_ref, after_ref, also_ref, out_ref):
    flipped = in_ref[...].T
    values = []
    for v in range(4):
        lanes = slice(128 * v, 128 * (v + 1))
        values.append(
            [
                jnp.concatenate(
                    [flipped[16 * m + 8 * ri : 16 * m + 8 * ri + 8, lanes] for m in range(6)],
                    axis=0,
                )
                for ri in range(2)
            ]
        )
    inner = [
        (table_ref[256 + b : 257 + b, 0:128], table_ref[256 + b : 257 + b, 128:256])
        for b in range(4)
    ]
    outer = []
    for s in range(2):
        at = [264 + 16 * b + 8 * s for b in range(4)]
        cos = jnp.concatenate([table_ref[n : n + 8, 0:128] for n in at], axis=1)
        outer.append((cos, jnp.concatenate([table_ref[n : n + 8, 128:256] for n in at], axis=1)))
    values = radix_four(values, -1)
    values = [turn(*values[b], *inner[b], -1) for b in range(4)]
    values = dip_transform(values, table_ref[0:128, :], -1)
    real = jnp.concatenate([pair[0] for pair in values], axis=1)
    imag = jnp.concatenate([pair[1] for pair in values], axis=1)
    top = row_of((8, NF)) < 4
    sign = jnp.where(top, 1.0, -1.0).astype(jnp.float32)
    reals, imags = [], []
    for c in range(3):
        turned = []
        for s in range(2):
            rows = slice(16 * c + 8 * s, 16 * c + 8 * s + 8)
            turned.append(turn(real[rows], imag[rows], *outer[s], -1))
        even = [turned[0][ri] + turned[1][ri] for ri in range(2)]
        odd = [turned[0][ri] - turned[1][ri] for ri in range(2)]
        odd = [jnp.where(top, odd[0], odd[1]), jnp.where(top, odd[1], -odd[0])]
        response = []
        for parity, value in enumerate((even, odd)):
            spectrum = [roll(part, 4, 0) + sign * part for part in value]
            response.append(
                [
                    weight_ref[parity] * spectrum[ri] + past_ref[c, parity, ri]
                    for ri in range(2)
                ]
            )
        response = [[roll(part, 4, 0) + sign * part for part in pair] for pair in response]
        even = response[0]
        odd = [
            jnp.where(top, response[1][0], -response[1][1]),
            jnp.where(top, response[1][1], response[1][0]),
        ]
        for s in range(2):
            pair = [even[ri] + odd[ri] if s == 0 else even[ri] - odd[ri] for ri in range(2)]
            pair = turn(*pair, *outer[s], 1)
            reals.append(pair[0])
            imags.append(pair[1])
    real, imag = jnp.concatenate(reals, axis=0), jnp.concatenate(imags, axis=0)
    values = [
        (real[:, 128 * b : 128 * (b + 1)], imag[:, 128 * b : 128 * (b + 1)]) for b in range(4)
    ]
    values = dip_transform(values, table_ref[128:256, :], 1)
    values = [turn(*values[b], *inner[b], 1) for b in range(4)]
    values = radix_four(values, 1)
    real = jnp.concatenate([pair[0] for pair in values], axis=1)
    imag = jnp.concatenate([pair[1] for pair in values], axis=1)
    groups = []
    for m in range(6):
        groups += [real[8 * m : 8 * m + 8], imag[8 * m : 8 * m + 8]]
    early = lane_of((8, NF)) % 32 < 16
    edges = []
    for c in range(3):
        for ri in range(2):
            before = roll(roll(groups[4 * c + 2 + ri], 4, 0), 1, 1)
            after = roll(groups[4 * c + ri], -1, 1)
            edges.append(jnp.where(early, before, after))
    for ri in range(2):
        groups.append(jnp.where(top, edges[ri], roll(edges[2 + ri], 4, 0)))
    for ri in range(2):
        groups.append(jnp.where(top, edges[4 + ri], 0.0))
    out_ref[...] = jnp.concatenate(groups, axis=0).T


def mode_groups(tiles, rows_ref):
    for a in range(4):
        rows_ref[:, a, :] = tiles[a]
        rows_ref[:, 4 + a, :] = tiles[a]
    block = lane_of((8, 128)) // 32
    top = row_of((8, 128)) < 4
    columns = []
    for t in range(4):
        parts = [rows_ref[4 * n + t] for n in range(4)]
        for step in (1, 2):
            upper = (block // step) % 2 == 1
            for n in range(4):
                if (n // step) % 2 == 0:
                    low, high = parts[n], parts[n + step]
                    parts[n] = jnp.where(upper, roll(high, 32 * step, 1), low)
                    parts[n + step] = jnp.where(upper, high, roll(low, -32 * step, 1))
        columns.append([jnp.where(top, parts[n], parts[2 + n]) for n in range(2)])
    return [jnp.concatenate([column[n] for column in columns], axis=1) for n in range(2)]


def past_kernel(
    kernel_hbm, history_hbm, weight_ref, out_ref, rows_ref, kernel_ref, history_ref, arrived
):
    first = pltpu.make_async_copy(kernel_hbm, kernel_ref, arrived.at[0])
    second = pltpu.make_async_copy(history_hbm, history_ref, arrived.at[1])
    first.start()
    second.start()
    first.wait()
    groups = mode_groups([kernel_ref[0, a, 0] for a in range(4)], rows_ref.at[6])
    for parity in range(2):
        weight_ref[parity] = groups[parity]
    second.wait()
    for z in range(2):
        for c in range(3):
            tiles = []
            for a in range(4):
                total = kernel_ref[1, a, 0] * history_ref[0, z, c, a, 0]
                for h in range(1, 6):
                    total = total + kernel_ref[h + 1, a, 0] * history_ref[h, z, c, a, 0]
                tiles.append(total)
            groups = mode_groups(tiles, rows_ref.at[3 * z + c])
            for parity in range(2):
                out_ref[c, parity, z] = groups[parity]


ACROSS, ALONG, DEEP = (0, 3, 4), (3, 1, 5), (4, 5, 2)
STEP = 0.5 * COURANT


def pack_columns(stress_ref, part_ref, side):
    lane = lane_of((64, 128))
    total = jnp.zeros((64, 128), jnp.float32)
    for n in range(3):
        for z in range(4):
            fields = (stress_ref[ALONG[n], z], part_ref[n, z], stress_ref[ACROSS[n], z])
            for i in range(3):
                to = 12 * i + 4 * n + z
                total = jnp.where(lane == to, roll(fields[i], to - side, 1), total)
    return total


def part_kernel(
    velocity_ref, stress_ref, after_ref, part_ref, ylo_ref, yhi_ref, xlo_ref, xhi_ref
):
    row, lane = row_of((64, 128)), lane_of((64, 128))
    for n in range(3):
        for z in range(4):
            across, along = stress_ref[ACROSS[n], z], stress_ref[ALONG[n], z]
            total = jnp.where(row == 63, 0.0, roll(across, -1, 0))
            total = total - jnp.where(row == 0, 0.0, roll(across, 1, 0))
            total = total + jnp.where(lane == 127, 0.0, roll(along, -1, 1))
            total = total - jnp.where(lane == 0, 0.0, roll(along, 1, 1))
            if z < 3:
                total = total + stress_ref[DEEP[n], z + 1]
            if z > 0:
                total = total - stress_ref[DEEP[n], z - 1]
            part_ref[n, z] = velocity_ref[n, z] + STEP * total
    ylo_ref[...] = pack_columns(stress_ref, part_ref, 0)
    yhi_ref[...] = pack_columns(stress_ref, part_ref, 127)
    pad = jnp.zeros((8, 128), jnp.float32)
    for at, ref in ((0, xlo_ref), (63, xhi_ref)):
        rows = [stress_ref[ACROSS[n], z, at : at + 1, :] for n in range(3) for z in range(4)]
        rows += [part_ref[n, z, at : at + 1, :] for n in range(3) for z in range(4)]
        ref[...] = jnp.concatenate(rows + [pad], axis=0)


def column_kernel(low_ref, high_ref, ylo_ref, yhi_ref, after_ref, out_low_ref, out_high_ref):
    lane, row = lane_of((32, 128)), row_of((32, 128))
    for at, ref, out_ref in ((0, low_ref, out_low_ref), (63, high_ref, out_high_ref)):
        low = jnp.broadcast_to(ylo_ref[at : at + 1, :], (32, 128))
        high = jnp.broadcast_to(yhi_ref[at : at + 1, :], (32, 128))
        before = jnp.zeros((32, 128), jnp.float32)
        after = jnp.zeros((32, 128), jnp.float32)
        for n in range(12):
            before = jnp.where((row == 12 + n) & (lane == 0), roll(low, -n, 1), before)
            after = jnp.where((row == 12 + n) & (lane == 127), roll(high, 127 - n, 1), after)
        edge = ref[...] + STEP * (after - before)
        edge = jnp.where(row == 24, low, edge)
        out_ref[...] = jnp.where(row == 25, high, edge)


def row_kernel(
    part_ref, xlo_ref, xhi_ref, ylo_ref, yhi_ref,
    own_xlo_ref, own_xhi_ref, own_ylo_ref, own_yhi_ref, after_ref,
    out_ref, vxlo_ref, vxhi_ref, vylo_ref, vyhi_ref,
):
    row, lane = row_of((64, 128)), lane_of((64, 128))
    ylo, yhi = ylo_ref[...], yhi_ref[...]
    for n in range(3):
        for z in range(4):
            at = 4 * n + z
            field = part_ref[n, z]
            field = field - jnp.where(row == 0, STEP * xlo_ref[at : at + 1, :], 0.0)
            field = field + jnp.where(row == 63, STEP * xhi_ref[at : at + 1, :], 0.0)
            field = field - jnp.where(lane == 0, STEP * roll(ylo, -at, 1), 0.0)
            field = field + jnp.where(lane == 127, STEP * roll(yhi, 127 - at, 1), 0.0)
            out_ref[n, z] = field
    vxlo_ref[...] = xlo_ref[12:28, :] + STEP * own_xlo_ref[0:16, :]
    vxhi_ref[...] = xhi_ref[12:28, :] - STEP * own_xhi_ref[0:16, :]
    for side, ref in enumerate((vylo_ref, vyhi_ref)):
        corner = jnp.where(row == 63, STEP * xhi_ref[24 + side : 25 + side, :], 0.0)
        corner = corner - jnp.where(row == 0, STEP * xlo_ref[24 + side : 25 + side, :], 0.0)
        if side == 0:
            columns = roll(ylo, -12, 1) + STEP * own_ylo_ref[...]
        else:
            columns = roll(yhi, -12, 1) - STEP * own_yhi_ref[...]
        ref[...] = columns + roll(corner, -24, 1)


def strike_diff(field, low, high):
    row = row_of(field.shape)
    before = jnp.where(row == 0, low, roll(field, 1, 0))
    after = jnp.where(row == 63, high, roll(field, -1, 0))
    return 0.5 * (after - before)


def dip_diff(field, low, high, to):
    lane = lane_of(field.shape)
    before = jnp.where(lane == 0, roll(low, -to, 1), roll(field, 1, 1))
    after = jnp.where(lane == 127, roll(high, 127 - to, 1), roll(field, -1, 1))
    return 0.5 * (after - before)


def slab_kernel(
    in_ref, before_ref, stress_ref, cohesion_ref, iv_ref,
    xlo_ref, xhi_ref, ylo_ref, yhi_ref,
    velocity_ref, out_ref, flipped_ref, edge_ref,
):
    last = in_ref[:, 7, :]
    xlo, xhi = [], []
    half = lane_of((32, 128)) < 64
    edge_ref[...] = jnp.zeros((128, 128), jnp.float32)
    for c in range(3):
        for s in range(2):
            for h in range(2):
                to = pl.ds(2 * s + h, 32, stride=4)
                piece = in_ref[:, 2 * c + s, :]
                piece = roll(piece, 64, 1) if h else piece
                shifted = roll(last, -2 * (4 * c + 2 * s + h), 1)
                flipped_ref[to, :] = jnp.where(half, piece, shifted)
        m, h = 6 + c // 2, c % 2
        edge_ref[4 * c : 4 * c + 1, 0:64] = in_ref[0, m : m + 1, NQ * h : NQ * (h + 1)]
        edge_ref[12 + 4 * c : 13 + 4 * c, 0:64] = in_ref[31, m : m + 1, NQ * h : NQ * (h + 1)]
        traction = flipped_ref[...].T
        velocity_ref[c, 0] = before_ref[c, 0] - 0.5 * COURANT * traction[:64]
        xlo.append(traction[64:65])
        xhi.append(traction[65:66])
        for z in range(1, 4):
            velocity_ref[c, z] = before_ref[c, z]
    edges = edge_ref[...].T[:64]
    lane = lane_of((64, 128))
    ylo = ylo_ref[...] - 0.5 * COURANT * jnp.where(lane < 12, edges, 0.0)
    yhi = yhi_ref[...] - 0.5 * COURANT * jnp.where(lane < 12, roll(edges, -12, 1), 0.0)
    for z in range(4):
        dx, dy, dz = [], [], []
        for c in range(3):
            field = velocity_ref[c, z]
            at = 4 * c + z
            low, high = xlo_ref[at : at + 1], xhi_ref[at : at + 1]
            if z == 0:
                low = low - 0.5 * COURANT * xlo[c]
                high = high - 0.5 * COURANT * xhi[c]
            dx.append(strike_diff(field, low, high))
            dy.append(dip_diff(field, ylo, yhi, at))
            under = iv_ref[c] if z == 0 else velocity_ref[c, z - 1]
            if z < 3:
                dz.append(0.5 * (velocity_ref[c, z + 1] - under))
            else:
                dz.append(-0.5 * under)
        dilation = dx[0] + dy[1] + dz[2]
        rates = [
            dilation + 2.0 * dx[0],
            dilation + 2.0 * dy[1],
            dilation + 2.0 * dz[2],
            dy[0] + dx[1],
            dz[0] + dx[2],
            dz[1] + dy[2],
        ]
        trial = [stress_ref[n, z] + COURANT * rates[n] for n in range(6)]
        pressure = (trial[0] + trial[1] + trial[2]) * (1.0 / 3.0)
        normal = [trial[n] - pressure for n in range(3)]
        second = 0.5 * (
            normal[0] * normal[0] + normal[1] * normal[1] + normal[2] * normal[2]
        ) + (trial[3] * trial[3] + trial[4] * trial[4] + trial[5] * trial[5])
        shear = jnp.sqrt(second)
        limit = cohesion_ref[z] + FRICTION * jnp.maximum(-pressure, 0.0)
        factor = limit / jnp.maximum(shear, limit)
        for n in range(3):
            out_ref[n, z] = pressure + factor * normal[n]
            out_ref[3 + n, z] = factor * trial[3 + n]


def f32(*shape):
    return jax.ShapeDtypeStruct(shape, jnp.float32)


def call(kernel, out_shape, arguments, after=(), scratch=()):
    many = isinstance(out_shape, tuple)
    return pl.pallas_call(
        kernel,
        out_shape=out_shape,
        in_specs=[VMEM] * len(arguments) + [pl.BlockSpec(memory_space=pl.ANY)] * len(after),
        out_specs=(VMEM,) * len(out_shape) if many else VMEM,
        scratch_shapes=list(scratch),
        compiler_params=PARAMS,
    )(*arguments, *after)


def scatter(iv):
    scratch = [pltpu.VMEM((128, 64), jnp.float32)]
    return call(scatter_kernel, f32(32, 8, 128), (iv,), scratch=scratch)


def strike_forward(arrived):
    return call(strike_forward_kernel, f32(512, 128), (arrived, strike_tables(False)))


def strike_inverse(arrived, after):
    arguments = (arrived, strike_tables(True))
    return call(strike_inverse_kernel, f32(32, 8, 128), arguments, after)


def dip(arrived, weight, past, after):
    return call(dip_kernel, f32(512, 128), (arrived, weight, past, dip_tables()), after)


def past_terms(kernel, history):
    return call(
        past_kernel,
        (f32(2, 8, NF), f32(3, 2, 2, 8, NF)),
        (),
        (kernel, history),
        [
            pltpu.VMEM((7, 16, 8, 128), jnp.float32),
            pltpu.VMEM(kernel.shape, jnp.float32),
            pltpu.VMEM(history.shape, jnp.float32),
            pltpu.SemaphoreType.DMA((2,)),
        ],
    )


def velocity_part(velocity, stress, after):
    columns, rows = (f32(64, 128),) * 2, (f32(32, 128),) * 2
    outs = (f32(3, 4, 64, 128), *columns, *rows)
    return call(part_kernel, outs, (velocity, stress), (after,))


def velocity_columns(edges, halo, after):
    return call(column_kernel, (f32(32, 128),) * 2, (*edges, *halo), (after,))


def velocity_rows(part, halo, own, after):
    return call(
        row_kernel,
        (f32(3, 4, 64, 128), f32(16, 128), f32(16, 128), f32(64, 128), f32(64, 128)),
        (part, *halo, *own),
        (after,),
    )


def slab(arrived, before, stress, cohesion, iv, halo):
    return call(
        slab_kernel,
        (f32(3, 4, 64, 128), f32(6, 4, 64, 128)),
        (arrived, before, stress, cohesion, iv, *halo),
        scratch=[pltpu.VMEM((128, 128), jnp.float32), pltpu.VMEM((128, 128), jnp.float32)],
    )


def exchange(axis, low, high):
    count = lax.axis_size(axis)
    return (
        lax.ppermute(high, axis, [(i, (i + 1) % count) for i in range(count)]),
        lax.ppermute(low, axis, [(i, (i - 1) % count) for i in range(count)]),
    )


def strike_swap(value):
    return lax.all_to_all(value, "bx", split_axis=0, concat_axis=0, tiled=True)


def whole_swap(value):
    value = value.reshape(512, 1, 128)
    value = lax.all_to_all(value, ("by", "bx"), split_axis=0, concat_axis=0, tiled=True)
    return value.reshape(512, 128)


def local(interface_velocity, history, kernel, velocity, stress, cohesion):
    arrived = strike_swap(scatter(interface_velocity))
    sent = strike_forward(arrived)
    arrived = whole_swap(sent)
    part, *edges = velocity_part(velocity, stress, sent)
    own_columns, own_rows = edges[:2], edges[2:]
    columns = exchange("by", *own_columns)
    weight, past = past_terms(kernel, history)
    sent = dip(arrived, weight, past, columns)
    arrived = whole_swap(sent)
    rows = exchange("bx", *velocity_columns(own_rows, columns, sent))
    sent = strike_inverse(arrived, rows)
    arrived = strike_swap(sent)
    before, *halo = velocity_rows(part, (*rows, *columns), (*own_rows, *own_columns), sent)
    return slab(arrived, before, stress, cohesion, interface_velocity, halo)


def solution(mesh):
    return jax.shard_map(
        local,
        mesh=mesh,
        in_specs=(
            P(None, "bx", "by"),
            P(None, None, None, "by", "bx", None, None),
            P(None, "by", "bx", None, None),
            P(None, None, "bx", "by"),
            P(None, None, "bx", "by"),
            P(None, "bx", "by"),
        ),
        out_specs=(P(None, None, "bx", "by"), P(None, None, "bx", "by")),
        check_vma=False,
    )
```

```python
import jax
import jax.numpy as jnp
import numpy as np
from jax import lax
from jax.experimental import pallas as pl
from jax.experimental.pallas import tpu as pltpu
from jax.sharding import PartitionSpec as P

COURANT = 0.3
FRICTION = 0.6
NP_, NQ = 32, 64
NJ = 16
NF = 512
SCALE = 1.0 / 2048.0
VMEM = pl.BlockSpec(memory_space=pltpu.VMEM)
PARAMS = pltpu.CompilerParams(vmem_limit_bytes=16 * 1024 * 1024)


def angles(rows, cols, length):
    return 2.0 * np.pi / length * ((rows[:, None] * cols[None, :]) % length)


def stack(*tables):
    wide = [np.pad(table, ((0, 0), (0, 256 - table.shape[1]))) for table in tables]
    return np.concatenate(wide, axis=0).astype(np.float32)


def cell_table():
    theta = angles(np.arange(64), np.arange(64), 64).reshape(64, 16, 4)
    cos, sin = np.cos(theta) * SCALE, np.sin(theta) * SCALE
    table = np.zeros((2, 2, 64, 16, 2, 2, 4))
    for h in range(2):
        table[0, h, :, :, 0, h] = cos
        table[1, h, :, :, 0, h] = sin
        table[0, h, :, :, 1, h] = -sin
        table[1, h, :, :, 1, h] = cos
    return table.reshape(256, 256)


def strike_tables(inverse):
    theta = angles(np.arange(32), np.arange(32), 32)
    cos, sin = np.cos(theta), np.sin(theta)
    twiddle = angles(np.arange(32), np.arange(128) % 64, 2048)
    twiddle = np.concatenate([np.cos(twiddle), np.sin(twiddle)], axis=1)
    if inverse:
        return stack(cell_table().T, twiddle, np.concatenate([cos, -sin], axis=1))
    return stack(cell_table(), twiddle, np.concatenate([cos, -sin], axis=0))


def dip_order():
    lane = np.arange(128)
    return 4 * (lane % 32) + lane // 32


def dip_tables():
    theta = angles(np.arange(128), dip_order(), 128)
    forward = np.concatenate([np.cos(theta), np.sin(theta)], axis=1)
    inverse = np.concatenate([np.cos(theta).T, np.sin(theta).T], axis=1)
    theta = angles(np.arange(8), np.arange(128), 512)
    inner = np.concatenate([np.cos(theta), np.sin(theta)], axis=1)
    outer = []
    for b in range(4):
        for s in range(2):
            theta = angles(2 * s + np.arange(8) // 4, 4 * dip_order() + b, 2048)
            outer.append(np.concatenate([np.cos(theta), np.sin(theta)], axis=1))
    return stack(forward, inverse, inner, *outer)


def halves(value):
    high = value.astype(jnp.bfloat16)
    low = (value - high.astype(jnp.float32)).astype(jnp.bfloat16)
    return high, low


def dot(a, b):
    return jnp.dot(a, b, preferred_element_type=jnp.float32)


def stacked_dot(table, value):
    high, low = halves(value)
    table_high, table_low = halves(table)
    table = jnp.concatenate([table_high, table_high, table_low], axis=1)
    return dot(table, jnp.concatenate([high, low, high], axis=0))


def rows_dot(value, table):
    rows = value.shape[0]
    high, low = halves(value)
    table_high, table_low = halves(table)
    both = dot(jnp.concatenate([high, low], axis=0), table_high)
    return both[:rows] + both[rows:] + dot(high, table_low)


def radix_four(values, sign):
    (r0, i0), (r1, i1), (r2, i2), (r3, i3) = values
    ar, ai, br, bi = r0 + r2, i0 + i2, r0 - r2, i0 - i2
    cr, ci, dr, di = r1 + r3, i1 + i3, sign * (r1 - r3), sign * (i1 - i3)
    return [
        (ar + cr, ai + ci),
        (br - di, bi + dr),
        (ar - cr, ai - ci),
        (br + di, bi - dr),
    ]


def turn(real, imag, cos, sin, sign):
    if sign > 0:
        return real * cos - imag * sin, imag * cos + real * sin
    return real * cos + imag * sin, imag * cos - real * sin


def dip_transform(values, table, sign):
    stacked = jnp.concatenate([part for pair in values for part in pair], axis=0)
    product = rows_dot(stacked, table)
    out = []
    for n in range(4):
        real, imag = product[96 * n : 96 * n + 48], product[96 * n + 48 : 96 * (n + 1)]
        out.append(
            (
                real[:, :128] - sign * imag[:, 128:],
                imag[:, :128] + sign * real[:, 128:],
            )
        )
    return out


def roll(value, shift, axis):
    return pltpu.roll(value, shift % value.shape[axis], axis)


def lane_of(shape):
    return lax.broadcasted_iota(jnp.int32, shape, len(shape) - 1)


def row_of(shape):
    return lax.broadcasted_iota(jnp.int32, shape, len(shape) - 2)


def block_transpose(parts):
    parts = list(parts)
    block = lane_of(parts[0].shape) // 16
    for step in (1, 2, 4):
        upper = (block // step) % 2 == 1
        for t in range(8):
            if (t // step) % 2 == 0:
                low, high = parts[t], parts[t + step]
                parts[t] = jnp.where(upper, roll(high, 16 * step, 1), low)
                parts[t + step] = jnp.where(upper, high, roll(low, -16 * step, 1))
    return parts


def scatter_kernel(iv_ref, out_ref, flipped_ref):
    for c in range(3):
        flipped_ref[...] = iv_ref[c].T
        for s in range(2):
            for h in range(2):
                out_ref[:, 2 * c + s, NQ * h : NQ * (h + 1)] = flipped_ref[
                    pl.ds(2 * s + h, 32, stride=4), :
                ]
    zero = jnp.zeros((32, 128), jnp.float32)
    out_ref[:, 6, :] = zero
    out_ref[:, 7, :] = zero


def strike_forward_kernel(in_ref, table_ref, after_ref, also_ref, out_ref):
    value = jnp.concatenate([in_ref[:, m, :] for m in range(6)], axis=1)
    value = stacked_dot(table_ref[288:352, 0:32], value)
    cos, sin = table_ref[256:288, 0:128], table_ref[256:288, 128:256]
    rows = []
    for m in range(6):
        real = value[:32, 128 * m : 128 * (m + 1)]
        imag = value[32:, 128 * m : 128 * (m + 1)]
        rows.append(
            jnp.concatenate([real * cos + imag * sin, imag * cos - real * sin], axis=1)
        )
    value = rows_dot(jnp.concatenate(rows, axis=0), table_ref[0:256, :])
    zero = jnp.zeros((32, 128), jnp.float32)
    for t in range(2):
        parts = [value[32 * m : 32 * (m + 1), 128 * t : 128 * (t + 1)] for m in range(6)]
        parts = block_transpose(parts + [zero, zero])
        for b in range(8):
            out_ref[32 * (8 * t + b) : 32 * (8 * t + b + 1), :] = parts[b]


def strike_inverse_kernel(in_ref, table_ref, after_ref, also_ref, out_ref):
    columns = []
    for t in range(2):
        columns.append(
            block_transpose([in_ref[32 * (8 * t + b) : 32 * (8 * t + b + 1), :] for b in range(8)])
        )
    rows = [jnp.concatenate([columns[0][m], columns[1][m]], axis=1) for m in range(8)]
    value = rows_dot(jnp.concatenate(rows, axis=0), table_ref[0:256, :])
    cos, sin = table_ref[256:288, 0:128], table_ref[256:288, 128:256]
    reals, imags = [], []
    for m in range(8):
        real = value[32 * m : 32 * (m + 1), :128]
        imag = value[32 * m : 32 * (m + 1), 128:]
        reals.append(real * cos - imag * sin)
        imags.append(imag * cos + real * sin)
    value = jnp.concatenate(
        [jnp.concatenate(reals, axis=1), jnp.concatenate(imags, axis=1)], axis=0
    )
    value = stacked_dot(table_ref[288:320, 0:64], value)
    parts = [value[:, 128 * m : 128 * (m + 1)] for m in range(8)]
    lane = lane_of((32, 128))
    last = parts[7]
    for m in range(6):
        before = roll(parts[m], 1, 0)
        after = roll(parts[m], -1, 0)
        for h in range(2):
            to = 64 + 2 * (2 * m + h)
            last = jnp.where(lane == to, roll(before, to - (NQ * h + 63), 1), last)
            last = jnp.where(lane == to + 1, roll(after, to + 1 - NQ * h, 1), last)
    parts[7] = last
    for m in range(8):
        out_ref[:, m, :] = parts[m]


def dip_kernel(in_ref, weight_ref, past_ref, table_ref, after_ref, also_ref, out_ref):
    flipped = in_ref[...].T
    values = []
    for v in range(4):
        lanes = slice(128 * v, 128 * (v + 1))
        values.append(
            [
                jnp.concatenate(
                    [flipped[16 * m + 8 * ri : 16 * m + 8 * ri + 8, lanes] for m in range(6)],
                    axis=0,
                )
                for ri in range(2)
            ]
        )
    inner = [
        (table_ref[256 + b : 257 + b, 0:128], table_ref[256 + b : 257 + b, 128:256])
        for b in range(4)
    ]
    outer = []
    for s in range(2):
        at = [264 + 16 * b + 8 * s for b in range(4)]
        cos = jnp.concatenate([table_ref[n : n + 8, 0:128] for n in at], axis=1)
        outer.append((cos, jnp.concatenate([table_ref[n : n + 8, 128:256] for n in at], axis=1)))
    values = radix_four(values, -1)
    values = [turn(*values[b], *inner[b], -1) for b in range(4)]
    values = dip_transform(values, table_ref[0:128, :], -1)
    real = jnp.concatenate([pair[0] for pair in values], axis=1)
    imag = jnp.concatenate([pair[1] for pair in values], axis=1)
    top = row_of((8, NF)) < 4
    sign = jnp.where(top, 1.0, -1.0).astype(jnp.float32)
    reals, imags = [], []
    for c in range(3):
        turned = []
        for s in range(2):
            rows = slice(16 * c + 8 * s, 16 * c + 8 * s + 8)
            turned.append(turn(real[rows], imag[rows], *outer[s], -1))
        even = [turned[0][ri] + turned[1][ri] for ri in range(2)]
        odd = [turned[0][ri] - turned[1][ri] for ri in range(2)]
        odd = [jnp.where(top, odd[0], odd[1]), jnp.where(top, odd[1], -odd[0])]
        response = []
        for parity, value in enumerate((even, odd)):
            spectrum = [roll(part, 4, 0) + sign * part for part in value]
            response.append(
                [
                    weight_ref[parity] * spectrum[ri] + past_ref[c, parity, ri]
                    for ri in range(2)
                ]
            )
        response = [[roll(part, 4, 0) + sign * part for part in pair] for pair in response]
        even = response[0]
        odd = [
            jnp.where(top, response[1][0], -response[1][1]),
            jnp.where(top, response[1][1], response[1][0]),
        ]
        for s in range(2):
            pair = [even[ri] + odd[ri] if s == 0 else even[ri] - odd[ri] for ri in range(2)]
            pair = turn(*pair, *outer[s], 1)
            reals.append(pair[0])
            imags.append(pair[1])
    real, imag = jnp.concatenate(reals, axis=0), jnp.concatenate(imags, axis=0)
    values = [
        (real[:, 128 * b : 128 * (b + 1)], imag[:, 128 * b : 128 * (b + 1)]) for b in range(4)
    ]
    values = dip_transform(values, table_ref[128:256, :], 1)
    values = [turn(*values[b], *inner[b], 1) for b in range(4)]
    values = radix_four(values, 1)
    real = jnp.concatenate([pair[0] for pair in values], axis=1)
    imag = jnp.concatenate([pair[1] for pair in values], axis=1)
    groups = []
    for m in range(6):
        groups += [real[8 * m : 8 * m + 8], imag[8 * m : 8 * m + 8]]
    early = lane_of((8, NF)) % 32 < 16
    edges = []
    for c in range(3):
        for ri in range(2):
            before = roll(roll(groups[4 * c + 2 + ri], 4, 0), 1, 1)
            after = roll(groups[4 * c + ri], -1, 1)
            edges.append(jnp.where(early, before, after))
    for ri in range(2):
        groups.append(jnp.where(top, edges[ri], roll(edges[2 + ri], 4, 0)))
    for ri in range(2):
        groups.append(jnp.where(top, edges[4 + ri], 0.0))
    out_ref[...] = jnp.concatenate(groups, axis=0).T


def mode_groups(tiles, rows_ref):
    for a in range(4):
        rows_ref[:, a, :] = tiles[a]
        rows_ref[:, 4 + a, :] = tiles[a]
    block = lane_of((8, 128)) // 32
    top = row_of((8, 128)) < 4
    columns = []
    for t in range(4):
        parts = [rows_ref[4 * n + t] for n in range(4)]
        for step in (1, 2):
            upper = (block // step) % 2 == 1
            for n in range(4):
                if (n // step) % 2 == 0:
                    low, high = parts[n], parts[n + step]
                    parts[n] = jnp.where(upper, roll(high, 32 * step, 1), low)
                    parts[n + step] = jnp.where(upper, high, roll(low, -32 * step, 1))
        columns.append([jnp.where(top, parts[n], parts[2 + n]) for n in range(2)])
    return [jnp.concatenate([column[n] for column in columns], axis=1) for n in range(2)]


def past_kernel(
    kernel_hbm, history_hbm, weight_ref, out_ref, rows_ref, kernel_ref, history_ref, arrived
):
    first = pltpu.make_async_copy(kernel_hbm, kernel_ref, arrived.at[0])
    second = pltpu.make_async_copy(history_hbm, history_ref, arrived.at[1])
    first.start()
    second.start()
    first.wait()
    groups = mode_groups([kernel_ref[0, a, 0] for a in range(4)], rows_ref.at[6])
    for parity in range(2):
        weight_ref[parity] = groups[parity]
    second.wait()
    for z in range(2):
        for c in range(3):
            tiles = []
            for a in range(4):
                total = kernel_ref[1, a, 0] * history_ref[0, z, c, a, 0]
                for h in range(1, 6):
                    total = total + kernel_ref[h + 1, a, 0] * history_ref[h, z, c, a, 0]
                tiles.append(total)
            groups = mode_groups(tiles, rows_ref.at[3 * z + c])
            for parity in range(2):
                out_ref[c, parity, z] = groups[parity]


ACROSS, ALONG, DEEP = (0, 3, 4), (3, 1, 5), (4, 5, 2)
STEP = 0.5 * COURANT


def pack_columns(stress_ref, part_ref, side):
    lane = lane_of((64, 128))
    total = jnp.zeros((64, 128), jnp.float32)
    for n in range(3):
        for z in range(4):
            fields = (stress_ref[ALONG[n], z], part_ref[n, z], stress_ref[ACROSS[n], z])
            for i in range(3):
                to = 12 * i + 4 * n + z
                total = jnp.where(lane == to, roll(fields[i], to - side, 1), total)
    return total


def part_kernel(
    velocity_ref, stress_ref, after_ref, part_ref, ylo_ref, yhi_ref, xlo_ref, xhi_ref
):
    row, lane = row_of((64, 128)), lane_of((64, 128))
    for n in range(3):
        for z in range(4):
            across, along = stress_ref[ACROSS[n], z], stress_ref[ALONG[n], z]
            total = jnp.where(row == 63, 0.0, roll(across, -1, 0))
            total = total - jnp.where(row == 0, 0.0, roll(across, 1, 0))
            total = total + jnp.where(lane == 127, 0.0, roll(along, -1, 1))
            total = total - jnp.where(lane == 0, 0.0, roll(along, 1, 1))
            if z < 3:
                total = total + stress_ref[DEEP[n], z + 1]
            if z > 0:
                total = total - stress_ref[DEEP[n], z - 1]
            part_ref[n, z] = velocity_ref[n, z] + STEP * total
    ylo_ref[...] = pack_columns(stress_ref, part_ref, 0)
    yhi_ref[...] = pack_columns(stress_ref, part_ref, 127)
    pad = jnp.zeros((8, 128), jnp.float32)
    for at, ref in ((0, xlo_ref), (63, xhi_ref)):
        rows = [stress_ref[ACROSS[n], z, at : at + 1, :] for n in range(3) for z in range(4)]
        rows += [part_ref[n, z, at : at + 1, :] for n in range(3) for z in range(4)]
        ref[...] = jnp.concatenate(rows + [pad], axis=0)


def column_kernel(low_ref, high_ref, ylo_ref, yhi_ref, after_ref, out_low_ref, out_high_ref):
    lane, row = lane_of((32, 128)), row_of((32, 128))
    for at, ref, out_ref in ((0, low_ref, out_low_ref), (63, high_ref, out_high_ref)):
        low = jnp.broadcast_to(ylo_ref[at : at + 1, :], (32, 128))
        high = jnp.broadcast_to(yhi_ref[at : at + 1, :], (32, 128))
        before = jnp.zeros((32, 128), jnp.float32)
        after = jnp.zeros((32, 128), jnp.float32)
        for n in range(12):
            before = jnp.where((row == 12 + n) & (lane == 0), roll(low, -n, 1), before)
            after = jnp.where((row == 12 + n) & (lane == 127), roll(high, 127 - n, 1), after)
        edge = ref[...] + STEP * (after - before)
        edge = jnp.where(row == 24, low, edge)
        out_ref[...] = jnp.where(row == 25, high, edge)


def row_kernel(
    part_ref, xlo_ref, xhi_ref, ylo_ref, yhi_ref,
    own_xlo_ref, own_xhi_ref, own_ylo_ref, own_yhi_ref, after_ref,
    out_ref, vxlo_ref, vxhi_ref, vylo_ref, vyhi_ref,
):
    row, lane = row_of((64, 128)), lane_of((64, 128))
    ylo, yhi = ylo_ref[...], yhi_ref[...]
    for n in range(3):
        for z in range(4):
            at = 4 * n + z
            field = part_ref[n, z]
            field = field - jnp.where(row == 0, STEP * xlo_ref[at : at + 1, :], 0.0)
            field = field + jnp.where(row == 63, STEP * xhi_ref[at : at + 1, :], 0.0)
            field = field - jnp.where(lane == 0, STEP * roll(ylo, -at, 1), 0.0)
            field = field + jnp.where(lane == 127, STEP * roll(yhi, 127 - at, 1), 0.0)
            out_ref[n, z] = field
    vxlo_ref[...] = xlo_ref[12:28, :] + STEP * own_xlo_ref[0:16, :]
    vxhi_ref[...] = xhi_ref[12:28, :] - STEP * own_xhi_ref[0:16, :]
    for side, ref in enumerate((vylo_ref, vyhi_ref)):
        corner = jnp.where(row == 63, STEP * xhi_ref[24 + side : 25 + side, :], 0.0)
        corner = corner - jnp.where(row == 0, STEP * xlo_ref[24 + side : 25 + side, :], 0.0)
        if side == 0:
            columns = roll(ylo, -12, 1) + STEP * own_ylo_ref[...]
        else:
            columns = roll(yhi, -12, 1) - STEP * own_yhi_ref[...]
        ref[...] = columns + roll(corner, -24, 1)


def strike_diff(field, low, high):
    row = row_of(field.shape)
    before = jnp.where(row == 0, low, roll(field, 1, 0))
    after = jnp.where(row == 63, high, roll(field, -1, 0))
    return 0.5 * (after - before)


def dip_diff(field, low, high, to):
    lane = lane_of(field.shape)
    before = jnp.where(lane == 0, roll(low, -to, 1), roll(field, 1, 1))
    after = jnp.where(lane == 127, roll(high, 127 - to, 1), roll(field, -1, 1))
    return 0.5 * (after - before)


def slab_kernel(
    in_ref, before_ref, stress_ref, cohesion_ref, iv_ref,
    xlo_ref, xhi_ref, ylo_ref, yhi_ref,
    velocity_ref, out_ref, flipped_ref, edge_ref,
):
    last = in_ref[:, 7, :]
    xlo, xhi = [], []
    half = lane_of((32, 128)) < 64
    edge_ref[...] = jnp.zeros((128, 128), jnp.float32)
    for c in range(3):
        for s in range(2):
            for h in range(2):
                to = pl.ds(2 * s + h, 32, stride=4)
                piece = in_ref[:, 2 * c + s, :]
                piece = roll(piece, 64, 1) if h else piece
                shifted = roll(last, -2 * (4 * c + 2 * s + h), 1)
                flipped_ref[to, :] = jnp.where(half, piece, shifted)
        m, h = 6 + c // 2, c % 2
        edge_ref[4 * c : 4 * c + 1, 0:64] = in_ref[0, m : m + 1, NQ * h : NQ * (h + 1)]
        edge_ref[12 + 4 * c : 13 + 4 * c, 0:64] = in_ref[31, m : m + 1, NQ * h : NQ * (h + 1)]
        traction = flipped_ref[...].T
        velocity_ref[c, 0] = before_ref[c, 0] - 0.5 * COURANT * traction[:64]
        xlo.append(traction[64:65])
        xhi.append(traction[65:66])
        for z in range(1, 4):
            velocity_ref[c, z] = before_ref[c, z]
    edges = edge_ref[...].T[:64]
    lane = lane_of((64, 128))
    ylo = ylo_ref[...] - 0.5 * COURANT * jnp.where(lane < 12, edges, 0.0)
    yhi = yhi_ref[...] - 0.5 * COURANT * jnp.where(lane < 12, roll(edges, -12, 1), 0.0)
    for z in range(4):
        dx, dy, dz = [], [], []
        for c in range(3):
            field = velocity_ref[c, z]
            at = 4 * c + z
            low, high = xlo_ref[at : at + 1], xhi_ref[at : at + 1]
            if z == 0:
                low = low - 0.5 * COURANT * xlo[c]
                high = high - 0.5 * COURANT * xhi[c]
            dx.append(strike_diff(field, low, high))
            dy.append(dip_diff(field, ylo, yhi, at))
            under = iv_ref[c] if z == 0 else velocity_ref[c, z - 1]
            if z < 3:
                dz.append(0.5 * (velocity_ref[c, z + 1] - under))
            else:
                dz.append(-0.5 * under)
        dilation = dx[0] + dy[1] + dz[2]
        rates = [
            dilation + 2.0 * dx[0],
            dilation + 2.0 * dy[1],
            dilation + 2.0 * dz[2],
            dy[0] + dx[1],
            dz[0] + dx[2],
            dz[1] + dy[2],
        ]
        trial = [stress_ref[n, z] + COURANT * rates[n] for n in range(6)]
        pressure = (trial[0] + trial[1] + trial[2]) * (1.0 / 3.0)
        normal = [trial[n] - pressure for n in range(3)]
        second = 0.5 * (
            normal[0] * normal[0] + normal[1] * normal[1] + normal[2] * normal[2]
        ) + (trial[3] * trial[3] + trial[4] * trial[4] + trial[5] * trial[5])
        shear = jnp.sqrt(second)
        limit = cohesion_ref[z] + FRICTION * jnp.maximum(-pressure, 0.0)
        factor = limit / jnp.maximum(shear, limit)
        for n in range(3):
            out_ref[n, z] = pressure + factor * normal[n]
            out_ref[3 + n, z] = factor * trial[3 + n]


def f32(*shape):
    return jax.ShapeDtypeStruct(shape, jnp.float32)


def call(kernel, out_shape, arguments, after=(), scratch=()):
    many = isinstance(out_shape, tuple)
    return pl.pallas_call(
        kernel,
        out_shape=out_shape,
        in_specs=[VMEM] * len(arguments) + [pl.BlockSpec(memory_space=pl.ANY)] * len(after),
        out_specs=(VMEM,) * len(out_shape) if many else VMEM,
        scratch_shapes=list(scratch),
        compiler_params=PARAMS,
    )(*arguments, *after)


def scatter(iv):
    scratch = [pltpu.VMEM((128, 64), jnp.float32)]
    return call(scatter_kernel, f32(32, 8, 128), (iv,), scratch=scratch)


def strike_forward(arrived, after):
    arguments = (arrived, strike_tables(False))
    return call(strike_forward_kernel, f32(512, 128), arguments, after)


def strike_inverse(arrived, after):
    arguments = (arrived, strike_tables(True))
    return call(strike_inverse_kernel, f32(32, 8, 128), arguments, after)


def dip(arrived, weight, past, after):
    return call(dip_kernel, f32(512, 128), (arrived, weight, past, dip_tables()), after)


def past_terms(kernel, history):
    return call(
        past_kernel,
        (f32(2, 8, NF), f32(3, 2, 2, 8, NF)),
        (),
        (kernel, history),
        [
            pltpu.VMEM((7, 16, 8, 128), jnp.float32),
            pltpu.VMEM(kernel.shape, jnp.float32),
            pltpu.VMEM(history.shape, jnp.float32),
            pltpu.SemaphoreType.DMA((2,)),
        ],
    )


def velocity_part(velocity, stress, after):
    columns, rows = (f32(64, 128),) * 2, (f32(32, 128),) * 2
    outs = (f32(3, 4, 64, 128), *columns, *rows)
    return call(part_kernel, outs, (velocity, stress), (after,))


def velocity_columns(edges, halo, after):
    return call(column_kernel, (f32(32, 128),) * 2, (*edges, *halo), (after,))


def velocity_rows(part, halo, own, after):
    return call(
        row_kernel,
        (f32(3, 4, 64, 128), f32(16, 128), f32(16, 128), f32(64, 128), f32(64, 128)),
        (part, *halo, *own),
        (after,),
    )


def slab(arrived, before, stress, cohesion, iv, halo):
    return call(
        slab_kernel,
        (f32(3, 4, 64, 128), f32(6, 4, 64, 128)),
        (arrived, before, stress, cohesion, iv, *halo),
        scratch=[pltpu.VMEM((128, 128), jnp.float32), pltpu.VMEM((128, 128), jnp.float32)],
    )


def exchange(axis, low, high):
    count = lax.axis_size(axis)
    return (
        lax.ppermute(high, axis, [(i, (i + 1) % count) for i in range(count)]),
        lax.ppermute(low, axis, [(i, (i - 1) % count) for i in range(count)]),
    )


def strike_swap(value):
    return lax.all_to_all(value, "bx", split_axis=0, concat_axis=0, tiled=True)


def whole_swap(value):
    value = value.reshape(512, 1, 128)
    value = lax.all_to_all(value, ("by", "bx"), split_axis=0, concat_axis=0, tiled=True)
    return value.reshape(512, 128)


def local(interface_velocity, history, kernel, velocity, stress, cohesion):
    arrived = strike_swap(scatter(interface_velocity))
    weight, past = past_terms(kernel, history)
    sent = strike_forward(arrived, (weight, past))
    arrived = whole_swap(sent)
    part, *edges = velocity_part(velocity, stress, sent)
    own_columns, own_rows = edges[:2], edges[2:]
    columns = exchange("by", *own_columns)
    sent = dip(arrived, weight, past, columns)
    arrived = whole_swap(sent)
    rows = exchange("bx", *velocity_columns(own_rows, columns, sent))
    sent = strike_inverse(arrived, rows)
    arrived = strike_swap(sent)
    before, *halo = velocity_rows(part, (*rows, *columns), (*own_rows, *own_columns), sent)
    return slab(arrived, before, stress, cohesion, interface_velocity, halo)


def solution(mesh):
    return jax.shard_map(
        local,
        mesh=mesh,
        in_specs=(
            P(None, "bx", "by"),
            P(None, None, None, "by", "bx", None, None),
            P(None, "by", "bx", None, None),
            P(None, None, "bx", "by"),
            P(None, None, "bx", "by"),
            P(None, "bx", "by"),
        ),
        out_specs=(P(None, None, "bx", "by"), P(None, None, "bx", "by")),
        check_vma=False,
    )
```

```python
import jax
import jax.numpy as jnp
import numpy as np
from jax import lax
from jax.experimental import pallas as pl
from jax.experimental.pallas import tpu as pltpu
from jax.sharding import PartitionSpec as P

COURANT = 0.3
FRICTION = 0.6
NP_, NQ = 32, 64
NJ = 16
NF = 512
SCALE = 1.0 / 2048.0
VMEM = pl.BlockSpec(memory_space=pltpu.VMEM)
PARAMS = pltpu.CompilerParams(vmem_limit_bytes=16 * 1024 * 1024)


def angles(rows, cols, length):
    return 2.0 * np.pi / length * ((rows[:, None] * cols[None, :]) % length)


def stack(*tables):
    wide = [np.pad(table, ((0, 0), (0, 256 - table.shape[1]))) for table in tables]
    return np.concatenate(wide, axis=0).astype(np.float32)


def cell_table():
    theta = angles(np.arange(64), np.arange(64), 64).reshape(64, 16, 4)
    cos, sin = np.cos(theta) * SCALE, np.sin(theta) * SCALE
    table = np.zeros((2, 2, 64, 16, 2, 2, 4))
    for h in range(2):
        table[0, h, :, :, 0, h] = cos
        table[1, h, :, :, 0, h] = sin
        table[0, h, :, :, 1, h] = -sin
        table[1, h, :, :, 1, h] = cos
    return table.reshape(256, 256)


def strike_tables(inverse):
    theta = angles(np.arange(32), np.arange(32), 32)
    cos, sin = np.cos(theta), np.sin(theta)
    twiddle = angles(np.arange(32), np.arange(128) % 64, 2048)
    twiddle = np.concatenate([np.cos(twiddle), np.sin(twiddle)], axis=1)
    if inverse:
        return stack(cell_table().T, twiddle, np.concatenate([cos, -sin], axis=1))
    return stack(cell_table(), twiddle, np.concatenate([cos, -sin], axis=0))


def dip_order():
    lane = np.arange(128)
    return 4 * (lane % 32) + lane // 32


def dip_tables():
    theta = angles(np.arange(128), dip_order(), 128)
    forward = np.concatenate([np.cos(theta), np.sin(theta)], axis=1)
    inverse = np.concatenate([np.cos(theta).T, np.sin(theta).T], axis=1)
    theta = angles(np.arange(8), np.arange(128), 512)
    inner = np.concatenate([np.cos(theta), np.sin(theta)], axis=1)
    outer = []
    for b in range(4):
        for s in range(2):
            theta = angles(2 * s + np.arange(8) // 4, 4 * dip_order() + b, 2048)
            outer.append(np.concatenate([np.cos(theta), np.sin(theta)], axis=1))
    return stack(forward, inverse, inner, *outer)


def halves(value):
    high = value.astype(jnp.bfloat16)
    low = (value - high.astype(jnp.float32)).astype(jnp.bfloat16)
    return high, low


def dot(a, b):
    return jnp.dot(a, b, preferred_element_type=jnp.float32)


def stacked_dot(table, value):
    high, low = halves(value)
    table_high, table_low = halves(table)
    table = jnp.concatenate([table_high, table_high, table_low], axis=1)
    return dot(table, jnp.concatenate([high, low, high], axis=0))


def rows_dot(value, table):
    rows = value.shape[0]
    high, low = halves(value)
    table_high, table_low = halves(table)
    both = dot(jnp.concatenate([high, low], axis=0), table_high)
    return both[:rows] + both[rows:] + dot(high, table_low)


def radix_four(values, sign):
    (r0, i0), (r1, i1), (r2, i2), (r3, i3) = values
    ar, ai, br, bi = r0 + r2, i0 + i2, r0 - r2, i0 - i2
    cr, ci, dr, di = r1 + r3, i1 + i3, sign * (r1 - r3), sign * (i1 - i3)
    return [
        (ar + cr, ai + ci),
        (br - di, bi + dr),
        (ar - cr, ai - ci),
        (br + di, bi - dr),
    ]


def turn(real, imag, cos, sin, sign):
    if sign > 0:
        return real * cos - imag * sin, imag * cos + real * sin
    return real * cos + imag * sin, imag * cos - real * sin


def dip_transform(values, table, sign):
    stacked = jnp.concatenate([part for pair in values for part in pair], axis=0)
    product = rows_dot(stacked, table)
    out = []
    for n in range(4):
        real, imag = product[96 * n : 96 * n + 48], product[96 * n + 48 : 96 * (n + 1)]
        out.append(
            (
                real[:, :128] - sign * imag[:, 128:],
                imag[:, :128] + sign * real[:, 128:],
            )
        )
    return out


def roll(value, shift, axis):
    return pltpu.roll(value, shift % value.shape[axis], axis)


def lane_of(shape):
    return lax.broadcasted_iota(jnp.int32, shape, len(shape) - 1)


def row_of(shape):
    return lax.broadcasted_iota(jnp.int32, shape, len(shape) - 2)


def block_transpose(parts):
    parts = list(parts)
    block = lane_of(parts[0].shape) // 16
    for step in (1, 2, 4):
        upper = (block // step) % 2 == 1
        for t in range(8):
            if (t // step) % 2 == 0:
                low, high = parts[t], parts[t + step]
                parts[t] = jnp.where(upper, roll(high, 16 * step, 1), low)
                parts[t + step] = jnp.where(upper, high, roll(low, -16 * step, 1))
    return parts


def scatter_kernel(iv_ref, out_ref, flipped_ref):
    for c in range(3):
        flipped_ref[...] = iv_ref[c].T
        for s in range(2):
            for h in range(2):
                out_ref[:, 2 * c + s, NQ * h : NQ * (h + 1)] = flipped_ref[
                    pl.ds(2 * s + h, 32, stride=4), :
                ]
    zero = jnp.zeros((32, 128), jnp.float32)
    out_ref[:, 6, :] = zero
    out_ref[:, 7, :] = zero


def strike_forward_kernel(in_ref, table_ref, after_ref, also_ref, out_ref):
    value = jnp.concatenate([in_ref[:, m, :] for m in range(6)], axis=1)
    value = stacked_dot(table_ref[288:352, 0:32], value)
    cos, sin = table_ref[256:288, 0:128], table_ref[256:288, 128:256]
    rows = []
    for m in range(6):
        real = value[:32, 128 * m : 128 * (m + 1)]
        imag = value[32:, 128 * m : 128 * (m + 1)]
        rows.append(
            jnp.concatenate([real * cos + imag * sin, imag * cos - real * sin], axis=1)
        )
    value = rows_dot(jnp.concatenate(rows, axis=0), table_ref[0:256, :])
    zero = jnp.zeros((32, 128), jnp.float32)
    for t in range(2):
        parts = [value[32 * m : 32 * (m + 1), 128 * t : 128 * (t + 1)] for m in range(6)]
        parts = block_transpose(parts + [zero, zero])
        for b in range(8):
            out_ref[32 * (8 * t + b) : 32 * (8 * t + b + 1), :] = parts[b]


def strike_inverse_kernel(in_ref, table_ref, out_ref):
    columns = []
    for t in range(2):
        columns.append(
            block_transpose([in_ref[32 * (8 * t + b) : 32 * (8 * t + b + 1), :] for b in range(8)])
        )
    rows = [jnp.concatenate([columns[0][m], columns[1][m]], axis=1) for m in range(8)]
    value = rows_dot(jnp.concatenate(rows, axis=0), table_ref[0:256, :])
    cos, sin = table_ref[256:288, 0:128], table_ref[256:288, 128:256]
    reals, imags = [], []
    for m in range(8):
        real = value[32 * m : 32 * (m + 1), :128]
        imag = value[32 * m : 32 * (m + 1), 128:]
        reals.append(real * cos - imag * sin)
        imags.append(imag * cos + real * sin)
    value = jnp.concatenate(
        [jnp.concatenate(reals, axis=1), jnp.concatenate(imags, axis=1)], axis=0
    )
    value = stacked_dot(table_ref[288:320, 0:64], value)
    parts = [value[:, 128 * m : 128 * (m + 1)] for m in range(8)]
    lane = lane_of((32, 128))
    last = parts[7]
    for m in range(6):
        before = roll(parts[m], 1, 0)
        after = roll(parts[m], -1, 0)
        for h in range(2):
            to = 64 + 2 * (2 * m + h)
            last = jnp.where(lane == to, roll(before, to - (NQ * h + 63), 1), last)
            last = jnp.where(lane == to + 1, roll(after, to + 1 - NQ * h, 1), last)
    parts[7] = last
    for m in range(8):
        out_ref[:, m, :] = parts[m]


def dip_kernel(in_ref, weight_ref, past_ref, table_ref, after_ref, also_ref, out_ref):
    flipped = in_ref[...].T
    values = []
    for v in range(4):
        lanes = slice(128 * v, 128 * (v + 1))
        values.append(
            [
                jnp.concatenate(
                    [flipped[16 * m + 8 * ri : 16 * m + 8 * ri + 8, lanes] for m in range(6)],
                    axis=0,
                )
                for ri in range(2)
            ]
        )
    inner = [
        (table_ref[256 + b : 257 + b, 0:128], table_ref[256 + b : 257 + b, 128:256])
        for b in range(4)
    ]
    outer = []
    for s in range(2):
        at = [264 + 16 * b + 8 * s for b in range(4)]
        cos = jnp.concatenate([table_ref[n : n + 8, 0:128] for n in at], axis=1)
        outer.append((cos, jnp.concatenate([table_ref[n : n + 8, 128:256] for n in at], axis=1)))
    values = radix_four(values, -1)
    values = [turn(*values[b], *inner[b], -1) for b in range(4)]
    values = dip_transform(values, table_ref[0:128, :], -1)
    real = jnp.concatenate([pair[0] for pair in values], axis=1)
    imag = jnp.concatenate([pair[1] for pair in values], axis=1)
    top = row_of((8, NF)) < 4
    sign = jnp.where(top, 1.0, -1.0).astype(jnp.float32)
    reals, imags = [], []
    for c in range(3):
        turned = []
        for s in range(2):
            rows = slice(16 * c + 8 * s, 16 * c + 8 * s + 8)
            turned.append(turn(real[rows], imag[rows], *outer[s], -1))
        even = [turned[0][ri] + turned[1][ri] for ri in range(2)]
        odd = [turned[0][ri] - turned[1][ri] for ri in range(2)]
        odd = [jnp.where(top, odd[0], odd[1]), jnp.where(top, odd[1], -odd[0])]
        response = []
        for parity, value in enumerate((even, odd)):
            spectrum = [roll(part, 4, 0) + sign * part for part in value]
            response.append(
                [
                    weight_ref[parity] * spectrum[ri] + past_ref[c, parity, ri]
                    for ri in range(2)
                ]
            )
        response = [[roll(part, 4, 0) + sign * part for part in pair] for pair in response]
        even = response[0]
        odd = [
            jnp.where(top, response[1][0], -response[1][1]),
            jnp.where(top, response[1][1], response[1][0]),
        ]
        for s in range(2):
            pair = [even[ri] + odd[ri] if s == 0 else even[ri] - odd[ri] for ri in range(2)]
            pair = turn(*pair, *outer[s], 1)
            reals.append(pair[0])
            imags.append(pair[1])
    real, imag = jnp.concatenate(reals, axis=0), jnp.concatenate(imags, axis=0)
    values = [
        (real[:, 128 * b : 128 * (b + 1)], imag[:, 128 * b : 128 * (b + 1)]) for b in range(4)
    ]
    values = dip_transform(values, table_ref[128:256, :], 1)
    values = [turn(*values[b], *inner[b], 1) for b in range(4)]
    values = radix_four(values, 1)
    real = jnp.concatenate([pair[0] for pair in values], axis=1)
    imag = jnp.concatenate([pair[1] for pair in values], axis=1)
    groups = []
    for m in range(6):
        groups += [real[8 * m : 8 * m + 8], imag[8 * m : 8 * m + 8]]
    early = lane_of((8, NF)) % 32 < 16
    edges = []
    for c in range(3):
        for ri in range(2):
            before = roll(roll(groups[4 * c + 2 + ri], 4, 0), 1, 1)
            after = roll(groups[4 * c + ri], -1, 1)
            edges.append(jnp.where(early, before, after))
    for ri in range(2):
        groups.append(jnp.where(top, edges[ri], roll(edges[2 + ri], 4, 0)))
    for ri in range(2):
        groups.append(jnp.where(top, edges[4 + ri], 0.0))
    out_ref[...] = jnp.concatenate(groups, axis=0).T


def mode_groups(tiles, rows_ref):
    for a in range(4):
        rows_ref[:, a, :] = tiles[a]
        rows_ref[:, 4 + a, :] = tiles[a]
    block = lane_of((8, 128)) // 32
    top = row_of((8, 128)) < 4
    columns = []
    for t in range(4):
        parts = [rows_ref[4 * n + t] for n in range(4)]
        for step in (1, 2):
            upper = (block // step) % 2 == 1
            for n in range(4):
                if (n // step) % 2 == 0:
                    low, high = parts[n], parts[n + step]
                    parts[n] = jnp.where(upper, roll(high, 32 * step, 1), low)
                    parts[n + step] = jnp.where(upper, high, roll(low, -32 * step, 1))
        columns.append([jnp.where(top, parts[n], parts[2 + n]) for n in range(2)])
    return [jnp.concatenate([column[n] for column in columns], axis=1) for n in range(2)]


def past_kernel(
    kernel_hbm, history_hbm, weight_ref, out_ref, rows_ref, kernel_ref, history_ref, arrived
):
    first = pltpu.make_async_copy(kernel_hbm, kernel_ref, arrived.at[0])
    second = pltpu.make_async_copy(history_hbm, history_ref, arrived.at[1])
    first.start()
    second.start()
    first.wait()
    groups = mode_groups([kernel_ref[0, a, 0] for a in range(4)], rows_ref.at[6])
    for parity in range(2):
        weight_ref[parity] = groups[parity]
    second.wait()
    for z in range(2):
        for c in range(3):
            tiles = []
            for a in range(4):
                total = kernel_ref[1, a, 0] * history_ref[0, z, c, a, 0]
                for h in range(1, 6):
                    total = total + kernel_ref[h + 1, a, 0] * history_ref[h, z, c, a, 0]
                tiles.append(total)
            groups = mode_groups(tiles, rows_ref.at[3 * z + c])
            for parity in range(2):
                out_ref[c, parity, z] = groups[parity]


ACROSS, ALONG, DEEP = (0, 3, 4), (3, 1, 5), (4, 5, 2)
STEP = 0.5 * COURANT


def pack_columns(stress_ref, part_ref, side):
    lane = lane_of((64, 128))
    total = jnp.zeros((64, 128), jnp.float32)
    for n in range(3):
        for z in range(4):
            fields = (stress_ref[ALONG[n], z], part_ref[n, z], stress_ref[ACROSS[n], z])
            for i in range(3):
                to = 12 * i + 4 * n + z
                total = jnp.where(lane == to, roll(fields[i], to - side, 1), total)
    return total


def part_kernel(
    velocity_ref, stress_ref, after_ref, part_ref, ylo_ref, yhi_ref, xlo_ref, xhi_ref
):
    row, lane = row_of((64, 128)), lane_of((64, 128))
    for n in range(3):
        for z in range(4):
            across, along = stress_ref[ACROSS[n], z], stress_ref[ALONG[n], z]
            total = jnp.where(row == 63, 0.0, roll(across, -1, 0))
            total = total - jnp.where(row == 0, 0.0, roll(across, 1, 0))
            total = total + jnp.where(lane == 127, 0.0, roll(along, -1, 1))
            total = total - jnp.where(lane == 0, 0.0, roll(along, 1, 1))
            if z < 3:
                total = total + stress_ref[DEEP[n], z + 1]
            if z > 0:
                total = total - stress_ref[DEEP[n], z - 1]
            part_ref[n, z] = velocity_ref[n, z] + STEP * total
    ylo_ref[...] = pack_columns(stress_ref, part_ref, 0)
    yhi_ref[...] = pack_columns(stress_ref, part_ref, 127)
    pad = jnp.zeros((8, 128), jnp.float32)
    for at, ref in ((0, xlo_ref), (63, xhi_ref)):
        rows = [stress_ref[ACROSS[n], z, at : at + 1, :] for n in range(3) for z in range(4)]
        rows += [part_ref[n, z, at : at + 1, :] for n in range(3) for z in range(4)]
        ref[...] = jnp.concatenate(rows + [pad], axis=0)


def column_kernel(low_ref, high_ref, ylo_ref, yhi_ref, after_ref, out_low_ref, out_high_ref):
    lane, row = lane_of((32, 128)), row_of((32, 128))
    for at, ref, out_ref in ((0, low_ref, out_low_ref), (63, high_ref, out_high_ref)):
        low = jnp.broadcast_to(ylo_ref[at : at + 1, :], (32, 128))
        high = jnp.broadcast_to(yhi_ref[at : at + 1, :], (32, 128))
        before = jnp.zeros((32, 128), jnp.float32)
        after = jnp.zeros((32, 128), jnp.float32)
        for n in range(12):
            before = jnp.where((row == 12 + n) & (lane == 0), roll(low, -n, 1), before)
            after = jnp.where((row == 12 + n) & (lane == 127), roll(high, 127 - n, 1), after)
        edge = ref[...] + STEP * (after - before)
        edge = jnp.where(row == 24, low, edge)
        out_ref[...] = jnp.where(row == 25, high, edge)


def row_kernel(
    part_ref, xlo_ref, xhi_ref, ylo_ref, yhi_ref,
    own_xlo_ref, own_xhi_ref, own_ylo_ref, own_yhi_ref, after_ref,
    out_ref, vxlo_ref, vxhi_ref, vylo_ref, vyhi_ref,
):
    row, lane = row_of((64, 128)), lane_of((64, 128))
    ylo, yhi = ylo_ref[...], yhi_ref[...]
    for n in range(3):
        for z in range(4):
            at = 4 * n + z
            field = part_ref[n, z]
            field = field - jnp.where(row == 0, STEP * xlo_ref[at : at + 1, :], 0.0)
            field = field + jnp.where(row == 63, STEP * xhi_ref[at : at + 1, :], 0.0)
            field = field - jnp.where(lane == 0, STEP * roll(ylo, -at, 1), 0.0)
            field = field + jnp.where(lane == 127, STEP * roll(yhi, 127 - at, 1), 0.0)
            out_ref[n, z] = field
    vxlo_ref[...] = xlo_ref[12:28, :] + STEP * own_xlo_ref[0:16, :]
    vxhi_ref[...] = xhi_ref[12:28, :] - STEP * own_xhi_ref[0:16, :]
    for side, ref in enumerate((vylo_ref, vyhi_ref)):
        corner = jnp.where(row == 63, STEP * xhi_ref[24 + side : 25 + side, :], 0.0)
        corner = corner - jnp.where(row == 0, STEP * xlo_ref[24 + side : 25 + side, :], 0.0)
        if side == 0:
            columns = roll(ylo, -12, 1) + STEP * own_ylo_ref[...]
        else:
            columns = roll(yhi, -12, 1) - STEP * own_yhi_ref[...]
        ref[...] = columns + roll(corner, -24, 1)


def strike_diff(field, low, high):
    row = row_of(field.shape)
    before = jnp.where(row == 0, low, roll(field, 1, 0))
    after = jnp.where(row == 63, high, roll(field, -1, 0))
    return 0.5 * (after - before)


def dip_diff(field, low, high, to):
    lane = lane_of(field.shape)
    before = jnp.where(lane == 0, roll(low, -to, 1), roll(field, 1, 1))
    after = jnp.where(lane == 127, roll(high, 127 - to, 1), roll(field, -1, 1))
    return 0.5 * (after - before)


def slab_kernel(
    in_ref, before_ref, stress_ref, cohesion_ref, iv_ref,
    xlo_ref, xhi_ref, ylo_ref, yhi_ref,
    velocity_ref, out_ref, flipped_ref, edge_ref,
):
    last = in_ref[:, 7, :]
    xlo, xhi = [], []
    half = lane_of((32, 128)) < 64
    edge_ref[...] = jnp.zeros((128, 128), jnp.float32)
    for c in range(3):
        for s in range(2):
            for h in range(2):
                to = pl.ds(2 * s + h, 32, stride=4)
                piece = in_ref[:, 2 * c + s, :]
                piece = roll(piece, 64, 1) if h else piece
                shifted = roll(last, -2 * (4 * c + 2 * s + h), 1)
                flipped_ref[to, :] = jnp.where(half, piece, shifted)
        m, h = 6 + c // 2, c % 2
        edge_ref[4 * c : 4 * c + 1, 0:64] = in_ref[0, m : m + 1, NQ * h : NQ * (h + 1)]
        edge_ref[12 + 4 * c : 13 + 4 * c, 0:64] = in_ref[31, m : m + 1, NQ * h : NQ * (h + 1)]
        traction = flipped_ref[...].T
        velocity_ref[c, 0] = before_ref[c, 0] - 0.5 * COURANT * traction[:64]
        xlo.append(traction[64:65])
        xhi.append(traction[65:66])
        for z in range(1, 4):
            velocity_ref[c, z] = before_ref[c, z]
    edges = edge_ref[...].T[:64]
    lane = lane_of((64, 128))
    ylo = ylo_ref[...] - 0.5 * COURANT * jnp.where(lane < 12, edges, 0.0)
    yhi = yhi_ref[...] - 0.5 * COURANT * jnp.where(lane < 12, roll(edges, -12, 1), 0.0)
    for z in range(4):
        dx, dy, dz = [], [], []
        for c in range(3):
            field = velocity_ref[c, z]
            at = 4 * c + z
            low, high = xlo_ref[at : at + 1], xhi_ref[at : at + 1]
            if z == 0:
                low = low - 0.5 * COURANT * xlo[c]
                high = high - 0.5 * COURANT * xhi[c]
            dx.append(strike_diff(field, low, high))
            dy.append(dip_diff(field, ylo, yhi, at))
            under = iv_ref[c] if z == 0 else velocity_ref[c, z - 1]
            if z < 3:
                dz.append(0.5 * (velocity_ref[c, z + 1] - under))
            else:
                dz.append(-0.5 * under)
        dilation = dx[0] + dy[1] + dz[2]
        rates = [
            dilation + 2.0 * dx[0],
            dilation + 2.0 * dy[1],
            dilation + 2.0 * dz[2],
            dy[0] + dx[1],
            dz[0] + dx[2],
            dz[1] + dy[2],
        ]
        trial = [stress_ref[n, z] + COURANT * rates[n] for n in range(6)]
        pressure = (trial[0] + trial[1] + trial[2]) * (1.0 / 3.0)
        normal = [trial[n] - pressure for n in range(3)]
        second = 0.5 * (
            normal[0] * normal[0] + normal[1] * normal[1] + normal[2] * normal[2]
        ) + (trial[3] * trial[3] + trial[4] * trial[4] + trial[5] * trial[5])
        shear = jnp.sqrt(second)
        limit = cohesion_ref[z] + FRICTION * jnp.maximum(-pressure, 0.0)
        factor = limit / jnp.maximum(shear, limit)
        for n in range(3):
            out_ref[n, z] = pressure + factor * normal[n]
            out_ref[3 + n, z] = factor * trial[3 + n]


def f32(*shape):
    return jax.ShapeDtypeStruct(shape, jnp.float32)


def call(kernel, out_shape, arguments, after=(), scratch=()):
    many = isinstance(out_shape, tuple)
    return pl.pallas_call(
        kernel,
        out_shape=out_shape,
        in_specs=[VMEM] * len(arguments) + [pl.BlockSpec(memory_space=pl.ANY)] * len(after),
        out_specs=(VMEM,) * len(out_shape) if many else VMEM,
        scratch_shapes=list(scratch),
        compiler_params=PARAMS,
    )(*arguments, *after)


def scatter(iv):
    scratch = [pltpu.VMEM((128, 64), jnp.float32)]
    return call(scatter_kernel, f32(32, 8, 128), (iv,), scratch=scratch)


def strike_forward(arrived, after):
    arguments = (arrived, strike_tables(False))
    return call(strike_forward_kernel, f32(512, 128), arguments, after)


def strike_inverse(arrived):
    return call(strike_inverse_kernel, f32(32, 8, 128), (arrived, strike_tables(True)))


def dip(arrived, weight, past, after):
    return call(dip_kernel, f32(512, 128), (arrived, weight, past, dip_tables()), after)


def past_terms(kernel, history):
    return call(
        past_kernel,
        (f32(2, 8, NF), f32(3, 2, 2, 8, NF)),
        (),
        (kernel, history),
        [
            pltpu.VMEM((7, 16, 8, 128), jnp.float32),
            pltpu.VMEM(kernel.shape, jnp.float32),
            pltpu.VMEM(history.shape, jnp.float32),
            pltpu.SemaphoreType.DMA((2,)),
        ],
    )


def velocity_part(velocity, stress, after):
    columns, rows = (f32(64, 128),) * 2, (f32(32, 128),) * 2
    outs = (f32(3, 4, 64, 128), *columns, *rows)
    return call(part_kernel, outs, (velocity, stress), (after,))


def velocity_columns(edges, halo, after):
    return call(column_kernel, (f32(32, 128),) * 2, (*edges, *halo), (after,))


def velocity_rows(part, halo, own, after):
    return call(
        row_kernel,
        (f32(3, 4, 64, 128), f32(16, 128), f32(16, 128), f32(64, 128), f32(64, 128)),
        (part, *halo, *own),
        (after,),
    )


def slab(arrived, before, stress, cohesion, iv, halo):
    return call(
        slab_kernel,
        (f32(3, 4, 64, 128), f32(6, 4, 64, 128)),
        (arrived, before, stress, cohesion, iv, *halo),
        scratch=[pltpu.VMEM((128, 128), jnp.float32), pltpu.VMEM((128, 128), jnp.float32)],
    )


def exchange(axis, low, high):
    count = lax.axis_size(axis)
    return (
        lax.ppermute(high, axis, [(i, (i + 1) % count) for i in range(count)]),
        lax.ppermute(low, axis, [(i, (i - 1) % count) for i in range(count)]),
    )


def strike_swap(value):
    return lax.all_to_all(value, "bx", split_axis=0, concat_axis=0, tiled=True)


def whole_swap(value):
    value = value.reshape(512, 1, 128)
    value = lax.all_to_all(value, ("by", "bx"), split_axis=0, concat_axis=0, tiled=True)
    return value.reshape(512, 128)


def local(interface_velocity, history, kernel, velocity, stress, cohesion):
    arrived = strike_swap(scatter(interface_velocity))
    weight, past = past_terms(kernel, history)
    sent = strike_forward(arrived, (weight, past))
    arrived = whole_swap(sent)
    part, *edges = velocity_part(velocity, stress, sent)
    own_columns, own_rows = edges[:2], edges[2:]
    columns = exchange("by", *own_columns)
    sent = dip(arrived, weight, past, columns)
    arrived = whole_swap(sent)
    sent = strike_inverse(arrived)
    arrived = strike_swap(sent)
    rows = exchange("bx", *velocity_columns(own_rows, columns, sent))
    before, *halo = velocity_rows(part, (*rows, *columns), (*own_rows, *own_columns), sent)
    return slab(arrived, before, stress, cohesion, interface_velocity, halo)


def solution(mesh):
    return jax.shard_map(
        local,
        mesh=mesh,
        in_specs=(
            P(None, "bx", "by"),
            P(None, None, None, "by", "bx", None, None),
            P(None, "by", "bx", None, None),
            P(None, None, "bx", "by"),
            P(None, None, "bx", "by"),
            P(None, "bx", "by"),
        ),
        out_specs=(P(None, None, "bx", "by"), P(None, None, "bx", "by")),
        check_vma=False,
    )
```
